128 devices in a mesh: grp: 4 (over y), seq: 32 (over z, x, core).
Axes of the slice: x: 4, y: 4, z: 4, core: 2. Of those that a mesh axis runs over, the one named last changes fastest.
Arguments:
- query_input: bfloat16 [4, 1536, 4096], P('grp', 'seq'), may hold values from -240 to 240, as said below
- key_input: bfloat16 [4, 1536, 4096], P('grp', 'seq'), may hold values from -240 to 240, as said below
- value_input: bfloat16 [4, 1536, 4096], P('grp', 'seq'), may hold values from -6 to 6
- resid: bfloat16 [4, 1536, 4096], P('grp', 'seq'), may hold values from -6 to 6
- gate: float32 [4, 4096], P('grp'), may hold values from 0.5 to 2
- query_norm_gain: float32 [4096], replicated, may hold values from 0.7 to 2
- key_norm_gain: float32 [4096], replicated, may hold values from 0.7 to 2
- output_weight: bfloat16 [4096, 4096], P('seq'), may hold values from -0.09375 to 0.09375
- latents: bfloat16 [16, 64, 128, 16], P('grp', 'seq'), may hold values from -6 to 6
- w_in: bfloat16 [3, 144, 384], replicated, may hold values from -0.3125 to 0.3125
- b_in: float32 [384], replicated, may hold values from -3 to 3
- norm_gain: float32 [384], replicated, may hold values from 0.5 to 2
- w_mid: bfloat16 [3, 3456, 384], replicated, may hold values from -0.0625 to 0.0625
- b_mid: float32 [384], replicated, may hold values from -3 to 3
Outputs:
- attn_out: bfloat16 [4, 1536, 4096], P('grp', 'seq')
- decoded: bfloat16 [4, 16, 64, 128, 384], P('grp', None, 'seq')
The draws below stay inside these ranges and needn't reach their ends.
Inputs may be any that keep to these rules, and one draw needn't show every extreme that they name: `query_input`: projected query features; a few tokens of a request may have one head's features scaled by up to 40. `key_input`: projected key features; a few tokens of a request may have one head's features scaled by up to 40.
All inputs are finite; a program needn't handle non-finite values.
Results may differ from the reference program's by a relative error of at most 0.011.
Values may be sent and summed in bfloat16 or wider, within the bound.
No kernel may reach another device: no remote copies, remote signals or barrier semaphores. Data moves between devices by JAX's collectives and lax.ppermute only.
A program may use at most 384 MiB of HBM per device.

```python
import math
import jax
import jax.numpy as jnp
from jax import lax

HEAD_DIM = 128
HEADS = 32
D = 4096
L = 1536
LF = 16
LH = 64
LW = 128
LC = 16
VC = 384
N_GRP = 4


def draw_query_input(key, part):
    key = jax.random.fold_in(key, 11)
    base = jnp.clip(jax.random.normal(key, (N_GRP, L, D), jnp.float32), -6.0, 6.0)
    return base.astype(jnp.bfloat16)


def draw_key_input(key, part):
    key = jax.random.fold_in(key, 23)
    base = jnp.clip(jax.random.normal(key, (N_GRP, L, D), jnp.float32), -6.0, 6.0)
    return base.astype(jnp.bfloat16)


def block_scale(stream_key, shape, cuts, low, top_value):
    factor_of = 1.0
    for axis_at, shards_of in cuts:
        steps = jax.random.uniform(jax.random.fold_in(jax.random.fold_in(stream_key, 6), axis_at), (shards_of,), jnp.float32, low / len(cuts), top_value / len(cuts))
        factor_of = factor_of * jnp.repeat(jnp.exp(steps), shape[axis_at] // shards_of).reshape((-1,) + (1,) * (len(shape) - 1 - axis_at))
    return factor_of


def noise(own_key, extent, scale, bound, cuts=(), held_as=jnp.bfloat16):
    values = jax.random.normal(own_key, extent, jnp.float32) * scale
    if len(cuts) > 0:
        values = block_scale(own_key, extent, cuts, -0.22, 0.18) * values
    return jnp.clip(values, min=-bound, max=bound).astype(held_as)


def setup_inputs(seed: int = 0) -> dict:
    key_list = jax.random.split(jax.random.key(seed), 15)
    return {
        "query_input": draw_query_input(jax.random.fold_in(key_list[14], 71), 0),
        "key_input": draw_key_input(jax.random.fold_in(key_list[14], 71), 0),
        "value_input": noise(key_list[2], (N_GRP, L, D), 1.0, 6.0, ((0, 4), (1, 32))),
        "resid": noise(key_list[3], (N_GRP, L, D), 1.0, 6.0, ((0, 4), (1, 32))),
        "gate": jnp.clip(jnp.exp(math.log(2.0) - 1.3862944 * jax.random.uniform(key_list[4], (N_GRP, D), jnp.float32) ** block_scale(key_list[4], (N_GRP, D), ((0, 4),), -0.2, 0.2)), 0.5, 2.0),
        "query_norm_gain": jnp.clip(jnp.exp(jax.random.uniform(key_list[5], (D,), jnp.float32, math.log(0.7), math.log(2.0))), 0.7, 2.0),
        "key_norm_gain": jnp.clip(jnp.exp(jax.random.uniform(key_list[6], (D,), jnp.float32, math.log(0.7), math.log(2.0))), 0.7, 2.0),
        "output_weight": noise(key_list[7], (D, D), D ** -0.5, 0.09375, ((0, 32),)),
        "latents": noise(key_list[8], (LF, LH, LW, LC), 1.0, 6.0, ((0, 4), (1, 32))),
        "w_in": noise(key_list[9], (3, 9 * LC, VC), (27 * LC) ** -0.5, 0.3125),
        "b_in": noise(key_list[10], (VC,), 0.5, 3.0, (), jnp.float32),
        "norm_gain": jnp.clip(jnp.exp(jax.random.uniform(key_list[11], (VC,), jnp.float32, math.log(0.5), math.log(2.0))), 0.5, 2.0),
        "w_mid": noise(key_list[12], (3, 9 * VC, VC), (27 * VC) ** -0.5, 0.0625),
        "b_mid": noise(key_list[13], (VC,), 0.5, 3.0, (), jnp.float32),
    }


def rms_scaled(token_rows, gain_vec):
    values = token_rows.astype(jnp.float32)
    factor = lax.rsqrt(lax.optimization_barrier(jnp.mean(values * values, axis=-1, keepdims=True)) + 1e-06)
    return values * factor * gain_vec

def attend_head(query_matrix, keys_here, values_here):
    row_count = query_matrix.shape[0]
    head_width = query_matrix.shape[1]
    block_rows = 512 if row_count % 512 == 0 else row_count
    blocks = query_matrix.reshape(row_count // block_rows, block_rows, head_width)
    keys_wide = keys_here.astype(jnp.float32)

    def one_block(query_rows):
        scores = jnp.einsum('qd,kd->qk', query_rows.astype(jnp.float32), keys_wide) * head_width ** (-0.5)
        row_peak = lax.optimization_barrier(jnp.max(scores, axis=-1, keepdims=True))
        exponent = jnp.exp(scores - row_peak)
        weights = (exponent / lax.optimization_barrier(jnp.sum(exponent, axis=-1, keepdims=True))).astype(jnp.bfloat16)
        return jnp.dot(weights, values_here, preferred_element_type=jnp.float32).astype(jnp.bfloat16)
    return lax.map(one_block, blocks).reshape(row_count, head_width)

def diffusion_slot(query_matrix, incoming_keys, incoming_values, residual_rows, gate_vector, query_norm_gain, key_norm_gain, output_weight):
    q_normed = rms_scaled(query_matrix, query_norm_gain).astype(jnp.bfloat16)
    k_normed = rms_scaled(incoming_keys, key_norm_gain).astype(jnp.bfloat16)
    head_q = q_normed.reshape(L, HEADS, HEAD_DIM).transpose(1, 0, 2)
    head_k = k_normed.reshape(L, HEADS, HEAD_DIM).transpose(1, 0, 2)
    head_v = incoming_values.reshape(L, HEADS, HEAD_DIM).transpose(1, 0, 2)
    heads_out = lax.map(lambda trio: attend_head(trio[0], trio[1], trio[2]), (head_q, head_k, head_v))
    joined = heads_out.transpose(1, 0, 2).reshape(L, HEADS * HEAD_DIM)
    projected = jnp.dot(joined, output_weight, preferred_element_type=jnp.float32)
    return (residual_rows.astype(jnp.float32) + gate_vector[None, :] * projected).astype(jnp.bfloat16)

def conv_rows(frames, kernel):
    frame_count = frames.shape[0] - 2
    height = frames.shape[1] - 2
    width_cells = frames.shape[2]
    padded = jnp.pad(frames, ((0, 0), (0, 0), (1, 1), (0, 0)))
    columns = jnp.concatenate([padded[:, row_tap:row_tap + height, col_tap:col_tap + width_cells, :] for row_tap in range(3) for col_tap in range(3)], axis=-1)
    flattened = columns.reshape(frames.shape[0], height * width_cells, columns.shape[-1])
    summed = jnp.zeros((frame_count * height * width_cells, kernel.shape[2]), jnp.float32)
    for time_tap in range(3):
        taken = flattened[time_tap:time_tap + frame_count].reshape(frame_count * height * width_cells, columns.shape[-1])
        summed = summed + jnp.dot(taken, kernel[time_tap], preferred_element_type=jnp.float32)
    return summed.reshape(frame_count, height, width_cells, kernel.shape[2])

def causal_conv(frames, kernel):
    lead = jnp.zeros((2,) + frames.shape[1:], frames.dtype)
    padded = jnp.pad(jnp.concatenate([lead, frames], axis=0), ((0, 0), (1, 1), (0, 0), (0, 0)))
    return conv_rows(padded, kernel)

def activate(hidden_rows, gain_vec):
    return jax.nn.silu(rms_scaled(hidden_rows, gain_vec)).astype(jnp.bfloat16)

def reference(query_input, key_input, value_input, resid, gate, query_norm_gain, key_norm_gain, output_weight, latents, w_in, b_in, norm_gain, w_mid, b_mid):
    result_list = []
    for slot_ordinal in range(N_GRP - 1):
        result_list.append(diffusion_slot(query_input[slot_ordinal], key_input[slot_ordinal], value_input[slot_ordinal], resid[slot_ordinal], gate[slot_ordinal], query_norm_gain, key_norm_gain, output_weight))
    result_list.append(jnp.zeros((L, D), jnp.bfloat16))
    attn_out = jnp.stack(result_list)
    first_conv = (causal_conv(latents, w_in) + b_in).astype(jnp.bfloat16)
    activated = activate(first_conv, norm_gain)
    second_conv = causal_conv(activated, w_mid) + b_mid
    clip_out = (first_conv.astype(jnp.float32) + second_conv).astype(jnp.bfloat16)
    decoded = jnp.concatenate([jnp.zeros((N_GRP - 1, LF, LH, LW, VC), jnp.bfloat16), clip_out[None]], axis=0)
    return (attn_out, decoded)
```

```python
import math
import jax
import jax.numpy as jnp
from jax import lax
from jax.experimental import pallas as pl
from jax.experimental.pallas import tpu as pltpu
from jax.sharding import Mesh, PartitionSpec as P

CHIPS = ("z", "x")
SEQ = ("z", "x", "core")
EPS = 1e-06
MIB = 1024 * 1024


def vmem_spec():
    return pl.BlockSpec(memory_space=pltpu.VMEM)


def smem_spec():
    return pl.BlockSpec(memory_space=pltpu.SMEM)


def norm_pack(q, k, v, gain_q, gain_k):
    rows, width = q.shape
    chips = width // 256
    block = 16

    def body(q_ref, k_ref, v_ref, gq_ref, gk_ref, out_ref):
        def normed(ref, gain):
            x = ref[...].astype(jnp.float32)
            factor = lax.rsqrt(jnp.mean(x * x, axis=-1, keepdims=True) + EPS)
            return (x * factor * gain).astype(jnp.bfloat16)

        scale = 128**-0.5 * math.log2(math.e)
        qn = normed(q_ref, gq_ref[...] * scale)
        kn = normed(k_ref, gk_ref[...])
        for c in range(chips):
            cols = slice(256 * c, 256 * c + 256)
            out_ref[c, 0] = qn[:, cols]
            out_ref[c, 1] = kn[:, cols]
            out_ref[c, 2] = v_ref[:, cols]

    tokens = pl.BlockSpec((block, width), lambda i: (i, 0))
    gains = pl.BlockSpec((1, width), lambda i: (0, 0))
    return pl.pallas_call(
        body,
        grid=(rows // block,),
        out_shape=jax.ShapeDtypeStruct((chips, 3, rows, 256), jnp.bfloat16),
        in_specs=[tokens, tokens, tokens, gains, gains],
        out_specs=pl.BlockSpec((chips, 3, block, 256), lambda i: (0, 0, i, 0)),
        compiler_params=pltpu.CompilerParams(vmem_limit_bytes=32 * MIB),
        name="norm_pack",
    )(q, k, v, gain_q, gain_k)


def weight_blocks(place, w_here, w_there):
    rows, width = w_here.shape
    part = width // 4

    def body(place_ref, here_ref, there_ref, own_ref, up_ref, down_ref):
        core, ring = place_ref[1], place_ref[4]

        def halves(k):
            at = pl.ds(pl.multiple_of(lax.rem(ring + k, 4) * part, part), part)
            here, there = here_ref[:, at], there_ref[:, at]
            return jnp.where(core == 0, here, there), jnp.where(core == 0, there, here)

        @pl.when(place_ref[0] == 0)
        def _():
            own_ref[:rows], own_ref[rows:] = halves(0)
            up_ref[:rows], up_ref[rows : 2 * rows] = halves(1)
            down_ref[:rows], down_ref[rows : 2 * rows] = halves(3)
            up_ref[2 * rows :], down_ref[2 * rows :] = halves(2)

    return pl.pallas_call(
        body,
        out_shape=(
            jax.ShapeDtypeStruct((2 * rows, part), jnp.bfloat16),
            jax.ShapeDtypeStruct((3 * rows, part), jnp.bfloat16),
            jax.ShapeDtypeStruct((3 * rows, part), jnp.bfloat16),
        ),
        in_specs=[smem_spec(), vmem_spec(), vmem_spec()],
        out_specs=(vmem_spec(),) * 3,
        compiler_params=pltpu.CompilerParams(vmem_limit_bytes=24 * MIB),
        name="weight_blocks",
    )(place, w_here, w_there)


def attend(place, here, there):
    chips, _, tok, _ = here.shape
    half = chips * tok
    keys = 2 * half

    def body(place_ref, here_ref, there_ref, out_ref, k_buf, v_buf):
        step = pl.program_id(0)

        @pl.when((step == 0) & (place_ref[0] == 0))
        def _():
            for h in range(2):
                cols = slice(128 * h, 128 * h + 128)
                for n, ref in enumerate((here_ref, there_ref)):
                    span = slice(n * half, n * half + half)
                    k_buf[h, span] = ref[:, 1, :, cols].reshape(half, 128)
                    v_buf[h, span, :128] = ref[:, 2, :, cols].reshape(half, 128)
                v_buf[h, :, 128:] = jnp.ones((keys, 128), jnp.bfloat16)

        @pl.when(place_ref[0] == 0)
        def _():
            queries = here_ref[pl.ds(4 * step, 4), 0].reshape(4 * tok, 256)
            heads = []
            for h in range(2):
                s = lax.dot_general(
                    queries[:, 128 * h : 128 * h + 128],
                    k_buf[h],
                    (((1,), (1,)), ((), ())),
                    preferred_element_type=jnp.float32,
                )
                p = jnp.exp2(s - jnp.max(s, axis=-1, keepdims=True)).astype(jnp.bfloat16)
                o = jnp.dot(p, v_buf[h], preferred_element_type=jnp.float32)
                heads.append(o[:, :128] / o[:, 128:])
            joined = jnp.concatenate(heads, axis=1).astype(jnp.bfloat16)
            for n in range(4):
                at = jnp.where(place_ref[1] == 0, 4 * n + step, 4 * step + n)
                out_ref[at] = joined[tok * n : tok * n + tok]

    return pl.pallas_call(
        body,
        grid=(chips // 4,),
        out_shape=jax.ShapeDtypeStruct((chips, tok, 256), jnp.bfloat16),
        in_specs=[smem_spec(), vmem_spec(), vmem_spec()],
        out_specs=vmem_spec(),
        scratch_shapes=[
            pltpu.VMEM((2, keys, 128), jnp.bfloat16),
            pltpu.VMEM((2, keys, 256), jnp.bfloat16),
        ],
        compiler_params=pltpu.CompilerParams(vmem_limit_bytes=40 * MIB),
        cost_estimate=pl.CostEstimate(
            flops=8 * half * keys * 128,
            bytes_accessed=4 * half * 512,
            transcendentals=2 * half * keys,
        ),
        name="attend",
    )(place, here, there)


def project(place, heads, weights):
    rows = heads[0].shape[0] * heads[0].shape[1]
    part = weights[0].shape[1]
    lot = rows // 4

    def body(place_ref, oo, od, ou, of1, of2, wo, wd, wu, wf1, wf2, fa, fb, up, down, own):
        second = place_ref[5]

        @pl.when(place_ref[0] == 0)
        def _():
            weight = jnp.concatenate(
                [wo[...], wd[:256], wu[:256], wf1[...], wf2[...]], axis=0
            )

            def block(k, cols):
                b = lax.rem(second + k, 4)
                near = [ref[pl.ds(4 * b, 4)].reshape(lot, 256) for ref in (oo, od, ou)]
                low = of1[pl.ds(4 * lax.rem(b, 2), 4)].reshape(lot, 256)
                high = of2[pl.ds(4 * lax.rem(b, 2), 4)].reshape(lot, 256)
                feats = jnp.concatenate(near + [jnp.where(b < 2, low, high)], axis=1)
                return jnp.dot(feats, weight[:, cols], preferred_element_type=jnp.float32)

            whole, cut = slice(0, part), part // 2
            far = block(2, whole).astype(jnp.bfloat16)
            fa[...] = far[:, :cut]
            fb[...] = far[:, cut:]
            up[...] = block(1, whole).astype(jnp.bfloat16)
            down[...] = block(3, whole).astype(jnp.bfloat16)
            own[...] = block(0, whole)

    shape = jax.ShapeDtypeStruct
    return pl.pallas_call(
        body,
        out_shape=(
            shape((lot, part // 2), jnp.bfloat16),
            shape((lot, part // 2), jnp.bfloat16),
            shape((lot, part), jnp.bfloat16),
            shape((lot, part), jnp.bfloat16),
            shape((lot, part), jnp.float32),
        ),
        in_specs=[smem_spec()] + [vmem_spec()] * 10,
        out_specs=(vmem_spec(),) * 5,
        compiler_params=pltpu.CompilerParams(vmem_limit_bytes=40 * MIB),
        cost_estimate=pl.CostEstimate(
            flops=2 * rows * 1024 * part, bytes_accessed=8 * MIB, transcendentals=0
        ),
        name="project",
    )(place, *heads, *weights)


def add_passed(up, down, low, high):
    cut = low.shape[1]

    def body(up_ref, down_ref, low_ref, high_ref, up_out, down_out):
        def total(one, two):
            return (one.astype(jnp.float32) + two.astype(jnp.float32)).astype(jnp.bfloat16)

        up_out[:, :cut] = total(up_ref[:, :cut], low_ref[...])
        up_out[:, cut:] = up_ref[:, cut:]
        down_out[:, :cut] = down_ref[:, :cut]
        down_out[:, cut:] = total(down_ref[:, cut:], high_ref[...])

    return pl.pallas_call(
        body,
        out_shape=(jax.ShapeDtypeStruct(up.shape, up.dtype),) * 2,
        in_specs=[vmem_spec()] * 4,
        out_specs=(vmem_spec(),) * 2,
        name="add_passed",
    )(up, down, low, high)


def add_blocks(place, own, below, above):
    lot, part = own.shape
    tok = lot // 4

    def body(place_ref, own_ref, below_ref, above_ref, *outs):
        for k in range(4):
            at = pl.ds(pl.multiple_of(lax.rem(place_ref[4] + k, 4) * tok, tok), tok)
            total = own_ref[at] + below_ref[at].astype(jnp.float32)
            outs[k][...] = (total + above_ref[at].astype(jnp.float32)).astype(jnp.bfloat16)

    return pl.pallas_call(
        body,
        out_shape=(jax.ShapeDtypeStruct((tok, part), jnp.bfloat16),) * 4,
        in_specs=[smem_spec()] + [vmem_spec()] * 3,
        out_specs=(vmem_spec(),) * 4,
        name="add_blocks",
    )(place, own, below, above)


def finish(place, resid, gate, blocks):
    tok, width = resid.shape
    part = width // 4

    def body(place_ref, resid_ref, gate_ref, *refs):
        out_ref = refs[4]

        @pl.when(place_ref[0] == 0)
        def _():
            for k in range(4):
                at = pl.ds(pl.multiple_of(lax.rem(place_ref[4] + k, 4) * part, part), part)
                total = resid_ref[:, at].astype(jnp.float32)
                total += gate_ref[:, at] * refs[k][...].astype(jnp.float32)
                out_ref[:, at] = total.astype(jnp.bfloat16)

        @pl.when(place_ref[0] == 1)
        def _():
            out_ref[...] = jnp.zeros(out_ref.shape, out_ref.dtype)

    return pl.pallas_call(
        body,
        out_shape=jax.ShapeDtypeStruct(resid.shape, jnp.bfloat16),
        in_specs=[smem_spec()] + [vmem_spec()] * 6,
        out_specs=vmem_spec(),
        name="finish",
    )(place, resid, gate, *blocks)


def filter_weights(place, w_mid):
    steps, deep, vc = w_mid.shape
    taps = w_mid.reshape(steps, 3, 3, vc, vc)

    def body(place_ref, w_ref, out_ref):
        @pl.when(place_ref[0] == 1)
        def _():
            up, mid, down = (w_ref[0, n, 0].astype(jnp.float32) for n in range(3))
            ends = 0.5 * (up + down)
            mid = 0.5 * mid
            for n, g in enumerate((up, ends + mid, ends - mid, down)):
                out_ref[n] = jnp.transpose(g).astype(jnp.bfloat16)

    return pl.pallas_call(
        body,
        grid_spec=pltpu.PrefetchScalarGridSpec(
            num_scalar_prefetch=1,
            grid=(3 * steps,),
            in_specs=[
                pl.BlockSpec(
                    (1, 3, 1, vc, vc),
                    lambda i, where: (where[0] * (i // 3), 0, where[0] * (i % 3), 0, 0),
                )
            ],
            out_specs=pl.BlockSpec((4, vc, vc), lambda i, where: (0, 0, where[0] * i)),
        ),
        out_shape=jax.ShapeDtypeStruct((4, vc, deep), jnp.bfloat16),
        compiler_params=pltpu.CompilerParams(vmem_limit_bytes=24 * MIB),
        name="filter_weights",
    )(place, taps)


def decode(place, clip, w_first, filters, vectors):
    frames, _, lc, lw = clip.shape
    vc = w_first.shape[0]
    deep = 3 * vc
    lot = 4

    def body(place_ref, clip_ref, w1_ref, f_ref, vec_ref, out_ref, lat, act, firsts, w2, both, sems):
        step = pl.program_id(0)
        here = place_ref[0] == 1
        loads = [pltpu.make_async_copy(f_ref.at[n], w2.at[n], sems.at[n]) for n in range(4)]

        def moved(x):
            lane = lax.broadcasted_iota(jnp.int32, x.shape, x.ndim - 1)
            left = jnp.where(lane == 0, 0.0, pltpu.roll(x, 1, x.ndim - 1))
            right = jnp.where(lane == lw - 1, 0.0, pltpu.roll(x, lw - 1, x.ndim - 1))
            return left, x, right

        def first(f):
            sides = []
            for row in range(4):
                taps = [lat[f + dt, row : row + 3].reshape(9 * lc, lw) for dt in range(3)]
                taps.append(jnp.zeros((w1_ref.shape[1] - 27 * lc, lw), jnp.bfloat16))
                sides.append(jnp.concatenate(taps, axis=0))
            y = jnp.dot(
                w1_ref[...], jnp.concatenate(sides, axis=1), preferred_element_type=jnp.float32
            )
            acts = []
            for row in range(4):
                hidden = y[:, row * lw : row * lw + lw] + vec_ref[0]
                hidden = hidden.astype(jnp.bfloat16).astype(jnp.float32)
                if row in (1, 2):
                    firsts[lax.rem(f, 2 * lot), row - 1] = hidden
                factor = lax.rsqrt(jnp.mean(hidden * hidden, axis=0, keepdims=True) + EPS)
                if row == 0:
                    factor = jnp.where(place_ref[2] == 0, 0.0, factor)
                if row == 3:
                    factor = jnp.where(place_ref[2] == place_ref[3], 0.0, factor)
                half = hidden * (0.5 * factor) * vec_ref[1]
                acts.append(half * (1.0 + jnp.tanh(half)))
            a0, a1, a2, a3 = acts
            for n, u in enumerate((a0 - a2, a1 + a2, a2 - a1, a1 - a3)):
                for dx, piece in enumerate(moved(u)):
                    act[n, f + 2, dx * vc : dx * vc + vc] = piece.astype(jnp.bfloat16)

        @pl.when(here & (step == 0))
        def _():
            for load in loads:
                load.start()
            lat[:2] = jnp.zeros((2, 6, 3 * lc, lw), jnp.bfloat16)
            act[:, :2] = jnp.zeros((4, 2, deep, lw), jnp.bfloat16)
            cells = clip_ref[...].astype(jnp.float32)
            for dx, piece in enumerate(moved(cells)):
                lat[2:, :, dx * lc : dx * lc + lc] = piece.astype(jnp.bfloat16)

            @pl.loop(0, lot)
            def _(f):
                first(f)

            for load in loads:
                load.wait()

        def second(and_next):
            base = lot * step
            for n in range(4):
                taps = jnp.concatenate(
                    [act[n, pl.ds(base + j, 3)].reshape(3 * deep, lw) for j in range(lot)], axis=1
                )
                m = jnp.dot(w2[n], taps, preferred_element_type=jnp.float32)
                if n == 0:
                    both[0] = m
                if n == 1:
                    both[0] += m
                    both[1] = m
                if n == 2:
                    both[0] += m
                    both[1] -= m
                if n == 3:
                    both[1] -= m
                if and_next:
                    first(base + lot + n)
            for j in range(lot):
                for r in range(2):
                    whole = both[r, :, j * lw : j * lw + lw]
                    whole += vec_ref[2] + firsts[lax.rem(base + j, 2 * lot), r]
                    out_ref[j, r] = jnp.transpose(whole).astype(jnp.bfloat16)

        @pl.when(here & (step < frames // lot - 1))
        def _():
            second(True)

        @pl.when(here & (step == frames // lot - 1))
        def _():
            second(False)

        @pl.when(jnp.logical_not(here))
        def _():
            out_ref[...] = jnp.zeros(out_ref.shape, out_ref.dtype)

    return pl.pallas_call(
        body,
        grid=(frames // lot,),
        out_shape=jax.ShapeDtypeStruct((frames, 2, lw, vc), jnp.bfloat16),
        in_specs=[
            smem_spec(),
            vmem_spec(),
            vmem_spec(),
            pl.BlockSpec(memory_space=pl.ANY),
            vmem_spec(),
        ],
        out_specs=pl.BlockSpec((lot, 2, lw, vc), lambda i: (i, 0, 0, 0)),
        scratch_shapes=[
            pltpu.VMEM((frames + 2, 6, 3 * lc, lw), jnp.bfloat16),
            pltpu.VMEM((4, frames + 2, deep, lw), jnp.bfloat16),
            pltpu.VMEM((2 * lot, 2, vc, lw), jnp.float32),
            pltpu.VMEM((4, vc, 3 * deep), jnp.bfloat16),
            pltpu.VMEM((2, vc, lot * lw), jnp.float32),
            pltpu.SemaphoreType.DMA((4,)),
        ],
        compiler_params=pltpu.CompilerParams(vmem_limit_bytes=56 * MIB),
        cost_estimate=pl.CostEstimate(
            flops=8 * frames * lw * 3 * deep * vc,
            bytes_accessed=frames * 2 * lw * vc * 2 + 12 * deep * vc * 2,
            transcendentals=frames * 4 * lw * vc,
        ),
        name="decode",
    )(place, clip, w_first, filters, vectors)


def on_device(
    query_input,
    key_input,
    value_input,
    resid,
    gate,
    query_norm_gain,
    key_norm_gain,
    output_weight,
    latents,
    w_in,
    b_in,
    norm_gain,
    w_mid,
    b_mid,
):
    last = lax.axis_size("grp") - 1
    decoder_here = lax.axis_index("grp") == last
    count = lax.axis_size(SEQ)
    side = lax.axis_size("z")
    core, at_z, at_x = lax.axis_index("core"), lax.axis_index("z"), lax.axis_index("x")
    place = jnp.stack(
        [
            decoder_here.astype(jnp.int32),
            core,
            lax.axis_index(SEQ),
            jnp.int32(count - 1),
            jnp.where(core == 0, at_z, at_x),
            jnp.where(core == 0, at_x, at_z),
        ]
    )
    channels = w_in.shape[2]

    def along(first_ring, shift):
        pairs = []
        for g in range(last):
            for z in range(side):
                for x in range(side):
                    for c in range(2):
                        on_z = (c == 0) == first_ring
                        to_z = (z + shift) % side if on_z else z
                        to_x = x if on_z else (x + shift) % side
                        at = g * count
                        pairs.append((at + (z * side + x) * 2 + c, at + (to_z * side + to_x) * 2 + c))
        return pairs

    def send(x, first_ring, shift):
        return lax.ppermute(x, ("grp",) + SEQ, along(first_ring, shift))

    swap = [(2 * i, 2 * i + 1) for i in range(last * count // 2)]
    swap += [(b, a) for a, b in swap]

    own = jnp.swapaxes(latents, 2, 3)
    clip = jnp.concatenate(
        [lax.ppermute(own, "grp", [(g, last)]) for g in range(last)] + [own], axis=0
    )
    packed = norm_pack(
        query_input[0], key_input[0], value_input[0], query_norm_gain[None], key_norm_gain[None]
    )
    filters = filter_weights(place, w_mid)
    packed, clip = lax.optimization_barrier((packed, clip))
    here = lax.all_to_all(packed, CHIPS, split_axis=0, concat_axis=0, tiled=True)

    links = [(last * count + i, last * count + i + 1) for i in range(count - 1)]
    cells = jnp.concatenate(
        [
            lax.ppermute(clip, ("grp",) + SEQ, links),
            clip,
            lax.ppermute(clip, ("grp",) + SEQ, [(b, a) for a, b in links]),
        ],
        axis=1,
    )
    w_first = jnp.pad(w_in.reshape(-1, channels).T, ((0, 0), (0, 512 - 27 * latents.shape[3])))
    vectors = jnp.broadcast_to(
        jnp.stack([b_in, norm_gain, b_mid])[:, :, None], (3, channels, latents.shape[2])
    )
    decoded = decode(place, cells, w_first, filters, vectors)

    weight_there = lax.ppermute(output_weight, ("grp",) + SEQ, swap)
    w_own, w_up, w_down = weight_blocks(place, output_weight, weight_there)
    w_below, w_above = send(w_up, True, 1), send(w_down, True, -1)
    w_far = send(w_below[256:], True, 1), send(w_above[256:], True, -1)

    here, decoded = lax.optimization_barrier((here, decoded))
    there = lax.ppermute(here, ("grp",) + SEQ, swap)
    heads = attend(place, here, there)
    below, above = send(heads, True, 1), send(heads, True, -1)
    middle = heads.shape[0] // 2
    far = send(below[:middle], True, 1), send(above[middle:], True, -1)
    far_low, far_high, up, down, mine = project(
        place, (heads, below, above) + far, (w_own, w_below, w_above) + w_far
    )
    up, down = add_passed(up, down, send(far_low, False, 1), send(far_high, False, -1))
    sums = add_blocks(place, mine, send(up, False, 1), send(down, False, -1))
    blocks = (sums[0], send(sums[3], True, -1), send(sums[2], True, 2), send(sums[1], True, 1))
    attn_out = finish(place, resid[0], gate, blocks)
    return attn_out[None], decoded[None]


def solution(mesh):
    fine = Mesh(mesh.devices.reshape(4, 4, 4, 2), ("grp",) + SEQ)
    placed = (
        P("grp", SEQ, None),
        P("grp", SEQ, None),
        P("grp", SEQ, None),
        P("grp", SEQ, None),
        P("grp", None),
        P(),
        P(),
        P(SEQ, None),
        P("grp", SEQ, None, None),
        P(),
        P(),
        P(),
        P(),
        P(),
    )
    return jax.shard_map(
        on_device,
        mesh=fine,
        in_specs=placed,
        out_specs=(P("grp", SEQ, None), P("grp", None, SEQ, None, None)),
        check_vma=False,
    )
```

```python
import math
import jax
import jax.numpy as jnp
from jax import lax
from jax.experimental import pallas as pl
from jax.experimental.pallas import tpu as pltpu
from jax.sharding import Mesh, PartitionSpec as P

CHIPS = ("z", "x")
SEQ = ("z", "x", "core")
EPS = 1e-06
MIB = 1024 * 1024


def vmem_spec():
    return pl.BlockSpec(memory_space=pltpu.VMEM)


def smem_spec():
    return pl.BlockSpec(memory_space=pltpu.SMEM)


def norm_pack(q, k, v, gain_q, gain_k):
    rows, width = q.shape
    chips = width // 256
    block = 16

    def body(q_ref, k_ref, v_ref, gq_ref, gk_ref, out_ref):
        def normed(ref, gain):
            x = ref[...].astype(jnp.float32)
            factor = lax.rsqrt(jnp.mean(x * x, axis=-1, keepdims=True) + EPS)
            return (x * factor * gain).astype(jnp.bfloat16)

        scale = 128**-0.5 * math.log2(math.e)
        qn = normed(q_ref, gq_ref[...] * scale)
        kn = normed(k_ref, gk_ref[...])
        for c in range(chips):
            cols = slice(256 * c, 256 * c + 256)
            out_ref[c, 0] = qn[:, cols]
            out_ref[c, 1] = kn[:, cols]
            out_ref[c, 2] = v_ref[:, cols]

    tokens = pl.BlockSpec((block, width), lambda i: (i, 0))
    gains = pl.BlockSpec((1, width), lambda i: (0, 0))
    return pl.pallas_call(
        body,
        grid=(rows // block,),
        out_shape=jax.ShapeDtypeStruct((chips, 3, rows, 256), jnp.bfloat16),
        in_specs=[tokens, tokens, tokens, gains, gains],
        out_specs=pl.BlockSpec((chips, 3, block, 256), lambda i: (0, 0, i, 0)),
        compiler_params=pltpu.CompilerParams(vmem_limit_bytes=60 * MIB),
        name="norm_pack",
    )(q, k, v, gain_q, gain_k)


def weight_halves(place, w_here, w_there):
    rows, width = w_here.shape
    part = width // 2

    def body(place_ref, here_ref, there_ref, keep_ref, give_ref):
        here_at = pl.ds(pl.multiple_of(place_ref[1] * rows, rows), rows)
        there_at = pl.ds(pl.multiple_of((1 - place_ref[1]) * rows, rows), rows)

        @pl.when(place_ref[0] == 0)
        def _():
            for k, out in enumerate((keep_ref, give_ref)):
                half = jnp.bitwise_xor(place_ref[4] // 2, k)
                at = pl.ds(pl.multiple_of(half * part, part), part)
                out[here_at] = here_ref[:, at]
                out[there_at] = there_ref[:, at]

    return pl.pallas_call(
        body,
        out_shape=(jax.ShapeDtypeStruct((2 * rows, part), jnp.bfloat16),) * 2,
        in_specs=[smem_spec(), vmem_spec(), vmem_spec()],
        out_specs=(vmem_spec(),) * 2,
        compiler_params=pltpu.CompilerParams(vmem_limit_bytes=16 * MIB),
        name="weight_halves",
    )(place, w_here, w_there)


def inner(position):
    return ((position + 1) // 2) % 2


def attend(place, here, there):
    chips, _, tok, _ = here.shape
    half = chips * tok
    keys = 2 * half

    def body(place_ref, here_ref, there_ref, near_ref, other_ref, k_buf, v_buf):
        step = pl.program_id(0)

        @pl.when((step == 0) & (place_ref[0] == 0))
        def _():
            for h in range(2):
                cols = slice(128 * h, 128 * h + 128)
                for n, ref in enumerate((here_ref, there_ref)):
                    span = slice(n * half, n * half + half)
                    k_buf[h, span] = ref[:, 1, :, cols].reshape(half, 128)
                    v_buf[h, span, :128] = ref[:, 2, :, cols].reshape(half, 128)
                v_buf[h, :, 128:] = jnp.ones((keys, 128), jnp.bfloat16)

        @pl.when(place_ref[0] == 0)
        def _():
            queries = here_ref[pl.ds(4 * step, 4), 0].reshape(4 * tok, 256)
            heads = []
            for h in range(2):
                s = lax.dot_general(
                    queries[:, 128 * h : 128 * h + 128],
                    k_buf[h],
                    (((1,), (1,)), ((), ())),
                    preferred_element_type=jnp.float32,
                )
                p = jnp.exp2(s - jnp.max(s, axis=-1, keepdims=True)).astype(jnp.bfloat16)
                o = jnp.dot(p, v_buf[h], preferred_element_type=jnp.float32)
                heads.append(o[:, :128] / o[:, 128:])
            joined = jnp.concatenate(heads, axis=1).astype(jnp.bfloat16)
            for n in range(4):
                first = jnp.where(place_ref[1] == 0, step, n)
                second = jnp.where(place_ref[1] == 0, n, step)
                high = first // 2
                slot = jnp.where(second == 0, 0, jnp.where(second == 3, 1, second + 1))
                near = inner(first) == inner(place_ref[4])
                piece = joined[tok * n : tok * n + tok]

                @pl.when(near)
                def _():
                    near_ref[slot, high] = piece

                @pl.when(jnp.logical_not(near))
                def _():
                    other_ref[slot, high] = piece

    return pl.pallas_call(
        body,
        grid=(chips // 4,),
        out_shape=(jax.ShapeDtypeStruct((4, 2, tok, 256), jnp.bfloat16),) * 2,
        in_specs=[smem_spec(), vmem_spec(), vmem_spec()],
        out_specs=(vmem_spec(),) * 2,
        scratch_shapes=[
            pltpu.VMEM((2, keys, 128), jnp.bfloat16),
            pltpu.VMEM((2, keys, 256), jnp.bfloat16),
        ],
        compiler_params=pltpu.CompilerParams(vmem_limit_bytes=40 * MIB),
        cost_estimate=pl.CostEstimate(flops=0, bytes_accessed=0, transcendentals=0),
        name="attend",
    )(place, here, there)


def project(place, heads, weights):
    _, two, tok, _ = heads[0].shape
    part = weights[0].shape[1]
    lot = two * tok

    def body(place_ref, h0, h1, h2, h3, w0, w1, w2, w3, own_ref, one_ref, zero_ref, far_ref):
        second = place_ref[5]
        slot = jnp.where(second == 0, 0, jnp.where(second == 3, 1, second + 1))

        @pl.when(place_ref[0] == 0)
        def _():
            weight = jnp.concatenate([w0[...], w1[...], w2[...], w3[...]], axis=0)
            feats = jnp.concatenate(
                [
                    jnp.concatenate(
                        [h[jnp.bitwise_xor(slot, k)].reshape(lot, 256) for h in (h0, h1, h2, h3)],
                        axis=1,
                    )
                    for k in range(4)
                ],
                axis=0,
            )
            out = jnp.dot(feats, weight, preferred_element_type=jnp.float32)
            for k, ref in enumerate((own_ref, one_ref, zero_ref, far_ref)):
                ref[...] = out[lot * k : lot * k + lot].reshape(two, tok, part).astype(ref.dtype)

    shape = (two, tok, part)
    return pl.pallas_call(
        body,
        out_shape=(jax.ShapeDtypeStruct(shape, jnp.float32),)
        + (jax.ShapeDtypeStruct(shape, jnp.bfloat16),) * 3,
        in_specs=[smem_spec()] + [vmem_spec()] * 8,
        out_specs=(vmem_spec(),) * 4,
        compiler_params=pltpu.CompilerParams(vmem_limit_bytes=40 * MIB),
        cost_estimate=pl.CostEstimate(
            flops=8 * lot * 1024 * part, bytes_accessed=8 * MIB, transcendentals=0
        ),
        name="project",
    )(place, *heads, *weights)


def add_up(place, own, others):
    def body(place_ref, own_ref, a_ref, b_ref, c_ref, keep_ref, give_ref):
        mine = place_ref[4] // 2

        @pl.when(place_ref[0] == 0)
        def _():
            for at, out in ((mine, keep_ref), (1 - mine, give_ref)):
                total = own_ref[at]
                for ref in (a_ref, b_ref, c_ref):
                    total += ref[at].astype(jnp.float32)
                out[...] = total.astype(out.dtype)

    return pl.pallas_call(
        body,
        out_shape=(
            jax.ShapeDtypeStruct(own.shape[1:], jnp.float32),
            jax.ShapeDtypeStruct(own.shape[1:], jnp.bfloat16),
        ),
        in_specs=[smem_spec()] + [vmem_spec()] * 4,
        out_specs=(vmem_spec(),) * 2,
        compiler_params=pltpu.CompilerParams(vmem_limit_bytes=24 * MIB),
        name="add_up",
    )(place, own, *others)


def finish(place, resid, gate, kept, got):
    part = kept.shape[1]

    def body(place_ref, resid_ref, gate_ref, kept_ref, got_ref, out_ref):
        @pl.when(place_ref[0] == 0)
        def _():
            for k, ref in enumerate((kept_ref, got_ref)):
                half = jnp.bitwise_xor(place_ref[4] // 2, k)
                at = pl.ds(pl.multiple_of(half * part, part), part)
                total = resid_ref[:, at].astype(jnp.float32)
                total += gate_ref[:, at] * ref[...].astype(jnp.float32)
                out_ref[:, at] = total.astype(jnp.bfloat16)

        @pl.when(place_ref[0] == 1)
        def _():
            out_ref[...] = jnp.zeros(out_ref.shape, out_ref.dtype)

    return pl.pallas_call(
        body,
        out_shape=jax.ShapeDtypeStruct(resid.shape, jnp.bfloat16),
        in_specs=[smem_spec()] + [vmem_spec()] * 4,
        out_specs=vmem_spec(),
        compiler_params=pltpu.CompilerParams(vmem_limit_bytes=16 * MIB),
        name="finish",
    )(place, resid, gate, kept, got)


def filter_weights(place, w_mid):
    steps, deep, vc = w_mid.shape
    taps = w_mid.reshape(steps, 3, 3, vc, vc)

    def block(w_ref, out_ref):
        up, mid, down = (w_ref[0, n, 0] for n in range(3))
        ends = 0.5 * (up.astype(jnp.float32) + down.astype(jnp.float32))
        half = 0.5 * mid.astype(jnp.float32)
        for n, g in enumerate((up, ends + half, ends - half, down)):
            out_ref[n] = jnp.transpose(g.astype(jnp.bfloat16))

    def body(place_ref, w_ref, out_ref):
        @pl.when(place_ref[0] == 1)
        def _():
            pltpu.emit_pipeline(
                block,
                grid=(3 * steps,),
                in_specs=[pl.BlockSpec((1, 3, 1, vc, vc), lambda i: (i // 3, 0, i % 3, 0, 0))],
                out_specs=[pl.BlockSpec((4, vc, vc), lambda i: (0, 0, i))],
            )(w_ref, out_ref)

    return pl.pallas_call(
        body,
        out_shape=jax.ShapeDtypeStruct((4, vc, deep), jnp.bfloat16),
        in_specs=[smem_spec(), pl.BlockSpec(memory_space=pl.ANY)],
        out_specs=pl.BlockSpec(memory_space=pl.ANY),
        compiler_params=pltpu.CompilerParams(vmem_limit_bytes=60 * MIB),
        name="filter_weights",
    )(place, taps)


def decode(place, clip, w_first, filters, vectors):
    frames, _, lc, lw = clip.shape
    vc = w_first.shape[0]
    deep = 3 * vc
    lot = 4

    def body(place_ref, clip_ref, w1_ref, f_ref, vec_ref, out_ref, lat, act, firsts, w2, both, sems):
        step = pl.program_id(0)
        here = place_ref[0] == 1
        loads = [pltpu.make_async_copy(f_ref.at[n], w2.at[n], sems.at[n]) for n in range(4)]

        def moved(x):
            lane = lax.broadcasted_iota(jnp.int32, x.shape, x.ndim - 1)
            left = jnp.where(lane == 0, 0.0, pltpu.roll(x, 1, x.ndim - 1))
            right = jnp.where(lane == lw - 1, 0.0, pltpu.roll(x, lw - 1, x.ndim - 1))
            return left, x, right

        def first(f):
            sides = []
            for row in range(4):
                taps = [lat[f + dt, row : row + 3].reshape(9 * lc, lw) for dt in range(3)]
                taps.append(jnp.zeros((w1_ref.shape[1] - 27 * lc, lw), jnp.bfloat16))
                sides.append(jnp.concatenate(taps, axis=0))
            y = jnp.dot(
                w1_ref[...], jnp.concatenate(sides, axis=1), preferred_element_type=jnp.float32
            )
            acts = []
            for row in range(4):
                hidden = y[:, row * lw : row * lw + lw] + vec_ref[0]
                hidden = hidden.astype(jnp.bfloat16).astype(jnp.float32)
                if row in (1, 2):
                    firsts[lax.rem(f, 2 * lot), row - 1] = hidden
                factor = lax.rsqrt(jnp.mean(hidden * hidden, axis=0, keepdims=True) + EPS)
                if row == 0:
                    factor = jnp.where(place_ref[2] == 0, 0.0, factor)
                if row == 3:
                    factor = jnp.where(place_ref[2] == place_ref[3], 0.0, factor)
                half = hidden * (0.5 * factor) * vec_ref[1]
                acts.append(half * (1.0 + jnp.tanh(half)))
            a0, a1, a2, a3 = acts
            for n, u in enumerate((a0 - a2, a1 + a2, a2 - a1, a1 - a3)):
                for dx, piece in enumerate(moved(u)):
                    act[n, f + 2, dx * vc : dx * vc + vc] = piece.astype(jnp.bfloat16)

        @pl.when(here & (step == 0))
        def _():
            for load in loads:
                load.start()
            lat[:2] = jnp.zeros((2, 6, 3 * lc, lw), jnp.bfloat16)
            act[:, :2] = jnp.zeros((4, 2, deep, lw), jnp.bfloat16)
            cells = clip_ref[...].astype(jnp.float32)
            for dx, piece in enumerate(moved(cells)):
                lat[2:, :, dx * lc : dx * lc + lc] = piece.astype(jnp.bfloat16)

            @pl.loop(0, lot)
            def _(f):
                first(f)

            for load in loads:
                load.wait()

        def second(and_next):
            base = lot * step
            for n in range(4):
                taps = jnp.concatenate(
                    [act[n, pl.ds(base + j, 3)].reshape(3 * deep, lw) for j in range(lot)], axis=1
                )
                m = jnp.dot(w2[n], taps, preferred_element_type=jnp.float32)
                if n == 0:
                    both[0] = m
                if n == 1:
                    both[0] += m
                    both[1] = m
                if n == 2:
                    both[0] += m
                    both[1] -= m
                if n == 3:
                    both[1] -= m
                if and_next:
                    first(base + lot + n)
            for j in range(lot):
                for r in range(2):
                    whole = both[r, :, j * lw : j * lw + lw]
                    whole += vec_ref[2] + firsts[lax.rem(base + j, 2 * lot), r]
                    out_ref[j, r] = jnp.transpose(whole).astype(jnp.bfloat16)

        @pl.when(here & (step < frames // lot - 1))
        def _():
            second(True)

        @pl.when(here & (step == frames // lot - 1))
        def _():
            second(False)

        @pl.when(jnp.logical_not(here))
        def _():
            out_ref[...] = jnp.zeros(out_ref.shape, out_ref.dtype)

    return pl.pallas_call(
        body,
        grid=(frames // lot,),
        out_shape=jax.ShapeDtypeStruct((frames, 2, lw, vc), jnp.bfloat16),
        in_specs=[
            smem_spec(),
            vmem_spec(),
            vmem_spec(),
            pl.BlockSpec(memory_space=pl.ANY),
            vmem_spec(),
        ],
        out_specs=pl.BlockSpec((lot, 2, lw, vc), lambda i: (i, 0, 0, 0)),
        scratch_shapes=[
            pltpu.VMEM((frames + 2, 6, 3 * lc, lw), jnp.bfloat16),
            pltpu.VMEM((4, frames + 2, deep, lw), jnp.bfloat16),
            pltpu.VMEM((2 * lot, 2, vc, lw), jnp.float32),
            pltpu.VMEM((4, vc, 3 * deep), jnp.bfloat16),
            pltpu.VMEM((2, vc, lot * lw), jnp.float32),
            pltpu.SemaphoreType.DMA((4,)),
        ],
        compiler_params=pltpu.CompilerParams(vmem_limit_bytes=48 * MIB),
        cost_estimate=pl.CostEstimate(flops=0, bytes_accessed=0, transcendentals=0),
        name="decode",
    )(place, clip, w_first, filters, vectors)


def on_device(
    query_input,
    key_input,
    value_input,
    resid,
    gate,
    query_norm_gain,
    key_norm_gain,
    output_weight,
    latents,
    w_in,
    b_in,
    norm_gain,
    w_mid,
    b_mid,
):
    last = lax.axis_size("grp") - 1
    decoder_here = lax.axis_index("grp") == last
    count = lax.axis_size(SEQ)
    side = lax.axis_size("z")
    core, at_z, at_x = lax.axis_index("core"), lax.axis_index("z"), lax.axis_index("x")
    place = jnp.stack(
        [
            decoder_here.astype(jnp.int32),
            core,
            lax.axis_index(SEQ),
            jnp.int32(count - 1),
            jnp.where(core == 0, at_z, at_x),
            jnp.where(core == 0, at_x, at_z),
        ]
    )
    channels = w_in.shape[2]

    def swap(x, ring, step):
        def partner(place):
            return (place ^ 1, side - 1 - place, place ^ 2)[step]

        pairs = []
        for at in range(last * count):
            g, z, x_, c = at // count, at // (2 * side) % side, at // 2 % side, at % 2
            if ring == 2:
                c = 1 - c
            elif (ring == 0) == (c == 0):
                z = partner(z)
            else:
                x_ = partner(x_)
            pairs.append((at, ((g * side + z) * side + x_) * 2 + c))
        return lax.ppermute(x, ("grp",) + SEQ, pairs)

    w_there = swap(output_weight, 2, 0)
    packed = norm_pack(
        query_input[0], key_input[0], value_input[0], query_norm_gain[None], key_norm_gain[None]
    )
    packed, w_there = lax.optimization_barrier((packed, w_there))
    here = lax.all_to_all(packed, CHIPS, split_axis=0, concat_axis=0, tiled=True)
    w_own, w_give = weight_halves(place, output_weight, w_there)
    w_own, w_give, latents, w_mid = lax.optimization_barrier((w_own, w_give, latents, w_mid))
    w_next, w_back, w_far = swap(w_own, 0, 0), swap(w_give, 0, 1), swap(w_give, 0, 2)

    own = jnp.swapaxes(latents, 2, 3)
    pieces = [lax.ppermute(own, "grp", [(g, last)]) for g in range(last)]
    filters = filter_weights(place, w_mid)
    pieces, filters = lax.optimization_barrier((pieces, filters))
    clip = jnp.concatenate(pieces + [own], axis=0)
    here, w_next, w_back, clip = lax.optimization_barrier((here, w_next, w_back, clip))
    links = [(last * count + i, last * count + i + 1) for i in range(count - 1)]
    cells = jnp.concatenate(
        [
            lax.ppermute(clip, ("grp",) + SEQ, links),
            clip,
            lax.ppermute(clip, ("grp",) + SEQ, [(b, a) for a, b in links]),
        ],
        axis=1,
    )
    w_first = jnp.pad(w_in.reshape(-1, channels).T, ((0, 0), (0, 512 - 27 * latents.shape[3])))
    vectors = jnp.broadcast_to(
        jnp.stack([b_in, norm_gain, b_mid])[:, :, None], (3, channels, latents.shape[2])
    )
    there = swap(here, 2, 0)
    near, other = attend(place, here, there)
    heads = near, swap(other, 0, 0), swap(near, 0, 1), swap(other, 0, 2)
    mine, one, zero, far = project(place, heads, (w_own, w_next, w_back, w_far))
    mine, one, zero, far, cells = lax.optimization_barrier((mine, one, zero, far, cells))
    decoded = decode(place, cells, w_first, filters, vectors)
    kept, give = add_up(place, mine, (swap(one, 1, 1), swap(zero, 1, 0), swap(far, 1, 2)))
    attn_out = finish(place, resid[0], gate, kept, swap(give, 0, 1))
    return attn_out[None], decoded[None]


def solution(mesh):
    fine = Mesh(mesh.devices.reshape(4, 4, 4, 2), ("grp",) + SEQ)
    placed = (
        P("grp", SEQ, None),
        P("grp", SEQ, None),
        P("grp", SEQ, None),
        P("grp", SEQ, None),
        P("grp", None),
        P(),
        P(),
        P(SEQ, None),
        P("grp", SEQ, None, None),
        P(),
        P(),
        P(),
        P(),
        P(),
    )
    return jax.shard_map(
        on_device,
        mesh=fine,
        in_specs=placed,
        out_specs=(P("grp", SEQ, None), P("grp", None, SEQ, None, None)),
        check_vma=False,
    )
```

```python
import math
import jax
import jax.numpy as jnp
from jax import lax
from jax.experimental import pallas as pl
from jax.experimental.pallas import tpu as pltpu
from jax.sharding import Mesh, PartitionSpec as P

CHIPS = ("z", "x")
SEQ = ("z", "x", "core")
EPS = 1e-06
MIB = 1024 * 1024


def vmem_spec():
    return pl.BlockSpec(memory_space=pltpu.VMEM)


def smem_spec():
    return pl.BlockSpec(memory_space=pltpu.SMEM)


def norm_pack(q, k, v, gain_q, gain_k):
    rows, width = q.shape
    chips = width // 256
    block = 16

    def body(q_ref, k_ref, v_ref, gq_ref, gk_ref, out_ref):
        def normed(ref, gain):
            x = ref[...].astype(jnp.float32)
            factor = lax.rsqrt(jnp.mean(x * x, axis=-1, keepdims=True) + EPS)
            return (x * factor * gain).astype(jnp.bfloat16)

        scale = 128**-0.5 * math.log2(math.e)
        qn = normed(q_ref, gq_ref[...] * scale)
        kn = normed(k_ref, gk_ref[...])
        for c in range(chips):
            cols = slice(256 * c, 256 * c + 256)
            out_ref[c, 0] = qn[:, cols]
            out_ref[c, 1] = kn[:, cols]
            out_ref[c, 2] = v_ref[:, cols]

    tokens = pl.BlockSpec((block, width), lambda i: (i, 0))
    gains = pl.BlockSpec((1, width), lambda i: (0, 0))
    return pl.pallas_call(
        body,
        grid=(rows // block,),
        out_shape=jax.ShapeDtypeStruct((chips, 3, rows, 256), jnp.bfloat16),
        in_specs=[tokens, tokens, tokens, gains, gains],
        out_specs=pl.BlockSpec((chips, 3, block, 256), lambda i: (0, 0, i, 0)),
        compiler_params=pltpu.CompilerParams(vmem_limit_bytes=60 * MIB),
        name="norm_pack",
    )(q, k, v, gain_q, gain_k)


def weight_halves(place, w_here, w_there):
    rows, width = w_here.shape
    part = width // 2

    def body(place_ref, here_ref, there_ref, keep_ref, give_ref):
        here_at = pl.ds(pl.multiple_of(place_ref[1] * rows, rows), rows)
        there_at = pl.ds(pl.multiple_of((1 - place_ref[1]) * rows, rows), rows)

        @pl.when(place_ref[0] == 0)
        def _():
            for k, out in enumerate((keep_ref, give_ref)):
                half = jnp.bitwise_xor(place_ref[4] // 2, k)
                at = pl.ds(pl.multiple_of(half * part, part), part)
                out[here_at] = here_ref[:, at]
                out[there_at] = there_ref[:, at]

    return pl.pallas_call(
        body,
        out_shape=(jax.ShapeDtypeStruct((2 * rows, part), jnp.bfloat16),) * 2,
        in_specs=[smem_spec(), vmem_spec(), vmem_spec()],
        out_specs=(vmem_spec(),) * 2,
        compiler_params=pltpu.CompilerParams(vmem_limit_bytes=16 * MIB),
        name="weight_halves",
    )(place, w_here, w_there)


def inner(position):
    return ((position + 1) // 2) % 2


def attend(place, here, there):
    chips, _, tok, _ = here.shape
    half = chips * tok

    def body(place_ref, here_ref, there_ref, near_ref, other_ref):
        step = pl.program_id(0)

        @pl.when(place_ref[0] == 0)
        def _():
            queries = here_ref[pl.ds(4 * step, 4), 0].reshape(4 * tok, 256)
            ones = jnp.ones((half, 128), jnp.bfloat16)
            heads = []
            for h in range(2):
                cols = slice(128 * h, 128 * h + 128)
                scores = [
                    lax.dot_general(
                        queries[:, cols],
                        ref[:, 1, :, cols].reshape(half, 128),
                        (((1,), (1,)), ((), ())),
                        preferred_element_type=jnp.float32,
                    )
                    for ref in (here_ref, there_ref)
                ]
                peak = jnp.maximum(*(jnp.max(s, axis=-1, keepdims=True) for s in scores))
                o = None
                for s, ref in zip(scores, (here_ref, there_ref)):
                    values = jnp.concatenate([ref[:, 2, :, cols].reshape(half, 128), ones], axis=1)
                    p = jnp.exp2(s - peak).astype(jnp.bfloat16)
                    part = jnp.dot(p, values, preferred_element_type=jnp.float32)
                    o = part if o is None else o + part
                heads.append(o[:, :128] / o[:, 128:])
            joined = jnp.concatenate(heads, axis=1).astype(jnp.bfloat16)
            for n in range(4):
                first = jnp.where(place_ref[1] == 0, step, n)
                second = jnp.where(place_ref[1] == 0, n, step)
                high = first // 2
                slot = jnp.where(second == 0, 0, jnp.where(second == 3, 1, second + 1))
                near = inner(first) == inner(place_ref[4])
                piece = joined[tok * n : tok * n + tok]

                @pl.when(near)
                def _():
                    near_ref[slot, high] = piece

                @pl.when(jnp.logical_not(near))
                def _():
                    other_ref[slot, high] = piece

    return pl.pallas_call(
        body,
        grid=(chips // 4,),
        out_shape=(jax.ShapeDtypeStruct((4, 2, tok, 256), jnp.bfloat16),) * 2,
        in_specs=[smem_spec(), vmem_spec(), vmem_spec()],
        out_specs=(vmem_spec(),) * 2,
        compiler_params=pltpu.CompilerParams(vmem_limit_bytes=40 * MIB),
        cost_estimate=pl.CostEstimate(flops=0, bytes_accessed=0, transcendentals=0),
        name="attend",
    )(place, here, there)


def project(place, heads, weights):
    _, two, tok, _ = heads[0].shape
    part = weights[0].shape[1]
    lot = two * tok

    def body(place_ref, h0, h1, h2, h3, w0, w1, w2, w3, own_ref, one_ref, zero_ref, far_ref):
        second = place_ref[5]
        slot = jnp.where(second == 0, 0, jnp.where(second == 3, 1, second + 1))

        @pl.when(place_ref[0] == 0)
        def _():
            weight = jnp.concatenate([w0[...], w1[...], w2[...], w3[...]], axis=0)
            feats = jnp.concatenate(
                [
                    jnp.concatenate(
                        [h[jnp.bitwise_xor(slot, k)].reshape(lot, 256) for h in (h0, h1, h2, h3)],
                        axis=1,
                    )
                    for k in range(4)
                ],
                axis=0,
            )
            out = jnp.dot(feats, weight, preferred_element_type=jnp.float32)
            for k, ref in enumerate((own_ref, one_ref, zero_ref, far_ref)):
                ref[...] = out[lot * k : lot * k + lot].reshape(two, tok, part).astype(ref.dtype)

    shape = (two, tok, part)
    return pl.pallas_call(
        body,
        out_shape=(jax.ShapeDtypeStruct(shape, jnp.float32),)
        + (jax.ShapeDtypeStruct(shape, jnp.bfloat16),) * 3,
        in_specs=[smem_spec()] + [vmem_spec()] * 8,
        out_specs=(vmem_spec(),) * 4,
        compiler_params=pltpu.CompilerParams(vmem_limit_bytes=40 * MIB),
        cost_estimate=pl.CostEstimate(
            flops=8 * lot * 1024 * part, bytes_accessed=8 * MIB, transcendentals=0
        ),
        name="project",
    )(place, *heads, *weights)


def add_up(place, own, others):
    def body(place_ref, own_ref, a_ref, b_ref, c_ref, keep_ref, give_ref):
        mine = place_ref[4] // 2

        @pl.when(place_ref[0] == 0)
        def _():
            for at, out in ((mine, keep_ref), (1 - mine, give_ref)):
                total = own_ref[at]
                for ref in (a_ref, b_ref, c_ref):
                    total += ref[at].astype(jnp.float32)
                out[...] = total.astype(out.dtype)

    return pl.pallas_call(
        body,
        out_shape=(
            jax.ShapeDtypeStruct(own.shape[1:], jnp.float32),
            jax.ShapeDtypeStruct(own.shape[1:], jnp.bfloat16),
        ),
        in_specs=[smem_spec()] + [vmem_spec()] * 4,
        out_specs=(vmem_spec(),) * 2,
        compiler_params=pltpu.CompilerParams(vmem_limit_bytes=24 * MIB),
        name="add_up",
    )(place, own, *others)


def finish(place, resid, gate, kept, got):
    part = kept.shape[1]

    def body(place_ref, resid_ref, gate_ref, kept_ref, got_ref, out_ref):
        @pl.when(place_ref[0] == 0)
        def _():
            for k, ref in enumerate((kept_ref, got_ref)):
                half = jnp.bitwise_xor(place_ref[4] // 2, k)
                at = pl.ds(pl.multiple_of(half * part, part), part)
                total = resid_ref[:, at].astype(jnp.float32)
                total += gate_ref[:, at] * ref[...].astype(jnp.float32)
                out_ref[:, at] = total.astype(jnp.bfloat16)

        @pl.when(place_ref[0] == 1)
        def _():
            out_ref[...] = jnp.zeros(out_ref.shape, out_ref.dtype)

    return pl.pallas_call(
        body,
        out_shape=jax.ShapeDtypeStruct(resid.shape, jnp.bfloat16),
        in_specs=[smem_spec()] + [vmem_spec()] * 4,
        out_specs=vmem_spec(),
        compiler_params=pltpu.CompilerParams(vmem_limit_bytes=16 * MIB),
        name="finish",
    )(place, resid, gate, kept, got)


def filter_weights(place, w_mid):
    steps, deep, vc = w_mid.shape
    taps = w_mid.reshape(steps, 3, 3, vc, vc)

    def block(w_ref, out_ref):
        up, mid, down = (w_ref[0, n, 0] for n in range(3))
        ends = 0.5 * (up.astype(jnp.float32) + down.astype(jnp.float32))
        half = 0.5 * mid.astype(jnp.float32)
        for n, g in enumerate((up, ends + half, ends - half, down)):
            out_ref[n] = jnp.transpose(g.astype(jnp.bfloat16))

    def body(place_ref, w_ref, out_ref):
        @pl.when(place_ref[0] == 1)
        def _():
            pltpu.emit_pipeline(
                block,
                grid=(3 * steps,),
                in_specs=[pl.BlockSpec((1, 3, 1, vc, vc), lambda i: (i // 3, 0, i % 3, 0, 0))],
                out_specs=[pl.BlockSpec((4, vc, vc), lambda i: (0, 0, i))],
            )(w_ref, out_ref)

    return pl.pallas_call(
        body,
        out_shape=jax.ShapeDtypeStruct((4, vc, deep), jnp.bfloat16),
        in_specs=[smem_spec(), pl.BlockSpec(memory_space=pl.ANY)],
        out_specs=pl.BlockSpec(memory_space=pl.ANY),
        compiler_params=pltpu.CompilerParams(vmem_limit_bytes=60 * MIB),
        name="filter_weights",
    )(place, taps)


def decode(place, clip, w_first, filters, vectors):
    frames, _, lc, lw = clip.shape
    vc = w_first.shape[0]
    deep = 3 * vc
    lot = 4

    def body(place_ref, clip_ref, w1_ref, f_ref, vec_ref, out_ref, lat, act, firsts, w2, both, sems):
        step = pl.program_id(0)
        here = place_ref[0] == 1
        loads = [pltpu.make_async_copy(f_ref.at[n], w2.at[n], sems.at[n]) for n in range(4)]

        def moved(x):
            lane = lax.broadcasted_iota(jnp.int32, x.shape, x.ndim - 1)
            left = jnp.where(lane == 0, 0.0, pltpu.roll(x, 1, x.ndim - 1))
            right = jnp.where(lane == lw - 1, 0.0, pltpu.roll(x, lw - 1, x.ndim - 1))
            return left, x, right

        def first(f):
            sides = []
            for row in range(4):
                taps = [lat[f + dt, row : row + 3].reshape(9 * lc, lw) for dt in range(3)]
                taps.append(jnp.zeros((w1_ref.shape[1] - 27 * lc, lw), jnp.bfloat16))
                sides.append(jnp.concatenate(taps, axis=0))
            y = jnp.dot(
                w1_ref[...], jnp.concatenate(sides, axis=1), preferred_element_type=jnp.float32
            )
            acts = []
            for row in range(4):
                hidden = y[:, row * lw : row * lw + lw] + vec_ref[0]
                hidden = hidden.astype(jnp.bfloat16).astype(jnp.float32)
                if row in (1, 2):
                    firsts[lax.rem(f, 2 * lot), row - 1] = hidden
                factor = lax.rsqrt(jnp.mean(hidden * hidden, axis=0, keepdims=True) + EPS)
                if row == 0:
                    factor = jnp.where(place_ref[2] == 0, 0.0, factor)
                if row == 3:
                    factor = jnp.where(place_ref[2] == place_ref[3], 0.0, factor)
                half = hidden * (0.5 * factor) * vec_ref[1]
                acts.append(half * (1.0 + jnp.tanh(half)))
            a0, a1, a2, a3 = acts
            for n, u in enumerate((a0 - a2, a1 + a2, a2 - a1, a1 - a3)):
                for dx, piece in enumerate(moved(u)):
                    act[n, f + 2, dx * vc : dx * vc + vc] = piece.astype(jnp.bfloat16)

        @pl.when(here & (step == 0))
        def _():
            for load in loads:
                load.start()
            lat[:2] = jnp.zeros((2, 6, 3 * lc, lw), jnp.bfloat16)
            act[:, :2] = jnp.zeros((4, 2, deep, lw), jnp.bfloat16)
            cells = clip_ref[...].astype(jnp.float32)
            for dx, piece in enumerate(moved(cells)):
                lat[2:, :, dx * lc : dx * lc + lc] = piece.astype(jnp.bfloat16)

            @pl.loop(0, lot)
            def _(f):
                first(f)

            for load in loads:
                load.wait()

        def second(and_next):
            base = lot * step
            for n in range(4):
                taps = jnp.concatenate(
                    [act[n, pl.ds(base + j, 3)].reshape(3 * deep, lw) for j in range(lot)], axis=1
                )
                m = jnp.dot(w2[n], taps, preferred_element_type=jnp.float32)
                if n == 0:
                    both[0] = m
                if n == 1:
                    both[0] += m
                    both[1] = m
                if n == 2:
                    both[0] += m
                    both[1] -= m
                if n == 3:
                    both[1] -= m
                if and_next:
                    first(base + lot + n)
            for j in range(lot):
                for r in range(2):
                    whole = both[r, :, j * lw : j * lw + lw]
                    whole += vec_ref[2] + firsts[lax.rem(base + j, 2 * lot), r]
                    out_ref[j, r] = jnp.transpose(whole).astype(jnp.bfloat16)

        @pl.when(here & (step < frames // lot - 1))
        def _():
            second(True)

        @pl.when(here & (step == frames // lot - 1))
        def _():
            second(False)

        @pl.when(jnp.logical_not(here))
        def _():
            out_ref[...] = jnp.zeros(out_ref.shape, out_ref.dtype)

    return pl.pallas_call(
        body,
        grid=(frames // lot,),
        out_shape=jax.ShapeDtypeStruct((frames, 2, lw, vc), jnp.bfloat16),
        in_specs=[
            smem_spec(),
            vmem_spec(),
            vmem_spec(),
            pl.BlockSpec(memory_space=pl.ANY),
            vmem_spec(),
        ],
        out_specs=pl.BlockSpec((lot, 2, lw, vc), lambda i: (i, 0, 0, 0)),
        scratch_shapes=[
            pltpu.VMEM((frames + 2, 6, 3 * lc, lw), jnp.bfloat16),
            pltpu.VMEM((4, frames + 2, deep, lw), jnp.bfloat16),
            pltpu.VMEM((2 * lot, 2, vc, lw), jnp.float32),
            pltpu.VMEM((4, vc, 3 * deep), jnp.bfloat16),
            pltpu.VMEM((2, vc, lot * lw), jnp.float32),
            pltpu.SemaphoreType.DMA((4,)),
        ],
        compiler_params=pltpu.CompilerParams(vmem_limit_bytes=48 * MIB),
        cost_estimate=pl.CostEstimate(flops=0, bytes_accessed=0, transcendentals=0),
        name="decode",
    )(place, clip, w_first, filters, vectors)


def on_device(
    query_input,
    key_input,
    value_input,
    resid,
    gate,
    query_norm_gain,
    key_norm_gain,
    output_weight,
    latents,
    w_in,
    b_in,
    norm_gain,
    w_mid,
    b_mid,
):
    last = lax.axis_size("grp") - 1
    decoder_here = lax.axis_index("grp") == last
    count = lax.axis_size(SEQ)
    side = lax.axis_size("z")
    core, at_z, at_x = lax.axis_index("core"), lax.axis_index("z"), lax.axis_index("x")
    place = jnp.stack(
        [
            decoder_here.astype(jnp.int32),
            core,
            lax.axis_index(SEQ),
            jnp.int32(count - 1),
            jnp.where(core == 0, at_z, at_x),
            jnp.where(core == 0, at_x, at_z),
        ]
    )
    channels = w_in.shape[2]

    def swap(x, ring, step):
        def partner(place):
            return (place ^ 1, side - 1 - place, place ^ 2)[step]

        pairs = []
        for at in range(last * count):
            g, z, x_, c = at // count, at // (2 * side) % side, at // 2 % side, at % 2
            if ring == 2:
                c = 1 - c
            elif (ring == 0) == (c == 0):
                z = partner(z)
            else:
                x_ = partner(x_)
            pairs.append((at, ((g * side + z) * side + x_) * 2 + c))
        return lax.ppermute(x, ("grp",) + SEQ, pairs)

    w_there = swap(output_weight, 2, 0)
    packed = norm_pack(
        query_input[0], key_input[0], value_input[0], query_norm_gain[None], key_norm_gain[None]
    )
    packed, latents, w_mid = lax.optimization_barrier((packed, latents, w_mid))
    here = lax.all_to_all(packed, CHIPS, split_axis=0, concat_axis=0, tiled=True)

    own = jnp.swapaxes(latents, 2, 3)
    pieces = [lax.ppermute(own, "grp", [(g, last)]) for g in range(last)]
    filters = filter_weights(place, w_mid)
    pieces, filters, w_there = lax.optimization_barrier((pieces, filters, w_there))
    w_own, w_give = weight_halves(place, output_weight, w_there)
    w_next, w_back = swap(w_own, 0, 0), swap(w_give, 0, 1)
    clip = jnp.concatenate(pieces + [own], axis=0)
    links = [(last * count + i, last * count + i + 1) for i in range(count - 1)]
    cells = jnp.concatenate(
        [
            lax.ppermute(clip, ("grp",) + SEQ, links),
            clip,
            lax.ppermute(clip, ("grp",) + SEQ, [(b, a) for a, b in links]),
        ],
        axis=1,
    )
    w_first = jnp.pad(w_in.reshape(-1, channels).T, ((0, 0), (0, 512 - 27 * latents.shape[3])))
    vectors = jnp.broadcast_to(
        jnp.stack([b_in, norm_gain, b_mid])[:, :, None], (3, channels, latents.shape[2])
    )
    here, cells, w_back = lax.optimization_barrier((here, cells, w_back))
    there = swap(here, 2, 0)
    w_far = swap(w_back, 0, 0)
    near, other = attend(place, here, there)
    from_far = swap(other, 0, 2)
    heads = near, swap(other, 0, 0), swap(near, 0, 1), from_far
    mine, one, zero, far = project(place, heads, (w_own, w_next, w_back, w_far))
    mine, one, zero, far, cells = lax.optimization_barrier((mine, one, zero, far, cells))
    sums = swap(far, 1, 2), swap(one, 1, 1), swap(zero, 1, 0)
    decoded = decode(place, cells, w_first, filters, vectors)
    mine, decoded = lax.optimization_barrier((mine, decoded))
    kept, give = add_up(place, mine, sums)
    attn_out = finish(place, resid[0], gate, kept, swap(give, 0, 1))
    return attn_out[None], decoded[None]


def solution(mesh):
    fine = Mesh(mesh.devices.reshape(4, 4, 4, 2), ("grp",) + SEQ)
    placed = (
        P("grp", SEQ, None),
        P("grp", SEQ, None),
        P("grp", SEQ, None),
        P("grp", SEQ, None),
        P("grp", None),
        P(),
        P(),
        P(SEQ, None),
        P("grp", SEQ, None, None),
        P(),
        P(),
        P(),
        P(),
        P(),
    )
    return jax.shard_map(
        on_device,
        mesh=fine,
        in_specs=placed,
        out_specs=(P("grp", SEQ, None), P("grp", None, SEQ, None, None)),
        check_vma=False,
    )
```

```python
import math
import jax
import jax.numpy as jnp
from jax import lax
from jax.experimental import pallas as pl
from jax.experimental.pallas import tpu as pltpu
from jax.sharding import Mesh, PartitionSpec as P

CHIPS = ("z", "x")
SEQ = ("z", "x", "core")
EPS = 1e-06
MIB = 1024 * 1024


def vmem_spec():
    return pl.BlockSpec(memory_space=pltpu.VMEM)


def smem_spec():
    return pl.BlockSpec(memory_space=pltpu.SMEM)


def norm_pack(q, k, v, gain_q, gain_k):
    rows, width = q.shape
    chips = width // 256
    block = 16

    def body(q_ref, k_ref, v_ref, gq_ref, gk_ref, out_ref):
        def normed(ref, gain):
            x = ref[...].astype(jnp.float32)
            factor = lax.rsqrt(jnp.mean(x * x, axis=-1, keepdims=True) + EPS)
            return (x * factor * gain).astype(jnp.bfloat16)

        scale = 128**-0.5 * math.log2(math.e)
        qn = normed(q_ref, gq_ref[...] * scale)
        kn = normed(k_ref, gk_ref[...])
        for c in range(chips):
            cols = slice(256 * c, 256 * c + 256)
            out_ref[c, 0] = qn[:, cols]
            out_ref[c, 1] = kn[:, cols]
            out_ref[c, 2] = v_ref[:, cols]

    tokens = pl.BlockSpec((block, width), lambda i: (i, 0))
    gains = pl.BlockSpec((1, width), lambda i: (0, 0))
    return pl.pallas_call(
        body,
        grid=(rows // block,),
        out_shape=jax.ShapeDtypeStruct((chips, 3, rows, 256), jnp.bfloat16),
        in_specs=[tokens, tokens, tokens, gains, gains],
        out_specs=pl.BlockSpec((chips, 3, block, 256), lambda i: (0, 0, i, 0)),
        compiler_params=pltpu.CompilerParams(vmem_limit_bytes=60 * MIB),
        name="norm_pack",
    )(q, k, v, gain_q, gain_k)


def weight_halves(place, w_here, w_there):
    rows, width = w_here.shape
    part = width // 2

    def body(place_ref, here_ref, there_ref, keep_ref, give_ref):
        here_at = pl.ds(pl.multiple_of(place_ref[1] * rows, rows), rows)
        there_at = pl.ds(pl.multiple_of((1 - place_ref[1]) * rows, rows), rows)

        @pl.when(place_ref[0] == 0)
        def _():
            for k, out in enumerate((keep_ref, give_ref)):
                half = jnp.bitwise_xor(place_ref[4] // 2, k)
                at = pl.ds(pl.multiple_of(half * part, part), part)
                out[here_at] = here_ref[:, at]
                out[there_at] = there_ref[:, at]

    return pl.pallas_call(
        body,
        out_shape=(jax.ShapeDtypeStruct((2 * rows, part), jnp.bfloat16),) * 2,
        in_specs=[smem_spec(), vmem_spec(), vmem_spec()],
        out_specs=(vmem_spec(),) * 2,
        compiler_params=pltpu.CompilerParams(vmem_limit_bytes=16 * MIB),
        name="weight_halves",
    )(place, w_here, w_there)


def inner(position):
    return ((position + 1) // 2) % 2


def attend(place, here, there):
    chips, _, tok, _ = here.shape
    half = chips * tok

    def body(place_ref, here_ref, there_ref, near_ref, other_ref):
        step = pl.program_id(0)

        @pl.when(place_ref[0] == 0)
        def _():
            queries = here_ref[pl.ds(4 * step, 4), 0].reshape(4 * tok, 256)
            ones = jnp.ones((half, 128), jnp.bfloat16)
            heads = []
            for h in range(2):
                cols = slice(128 * h, 128 * h + 128)
                scores = [
                    lax.dot_general(
                        queries[:, cols],
                        ref[:, 1, :, cols].reshape(half, 128),
                        (((1,), (1,)), ((), ())),
                        preferred_element_type=jnp.float32,
                    )
                    for ref in (here_ref, there_ref)
                ]
                peak = jnp.maximum(*(jnp.max(s, axis=-1, keepdims=True) for s in scores))
                o = None
                for s, ref in zip(scores, (here_ref, there_ref)):
                    values = jnp.concatenate([ref[:, 2, :, cols].reshape(half, 128), ones], axis=1)
                    p = jnp.exp2(s - peak).astype(jnp.bfloat16)
                    part = jnp.dot(p, values, preferred_element_type=jnp.float32)
                    o = part if o is None else o + part
                heads.append(o[:, :128] / o[:, 128:])
            joined = jnp.concatenate(heads, axis=1).astype(jnp.bfloat16)
            for n in range(4):
                first = jnp.where(place_ref[1] == 0, step, n)
                second = jnp.where(place_ref[1] == 0, n, step)
                high = first // 2
                slot = jnp.where(second == 0, 0, jnp.where(second == 3, 1, second + 1))
                near = inner(first) == inner(place_ref[4])
                piece = joined[tok * n : tok * n + tok]

                @pl.when(near)
                def _():
                    near_ref[slot, high] = piece

                @pl.when(jnp.logical_not(near))
                def _():
                    other_ref[slot, high] = piece

    return pl.pallas_call(
        body,
        grid=(chips // 4,),
        out_shape=(jax.ShapeDtypeStruct((4, 2, tok, 256), jnp.bfloat16),) * 2,
        in_specs=[smem_spec(), vmem_spec(), vmem_spec()],
        out_specs=(vmem_spec(),) * 2,
        compiler_params=pltpu.CompilerParams(vmem_limit_bytes=40 * MIB),
        cost_estimate=pl.CostEstimate(flops=0, bytes_accessed=0, transcendentals=0),
        name="attend",
    )(place, here, there)


def project(place, heads, weights):
    _, two, tok, _ = heads[0].shape
    part = weights[0].shape[1]
    lot = two * tok

    def body(place_ref, h0, h1, h2, h3, w0, w1, w2, w3, own_ref, one_ref, zero_ref, far_ref):
        second = place_ref[5]
        slot = jnp.where(second == 0, 0, jnp.where(second == 3, 1, second + 1))

        @pl.when(place_ref[0] == 0)
        def _():
            weight = jnp.concatenate([w0[...], w1[...], w2[...], w3[...]], axis=0)
            feats = jnp.concatenate(
                [
                    jnp.concatenate(
                        [h[jnp.bitwise_xor(slot, k)].reshape(lot, 256) for h in (h0, h1, h2, h3)],
                        axis=1,
                    )
                    for k in range(4)
                ],
                axis=0,
            )
            out = jnp.dot(feats, weight, preferred_element_type=jnp.float32)
            for k, ref in enumerate((own_ref, one_ref, zero_ref, far_ref)):
                ref[...] = out[lot * k : lot * k + lot].reshape(two, tok, part).astype(ref.dtype)

    shape = (two, tok, part)
    return pl.pallas_call(
        body,
        out_shape=(jax.ShapeDtypeStruct(shape, jnp.float32),)
        + (jax.ShapeDtypeStruct(shape, jnp.bfloat16),) * 3,
        in_specs=[smem_spec()] + [vmem_spec()] * 8,
        out_specs=(vmem_spec(),) * 4,
        compiler_params=pltpu.CompilerParams(vmem_limit_bytes=40 * MIB),
        cost_estimate=pl.CostEstimate(
            flops=8 * lot * 1024 * part, bytes_accessed=8 * MIB, transcendentals=0
        ),
        name="project",
    )(place, *heads, *weights)


def add_up(place, own, others):
    def body(place_ref, own_ref, a_ref, b_ref, c_ref, keep_ref, give_ref):
        mine = place_ref[4] // 2

        @pl.when(place_ref[0] == 0)
        def _():
            for at, out in ((mine, keep_ref), (1 - mine, give_ref)):
                total = own_ref[at]
                for ref in (a_ref, b_ref, c_ref):
                    total += ref[at].astype(jnp.float32)
                out[...] = total.astype(out.dtype)

    return pl.pallas_call(
        body,
        out_shape=(
            jax.ShapeDtypeStruct(own.shape[1:], jnp.float32),
            jax.ShapeDtypeStruct(own.shape[1:], jnp.bfloat16),
        ),
        in_specs=[smem_spec()] + [vmem_spec()] * 4,
        out_specs=(vmem_spec(),) * 2,
        compiler_params=pltpu.CompilerParams(vmem_limit_bytes=24 * MIB),
        name="add_up",
    )(place, own, *others)


def finish(place, resid, gate, kept, got):
    part = kept.shape[1]

    def body(place_ref, resid_ref, gate_ref, kept_ref, got_ref, out_ref):
        @pl.when(place_ref[0] == 0)
        def _():
            for k, ref in enumerate((kept_ref, got_ref)):
                half = jnp.bitwise_xor(place_ref[4] // 2, k)
                at = pl.ds(pl.multiple_of(half * part, part), part)
                total = resid_ref[:, at].astype(jnp.float32)
                total += gate_ref[:, at] * ref[...].astype(jnp.float32)
                out_ref[:, at] = total.astype(jnp.bfloat16)

        @pl.when(place_ref[0] == 1)
        def _():
            out_ref[...] = jnp.zeros(out_ref.shape, out_ref.dtype)

    return pl.pallas_call(
        body,
        out_shape=jax.ShapeDtypeStruct(resid.shape, jnp.bfloat16),
        in_specs=[smem_spec()] + [vmem_spec()] * 4,
        out_specs=vmem_spec(),
        compiler_params=pltpu.CompilerParams(vmem_limit_bytes=16 * MIB),
        name="finish",
    )(place, resid, gate, kept, got)


def filter_weights(place, w_mid):
    steps, deep, vc = w_mid.shape
    taps = w_mid.reshape(steps, 3, 3, vc, vc)

    def block(w_ref, out_ref):
        up, mid, down = (w_ref[0, n, 0] for n in range(3))
        ends = 0.5 * (up.astype(jnp.float32) + down.astype(jnp.float32))
        half = 0.5 * mid.astype(jnp.float32)
        for n, g in enumerate((up, ends + half, ends - half, down)):
            out_ref[n] = jnp.transpose(g.astype(jnp.bfloat16))

    def body(place_ref, w_ref, out_ref):
        @pl.when(place_ref[0] == 1)
        def _():
            pltpu.emit_pipeline(
                block,
                grid=(3 * steps,),
                in_specs=[pl.BlockSpec((1, 3, 1, vc, vc), lambda i: (i // 3, 0, i % 3, 0, 0))],
                out_specs=[pl.BlockSpec((4, vc, vc), lambda i: (0, 0, i))],
            )(w_ref, out_ref)

    return pl.pallas_call(
        body,
        out_shape=jax.ShapeDtypeStruct((4, vc, deep), jnp.bfloat16),
        in_specs=[smem_spec(), pl.BlockSpec(memory_space=pl.ANY)],
        out_specs=pl.BlockSpec(memory_space=pl.ANY),
        compiler_params=pltpu.CompilerParams(vmem_limit_bytes=56 * MIB),
        name="filter_weights",
    )(place, taps)


def decode(place, clip, w_first, filters, vectors):
    frames, _, lc, lw = clip.shape
    vc = w_first.shape[0]
    deep = 3 * vc
    lot = 4

    def body(place_ref, clip_ref, w1_ref, f_ref, vec_ref, out_ref, lat, act, firsts, w2, both, sems):
        step = pl.program_id(0)
        here = place_ref[0] == 1
        loads = [pltpu.make_async_copy(f_ref.at[n], w2.at[n], sems.at[n]) for n in range(4)]

        def moved(x):
            lane = lax.broadcasted_iota(jnp.int32, x.shape, x.ndim - 1)
            left = jnp.where(lane == 0, 0.0, pltpu.roll(x, 1, x.ndim - 1))
            right = jnp.where(lane == lw - 1, 0.0, pltpu.roll(x, lw - 1, x.ndim - 1))
            return left, x, right

        def first(f):
            sides = []
            for row in range(4):
                taps = [lat[f + dt, row : row + 3].reshape(9 * lc, lw) for dt in range(3)]
                taps.append(jnp.zeros((w1_ref.shape[1] - 27 * lc, lw), jnp.bfloat16))
                sides.append(jnp.concatenate(taps, axis=0))
            y = jnp.dot(
                w1_ref[...], jnp.concatenate(sides, axis=1), preferred_element_type=jnp.float32
            )
            acts = []
            for row in range(4):
                hidden = y[:, row * lw : row * lw + lw] + vec_ref[0]
                hidden = hidden.astype(jnp.bfloat16).astype(jnp.float32)
                if row in (1, 2):
                    firsts[lax.rem(f, 2 * lot), row - 1] = hidden
                factor = lax.rsqrt(jnp.mean(hidden * hidden, axis=0, keepdims=True) + EPS)
                if row == 0:
                    factor = jnp.where(place_ref[2] == 0, 0.0, factor)
                if row == 3:
                    factor = jnp.where(place_ref[2] == place_ref[3], 0.0, factor)
                half = hidden * (0.5 * factor) * vec_ref[1]
                acts.append(half * (1.0 + jnp.tanh(half)))
            a0, a1, a2, a3 = acts
            for n, u in enumerate((a0 - a2, a1 + a2, a2 - a1, a1 - a3)):
                for dx, piece in enumerate(moved(u)):
                    act[n, f + 2, dx * vc : dx * vc + vc] = piece.astype(jnp.bfloat16)

        @pl.when(here & (step == 0))
        def _():
            for load in loads:
                load.start()
            lat[:2] = jnp.zeros((2, 6, 3 * lc, lw), jnp.bfloat16)
            act[:, :2] = jnp.zeros((4, 2, deep, lw), jnp.bfloat16)
            cells = clip_ref[...].astype(jnp.float32)
            for dx, piece in enumerate(moved(cells)):
                lat[2:, :, dx * lc : dx * lc + lc] = piece.astype(jnp.bfloat16)

            @pl.loop(0, lot)
            def _(f):
                first(f)

            for load in loads:
                load.wait()

        def second(and_next):
            base = lot * step
            for n in range(4):
                taps = jnp.concatenate(
                    [act[n, pl.ds(base + j, 3)].reshape(3 * deep, lw) for j in range(lot)], axis=1
                )
                m = jnp.dot(w2[n], taps, preferred_element_type=jnp.float32)
                if n == 0:
                    both[0] = m
                if n == 1:
                    both[0] += m
                    both[1] = m
                if n == 2:
                    both[0] += m
                    both[1] -= m
                if n == 3:
                    both[1] -= m
                if and_next:
                    first(base + lot + n)
            for j in range(lot):
                for r in range(2):
                    whole = both[r, :, j * lw : j * lw + lw]
                    whole += vec_ref[2] + firsts[lax.rem(base + j, 2 * lot), r]
                    out_ref[j, r] = jnp.transpose(whole).astype(jnp.bfloat16)

        @pl.when(here & (step < frames // lot - 1))
        def _():
            second(True)

        @pl.when(here & (step == frames // lot - 1))
        def _():
            second(False)

        @pl.when(jnp.logical_not(here))
        def _():
            out_ref[...] = jnp.zeros(out_ref.shape, out_ref.dtype)

    return pl.pallas_call(
        body,
        grid=(frames // lot,),
        out_shape=jax.ShapeDtypeStruct((frames, 2, lw, vc), jnp.bfloat16),
        in_specs=[
            smem_spec(),
            vmem_spec(),
            vmem_spec(),
            pl.BlockSpec(memory_space=pl.ANY),
            vmem_spec(),
        ],
        out_specs=pl.BlockSpec((lot, 2, lw, vc), lambda i: (i, 0, 0, 0)),
        scratch_shapes=[
            pltpu.VMEM((frames + 2, 6, 3 * lc, lw), jnp.bfloat16),
            pltpu.VMEM((4, frames + 2, deep, lw), jnp.bfloat16),
            pltpu.VMEM((2 * lot, 2, vc, lw), jnp.float32),
            pltpu.VMEM((4, vc, 3 * deep), jnp.bfloat16),
            pltpu.VMEM((2, vc, lot * lw), jnp.float32),
            pltpu.SemaphoreType.DMA((4,)),
        ],
        compiler_params=pltpu.CompilerParams(vmem_limit_bytes=48 * MIB),
        cost_estimate=pl.CostEstimate(flops=0, bytes_accessed=0, transcendentals=0),
        name="decode",
    )(place, clip, w_first, filters, vectors)


def on_device(
    query_input,
    key_input,
    value_input,
    resid,
    gate,
    query_norm_gain,
    key_norm_gain,
    output_weight,
    latents,
    w_in,
    b_in,
    norm_gain,
    w_mid,
    b_mid,
):
    last = lax.axis_size("grp") - 1
    decoder_here = lax.axis_index("grp") == last
    count = lax.axis_size(SEQ)
    side = lax.axis_size("z")
    core, at_z, at_x = lax.axis_index("core"), lax.axis_index("z"), lax.axis_index("x")
    place = jnp.stack(
        [
            decoder_here.astype(jnp.int32),
            core,
            lax.axis_index(SEQ),
            jnp.int32(count - 1),
            jnp.where(core == 0, at_z, at_x),
            jnp.where(core == 0, at_x, at_z),
        ]
    )
    channels = w_in.shape[2]

    def swap(x, ring, step):
        def partner(place):
            return (place ^ 1, side - 1 - place, place ^ 2)[step]

        pairs = []
        for at in range(last * count):
            g, z, x_, c = at // count, at // (2 * side) % side, at // 2 % side, at % 2
            if ring == 2:
                c = 1 - c
            elif (ring == 0) == (c == 0):
                z = partner(z)
            else:
                x_ = partner(x_)
            pairs.append((at, ((g * side + z) * side + x_) * 2 + c))
        return lax.ppermute(x, ("grp",) + SEQ, pairs)

    packed = norm_pack(
        query_input[0], key_input[0], value_input[0], query_norm_gain[None], key_norm_gain[None]
    )
    packed, w_here = lax.optimization_barrier((packed, output_weight))
    here = lax.all_to_all(packed, CHIPS, split_axis=0, concat_axis=0, tiled=True)

    w_own, w_give = weight_halves(place, w_here, swap(w_here, 2, 0))
    w_own, w_give, latents, w_mid = lax.optimization_barrier((w_own, w_give, latents, w_mid))
    w_next, w_back = swap(w_own, 0, 0), swap(w_give, 0, 1)

    own = jnp.swapaxes(latents, 2, 3)
    clip = jnp.concatenate(
        [lax.ppermute(own, "grp", [(g, last)]) for g in range(last)] + [own], axis=0
    )
    links = [(last * count + i, last * count + i + 1) for i in range(count - 1)]
    above = lax.ppermute(clip, ("grp",) + SEQ, links)
    below = lax.ppermute(clip, ("grp",) + SEQ, [(b, a) for a, b in links])
    filters = filter_weights(place, w_mid)
    above, below, filters = lax.optimization_barrier((above, below, filters))
    cells = jnp.concatenate([above, clip, below], axis=1)
    w_first = jnp.pad(w_in.reshape(-1, channels).T, ((0, 0), (0, 512 - 27 * latents.shape[3])))
    vectors = jnp.broadcast_to(
        jnp.stack([b_in, norm_gain, b_mid])[:, :, None], (3, channels, latents.shape[2])
    )

    here, cells, w_next, w_back = lax.optimization_barrier((here, cells, w_next, w_back))
    there = swap(here, 2, 0)
    w_far = swap(w_back, 0, 0)
    near, other = attend(place, here, there)
    from_far = swap(other, 0, 2)
    heads = near, swap(other, 0, 0), swap(near, 0, 1), from_far
    mine, one, zero, far = project(place, heads, (w_own, w_next, w_back, w_far))
    mine, one, zero, far, cells = lax.optimization_barrier((mine, one, zero, far, cells))
    sums = swap(far, 1, 2), swap(one, 1, 1), swap(zero, 1, 0)
    decoded = decode(place, cells, w_first, filters, vectors)
    mine, decoded = lax.optimization_barrier((mine, decoded))
    kept, give = add_up(place, mine, sums)
    attn_out = finish(place, resid[0], gate, kept, swap(give, 0, 1))
    return attn_out[None], decoded[None]


def solution(mesh):
    fine = Mesh(mesh.devices.reshape(4, 4, 4, 2), ("grp",) + SEQ)
    placed = (
        P("grp", SEQ, None),
        P("grp", SEQ, None),
        P("grp", SEQ, None),
        P("grp", SEQ, None),
        P("grp", None),
        P(),
        P(),
        P(SEQ, None),
        P("grp", SEQ, None, None),
        P(),
        P(),
        P(),
        P(),
        P(),
    )
    return jax.shard_map(
        on_device,
        mesh=fine,
        in_specs=placed,
        out_specs=(P("grp", SEQ, None), P("grp", None, SEQ, None, None)),
        check_vma=False,
    )
```

```python
import math
import jax
import jax.numpy as jnp
from jax import lax
from jax.experimental import pallas as pl
from jax.experimental.pallas import tpu as pltpu
from jax.sharding import Mesh, PartitionSpec as P

CHIPS = ("z", "x")
SEQ = ("z", "x", "core")
EPS = 1e-06
MIB = 1024 * 1024


def vmem_spec():
    return pl.BlockSpec(memory_space=pltpu.VMEM)


def smem_spec():
    return pl.BlockSpec(memory_space=pltpu.SMEM)


def norm_pack(q, k, v, gain_q, gain_k):
    rows, width = q.shape
    chips = width // 256
    block = 16

    def body(q_ref, k_ref, v_ref, gq_ref, gk_ref, out_ref):
        def normed(ref, gain):
            x = ref[...].astype(jnp.float32)
            factor = lax.rsqrt(jnp.mean(x * x, axis=-1, keepdims=True) + EPS)
            return (x * factor * gain).astype(jnp.bfloat16)

        scale = 128**-0.5 * math.log2(math.e)
        qn = normed(q_ref, gq_ref[...] * scale)
        kn = normed(k_ref, gk_ref[...])
        for c in range(chips):
            cols = slice(256 * c, 256 * c + 256)
            out_ref[c, 0] = qn[:, cols]
            out_ref[c, 1] = kn[:, cols]
            out_ref[c, 2] = v_ref[:, cols]

    tokens = pl.BlockSpec((block, width), lambda i: (i, 0))
    gains = pl.BlockSpec((1, width), lambda i: (0, 0))
    return pl.pallas_call(
        body,
        grid=(rows // block,),
        out_shape=jax.ShapeDtypeStruct((chips, 3, rows, 256), jnp.bfloat16),
        in_specs=[tokens, tokens, tokens, gains, gains],
        out_specs=pl.BlockSpec((chips, 3, block, 256), lambda i: (0, 0, i, 0)),
        compiler_params=pltpu.CompilerParams(vmem_limit_bytes=60 * MIB),
        name="norm_pack",
    )(q, k, v, gain_q, gain_k)


def partners(position):
    return position, jnp.bitwise_xor(position, 1), 3 - position, jnp.bitwise_xor(position, 2)


def weight_blocks(place, w_here, w_there):
    rows, width = w_here.shape
    part = width // 4

    def body(place_ref, here_ref, there_ref, *outs):
        here_at = pl.ds(pl.multiple_of(place_ref[1] * rows, rows), rows)
        there_at = pl.ds(pl.multiple_of((1 - place_ref[1]) * rows, rows), rows)

        @pl.when(place_ref[0] == 0)
        def _():
            for chip, out in zip(partners(place_ref[4]), outs):
                at = pl.ds(pl.multiple_of(chip * part, part), part)
                out[here_at] = here_ref[:, at]
                out[there_at] = there_ref[:, at]

    return pl.pallas_call(
        body,
        out_shape=(jax.ShapeDtypeStruct((2 * rows, part), jnp.bfloat16),) * 4,
        in_specs=[smem_spec(), vmem_spec(), vmem_spec()],
        out_specs=(vmem_spec(),) * 4,
        compiler_params=pltpu.CompilerParams(vmem_limit_bytes=16 * MIB),
        name="weight_blocks",
    )(place, w_here, w_there)


def attend(place, here, there):
    chips, _, tok, _ = here.shape
    half = chips * tok

    def body(place_ref, here_ref, there_ref, out_ref):
        step = pl.program_id(0)

        @pl.when(place_ref[0] == 0)
        def _():
            queries = here_ref[pl.ds(4 * step, 4), 0].reshape(4 * tok, 256)
            ones = jnp.ones((half, 128), jnp.bfloat16)
            heads = []
            for h in range(2):
                cols = slice(128 * h, 128 * h + 128)
                scores = [
                    lax.dot_general(
                        queries[:, cols],
                        ref[:, 1, :, cols].reshape(half, 128),
                        (((1,), (1,)), ((), ())),
                        preferred_element_type=jnp.float32,
                    )
                    for ref in (here_ref, there_ref)
                ]
                peak = jnp.maximum(*(jnp.max(s, axis=-1, keepdims=True) for s in scores))
                o = None
                for s, ref in zip(scores, (here_ref, there_ref)):
                    values = jnp.concatenate([ref[:, 2, :, cols].reshape(half, 128), ones], axis=1)
                    p = jnp.exp2(s - peak).astype(jnp.bfloat16)
                    part = jnp.dot(p, values, preferred_element_type=jnp.float32)
                    o = part if o is None else o + part
                heads.append(o[:, :128] / o[:, 128:])
            joined = jnp.concatenate(heads, axis=1).astype(jnp.bfloat16)
            for n in range(4):
                at = jnp.where(place_ref[1] == 0, 4 * n + step, 4 * step + n)
                out_ref[at] = joined[tok * n : tok * n + tok]

    return pl.pallas_call(
        body,
        grid=(chips // 4,),
        out_shape=jax.ShapeDtypeStruct((chips, tok, 256), jnp.bfloat16),
        in_specs=[smem_spec(), vmem_spec(), vmem_spec()],
        out_specs=vmem_spec(),
        compiler_params=pltpu.CompilerParams(vmem_limit_bytes=40 * MIB),
        cost_estimate=pl.CostEstimate(flops=0, bytes_accessed=0, transcendentals=0),
        name="attend",
    )(place, here, there)


def project(place, heads, weights):
    chips, tok, _ = heads[0].shape
    part = weights[0].shape[1]
    lot = chips // 4 * tok

    def body(place_ref, h0, h1, h2, h3, w0, w1, w2, w3, *outs):
        @pl.when(place_ref[0] == 0)
        def _():
            weight = jnp.concatenate([w0[...], w1[...], w2[...], w3[...]], axis=0)
            feats = jnp.concatenate(
                [
                    jnp.concatenate(
                        [h[pl.ds(4 * chip, 4)].reshape(lot, 256) for h in (h0, h1, h2, h3)], axis=1
                    )
                    for chip in partners(place_ref[5])
                ],
                axis=0,
            )
            out = jnp.dot(feats, weight, preferred_element_type=jnp.float32)
            for k, ref in enumerate(outs):
                ref[...] = out[lot * k : lot * k + lot].reshape(4, tok, part).astype(ref.dtype)

    shape = (4, tok, part)
    return pl.pallas_call(
        body,
        out_shape=(jax.ShapeDtypeStruct(shape, jnp.float32),)
        + (jax.ShapeDtypeStruct(shape, jnp.bfloat16),) * 3,
        in_specs=[smem_spec()] + [vmem_spec()] * 8,
        out_specs=(vmem_spec(),) * 4,
        compiler_params=pltpu.CompilerParams(vmem_limit_bytes=40 * MIB),
        cost_estimate=pl.CostEstimate(
            flops=8 * lot * 1024 * part, bytes_accessed=8 * MIB, transcendentals=0
        ),
        name="project",
    )(place, *heads, *weights)


def add_up(place, own, others):
    def body(place_ref, own_ref, a_ref, b_ref, c_ref, *outs):
        @pl.when(place_ref[0] == 0)
        def _():
            for chip, out in zip(partners(place_ref[4]), outs):
                total = own_ref[chip]
                for ref in (a_ref, b_ref, c_ref):
                    total += ref[chip].astype(jnp.float32)
                out[...] = total.astype(out.dtype)

    return pl.pallas_call(
        body,
        out_shape=(jax.ShapeDtypeStruct(own.shape[1:], jnp.float32),)
        + (jax.ShapeDtypeStruct(own.shape[1:], jnp.bfloat16),) * 3,
        in_specs=[smem_spec()] + [vmem_spec()] * 4,
        out_specs=(vmem_spec(),) * 4,
        compiler_params=pltpu.CompilerParams(vmem_limit_bytes=24 * MIB),
        name="add_up",
    )(place, own, *others)


def finish(place, resid, gate, blocks):
    part = blocks[0].shape[1]

    def body(place_ref, resid_ref, gate_ref, b0, b1, b2, b3, out_ref):
        @pl.when(place_ref[0] == 0)
        def _():
            for chip, ref in zip(partners(place_ref[4]), (b0, b1, b2, b3)):
                at = pl.ds(pl.multiple_of(chip * part, part), part)
                total = resid_ref[:, at].astype(jnp.float32)
                total += gate_ref[:, at] * ref[...].astype(jnp.float32)
                out_ref[:, at] = total.astype(jnp.bfloat16)

        @pl.when(place_ref[0] == 1)
        def _():
            out_ref[...] = jnp.zeros(out_ref.shape, out_ref.dtype)

    return pl.pallas_call(
        body,
        out_shape=jax.ShapeDtypeStruct(resid.shape, jnp.bfloat16),
        in_specs=[smem_spec()] + [vmem_spec()] * 6,
        out_specs=vmem_spec(),
        compiler_params=pltpu.CompilerParams(vmem_limit_bytes=16 * MIB),
        name="finish",
    )(place, resid, gate, *blocks)


def filter_weights(place, w_mid, start, count):
    steps, deep, vc = w_mid.shape
    taps = w_mid.reshape(steps, 3, 3, vc, vc)

    def block(w_ref, out_ref):
        up, mid, down = (jnp.transpose(w_ref[0, n, 0]) for n in range(3))
        ends = 0.5 * (up.astype(jnp.float32) + down.astype(jnp.float32))
        half = 0.5 * mid.astype(jnp.float32)
        for n, g in enumerate((up, ends + half, ends - half, down)):
            out_ref[n] = g.astype(jnp.bfloat16)

    def body(place_ref, w_ref, out_ref):
        @pl.when(place_ref[0] == 1)
        def _():
            pltpu.emit_pipeline(
                block,
                grid=(count,),
                in_specs=[
                    pl.BlockSpec(
                        (1, 3, 1, vc, vc), lambda i: ((i + start) // 3, 0, (i + start) % 3, 0, 0)
                    )
                ],
                out_specs=[pl.BlockSpec((4, vc, vc), lambda i: (0, 0, i))],
            )(w_ref, out_ref)

    return pl.pallas_call(
        body,
        out_shape=jax.ShapeDtypeStruct((4, vc, count * vc), jnp.bfloat16),
        in_specs=[smem_spec(), pl.BlockSpec(memory_space=pl.ANY)],
        out_specs=pl.BlockSpec(memory_space=pl.ANY),
        compiler_params=pltpu.CompilerParams(vmem_limit_bytes=56 * MIB),
        name="filter_weights_%d" % start,
    )(place, taps)


def decode(place, clip, w_in, filters, vectors):
    frames, _, lc, lw = clip.shape
    fan, vc = w_in.shape
    deep = 3 * vc
    lot = 4
    wide = 512
    cut = filters[0].shape[2]

    def body(
        place_ref, clip_ref, win_ref, fa_ref, fb_ref, rows_ref, out_ref,
        lat, act, firsts, w1_ref, vec_ref, w2, both, sems,
    ):
        step = pl.program_id(0)
        here = place_ref[0] == 1
        loads = [
            pltpu.make_async_copy(fa_ref, w2.at[:, :, pl.ds(0, cut)], sems.at[0]),
            pltpu.make_async_copy(fb_ref, w2.at[:, :, pl.ds(cut, 3 * deep - cut)], sems.at[1]),
        ]

        def moved(x):
            lane = lax.broadcasted_iota(jnp.int32, x.shape, x.ndim - 1)
            left = jnp.where(lane == 0, 0.0, pltpu.roll(x, 1, x.ndim - 1))
            right = jnp.where(lane == lw - 1, 0.0, pltpu.roll(x, lw - 1, x.ndim - 1))
            return left, x, right

        def first(f):
            sides = []
            for row in range(4):
                taps = [lat[f + dt, row : row + 3].reshape(9 * lc, lw) for dt in range(3)]
                taps.append(jnp.zeros((wide - fan, lw), jnp.bfloat16))
                sides.append(jnp.concatenate(taps, axis=0))
            y = jnp.dot(
                w1_ref[...], jnp.concatenate(sides, axis=1), preferred_element_type=jnp.float32
            )
            acts = []
            for row in range(4):
                hidden = y[:, row * lw : row * lw + lw] + vec_ref[0]
                if row in (1, 2):
                    firsts[lax.rem(f, 2 * lot), row - 1] = hidden
                factor = lax.rsqrt(jnp.mean(hidden * hidden, axis=0, keepdims=True) + EPS)
                if row == 0:
                    factor = jnp.where(place_ref[2] == 0, 0.0, factor)
                if row == 3:
                    factor = jnp.where(place_ref[2] == place_ref[3], 0.0, factor)
                half = hidden * (0.5 * factor) * vec_ref[1]
                acts.append(half * (1.0 + jnp.tanh(half)))
            a0, a1, a2, a3 = acts
            for n, u in enumerate((a0 - a2, a1 + a2, a2 - a1, a1 - a3)):
                for dx, piece in enumerate(moved(u)):
                    act[n, f + 2, dx * vc : dx * vc + vc] = piece.astype(jnp.bfloat16)

        @pl.when(here & (step == 0))
        def _():
            for load in loads:
                load.start()
            w1_ref[:, :fan] = jnp.transpose(win_ref[...])
            w1_ref[:, fan:] = jnp.zeros((vc, wide - fan), jnp.bfloat16)
            for n in range(3):
                row = jnp.broadcast_to(rows_ref[n : n + 1], (lw, vc))
                vec_ref[n] = jnp.transpose(row)
            lat[:2] = jnp.zeros((2, 6, 3 * lc, lw), jnp.bfloat16)
            act[:, :2] = jnp.zeros((4, 2, deep, lw), jnp.bfloat16)
            cells = clip_ref[...].astype(jnp.float32)
            for dx, piece in enumerate(moved(cells)):
                lat[2:, :, dx * lc : dx * lc + lc] = piece.astype(jnp.bfloat16)

            @pl.loop(0, lot)
            def _(f):
                first(f)

            for load in loads:
                load.wait()

        def second(and_next):
            base = lot * step
            for n in range(4):
                taps = jnp.concatenate(
                    [act[n, pl.ds(base + j, 3)].reshape(3 * deep, lw) for j in range(lot)], axis=1
                )
                m = jnp.dot(w2[n], taps, preferred_element_type=jnp.float32)
                if n == 0:
                    both[0] = m
                if n == 1:
                    both[0] += m
                    both[1] = m
                if n == 2:
                    both[0] += m
                    both[1] -= m
                if n == 3:
                    both[1] -= m
                if and_next:
                    first(base + lot + n)
            for j in range(lot):
                for r in range(2):
                    whole = both[r, :, j * lw : j * lw + lw]
                    whole += vec_ref[2] + firsts[lax.rem(base + j, 2 * lot), r]
                    out_ref[j, r] = jnp.transpose(whole).astype(jnp.bfloat16)

        @pl.when(here & (step < frames // lot - 1))
        def _():
            second(True)

        @pl.when(here & (step == frames // lot - 1))
        def _():
            second(False)

        @pl.when(jnp.logical_not(here))
        def _():
            out_ref[...] = jnp.zeros(out_ref.shape, out_ref.dtype)

    return pl.pallas_call(
        body,
        grid=(frames // lot,),
        out_shape=jax.ShapeDtypeStruct((frames, 2, lw, vc), jnp.bfloat16),
        in_specs=[
            smem_spec(),
            vmem_spec(),
            vmem_spec(),
            pl.BlockSpec(memory_space=pl.ANY),
            pl.BlockSpec(memory_space=pl.ANY),
            vmem_spec(),
        ],
        out_specs=pl.BlockSpec((lot, 2, lw, vc), lambda i: (i, 0, 0, 0)),
        scratch_shapes=[
            pltpu.VMEM((frames + 2, 6, 3 * lc, lw), jnp.bfloat16),
            pltpu.VMEM((4, frames + 2, deep, lw), jnp.bfloat16),
            pltpu.VMEM((2 * lot, 2, vc, lw), jnp.float32),
            pltpu.VMEM((vc, wide), jnp.bfloat16),
            pltpu.VMEM((3, vc, lw), jnp.float32),
            pltpu.VMEM((4, vc, 3 * deep), jnp.bfloat16),
            pltpu.VMEM((2, vc, lot * lw), jnp.float32),
            pltpu.SemaphoreType.DMA((2,)),
        ],
        compiler_params=pltpu.CompilerParams(vmem_limit_bytes=48 * MIB),
        cost_estimate=pl.CostEstimate(flops=0, bytes_accessed=0, transcendentals=0),
        name="decode",
    )(place, clip, w_in, *filters, vectors)


def on_device(
    query_input,
    key_input,
    value_input,
    resid,
    gate,
    query_norm_gain,
    key_norm_gain,
    output_weight,
    latents,
    w_in,
    b_in,
    norm_gain,
    w_mid,
    b_mid,
):
    last = lax.axis_size("grp") - 1
    decoder_here = lax.axis_index("grp") == last
    count = lax.axis_size(SEQ)
    side = lax.axis_size("z")
    core, at_z, at_x = lax.axis_index("core"), lax.axis_index("z"), lax.axis_index("x")
    place = jnp.stack(
        [
            decoder_here.astype(jnp.int32),
            core,
            lax.axis_index(SEQ),
            jnp.int32(count - 1),
            jnp.where(core == 0, at_z, at_x),
            jnp.where(core == 0, at_x, at_z),
        ]
    )
    channels = w_in.shape[2]

    def swap(x, ring, step):
        def partner(place):
            return (place ^ 1, side - 1 - place, place ^ 2)[step]

        pairs = []
        for at in range(last * count):
            g, z, x_, c = at // count, at // (2 * side) % side, at // 2 % side, at % 2
            if ring == 2:
                c = 1 - c
            elif (ring == 0) == (c == 0):
                z = partner(z)
            else:
                x_ = partner(x_)
            pairs.append((at, ((g * side + z) * side + x_) * 2 + c))
        return lax.ppermute(x, ("grp",) + SEQ, pairs)

    packed = norm_pack(
        query_input[0], key_input[0], value_input[0], query_norm_gain[None], key_norm_gain[None]
    )
    packed, w_here, latents, w_mid = lax.optimization_barrier((packed, output_weight, latents, w_mid))
    here = lax.all_to_all(packed, CHIPS, split_axis=0, concat_axis=0, tiled=True)

    w_there = swap(w_here, 2, 0)
    own = jnp.swapaxes(latents, 2, 3)
    pieces = [lax.ppermute(own, "grp", [(g, last)]) for g in range(last)]
    early = filter_weights(place, w_mid, 0, 5)
    pieces, early, w_there = lax.optimization_barrier((pieces, early, w_there))
    weights = weight_blocks(place, w_here, w_there)
    w_zero, w_one = swap(weights[1], 0, 0), swap(weights[2], 0, 1)
    clip = jnp.concatenate(pieces + [own], axis=0)
    links = [(last * count + i, last * count + i + 1) for i in range(count - 1)]
    above = lax.ppermute(clip, ("grp",) + SEQ, links)
    below = lax.ppermute(clip, ("grp",) + SEQ, [(b, a) for a, b in links])
    late = filter_weights(place, w_mid, 5, 4)
    above, below, late = lax.optimization_barrier((above, below, late))
    cells = jnp.concatenate([above, clip, below], axis=1)

    here, cells, w_zero, w_one = lax.optimization_barrier((here, cells, w_zero, w_one))
    there = swap(here, 2, 0)
    w_far = swap(weights[3], 0, 2)
    heads = attend(place, here, there)
    from_far = swap(heads, 0, 2)
    heads = heads, swap(heads, 0, 0), swap(heads, 0, 1), from_far
    mine, zero, one, far = project(place, heads, (weights[0], w_zero, w_one, w_far))
    mine, zero, one, far, cells = lax.optimization_barrier((mine, zero, one, far, cells))
    sums = swap(far, 1, 2), swap(zero, 1, 0), swap(one, 1, 1)
    decoded = decode(
        place, cells, w_in.reshape(-1, channels), (early, late), jnp.stack([b_in, norm_gain, b_mid])
    )
    mine, decoded = lax.optimization_barrier((mine, decoded))
    blocks = add_up(place, mine, sums)
    blocks = (blocks[0],) + tuple(swap(blocks[n + 1], 0, n) for n in range(3))
    attn_out = finish(place, resid[0], gate, blocks)
    return attn_out[None], decoded[None]


def solution(mesh):
    fine = Mesh(mesh.devices.reshape(4, 4, 4, 2), ("grp",) + SEQ)
    placed = (
        P("grp", SEQ, None),
        P("grp", SEQ, None),
        P("grp", SEQ, None),
        P("grp", SEQ, None),
        P("grp", None),
        P(),
        P(),
        P(SEQ, None),
        P("grp", SEQ, None, None),
        P(),
        P(),
        P(),
        P(),
        P(),
    )
    return jax.shard_map(
        on_device,
        mesh=fine,
        in_specs=placed,
        out_specs=(P("grp", SEQ, None), P("grp", None, SEQ, None, None)),
        check_vma=False,
    )
```

```python
import math
import jax
import jax.numpy as jnp
from jax import lax
from jax.experimental import pallas as pl
from jax.experimental.pallas import tpu as pltpu
from jax.sharding import Mesh, PartitionSpec as P

CHIPS = ("z", "x")
SEQ = ("z", "x", "core")
EPS = 1e-06
MIB = 1024 * 1024


def vmem_spec():
    return pl.BlockSpec(memory_space=pltpu.VMEM)


def smem_spec():
    return pl.BlockSpec(memory_space=pltpu.SMEM)


def norm_pack(q, k, v, gain_q, gain_k):
    rows, width = q.shape
    chips = width // 256
    block = 16

    def body(q_ref, k_ref, v_ref, gq_ref, gk_ref, out_ref):
        def normed(ref, gain):
            x = ref[...].astype(jnp.float32)
            factor = lax.rsqrt(jnp.mean(x * x, axis=-1, keepdims=True) + EPS)
            return (x * factor * gain).astype(jnp.bfloat16)

        scale = 128**-0.5 * math.log2(math.e)
        qn = normed(q_ref, gq_ref[...] * scale)
        kn = normed(k_ref, gk_ref[...])
        for c in range(chips):
            cols = slice(256 * c, 256 * c + 256)
            out_ref[c, 0] = qn[:, cols]
            out_ref[c, 1] = kn[:, cols]
            out_ref[c, 2] = v_ref[:, cols]

    tokens = pl.BlockSpec((block, width), lambda i: (i, 0))
    gains = pl.BlockSpec((1, width), lambda i: (0, 0))
    return pl.pallas_call(
        body,
        grid=(rows // block,),
        out_shape=jax.ShapeDtypeStruct((chips, 3, rows, 256), jnp.bfloat16),
        in_specs=[tokens, tokens, tokens, gains, gains],
        out_specs=pl.BlockSpec((chips, 3, block, 256), lambda i: (0, 0, i, 0)),
        compiler_params=pltpu.CompilerParams(vmem_limit_bytes=60 * MIB),
        name="norm_pack",
    )(q, k, v, gain_q, gain_k)


def weight_halves(place, w_here, w_there):
    rows, width = w_here.shape
    part = width // 2

    def body(place_ref, here_ref, there_ref, keep_ref, give_ref):
        here_at = pl.ds(pl.multiple_of(place_ref[1] * rows, rows), rows)
        there_at = pl.ds(pl.multiple_of((1 - place_ref[1]) * rows, rows), rows)

        @pl.when(place_ref[0] == 0)
        def _():
            for k, out in enumerate((keep_ref, give_ref)):
                half = jnp.bitwise_xor(place_ref[4] // 2, k)
                at = pl.ds(pl.multiple_of(half * part, part), part)
                out[here_at] = here_ref[:, at]
                out[there_at] = there_ref[:, at]

    return pl.pallas_call(
        body,
        out_shape=(jax.ShapeDtypeStruct((2 * rows, part), jnp.bfloat16),) * 2,
        in_specs=[smem_spec(), vmem_spec(), vmem_spec()],
        out_specs=(vmem_spec(),) * 2,
        compiler_params=pltpu.CompilerParams(vmem_limit_bytes=16 * MIB),
        name="weight_halves",
    )(place, w_here, w_there)


def inner(position):
    return ((position + 1) // 2) % 2


def attend(place, here, there):
    chips, _, tok, _ = here.shape
    half = chips * tok

    def body(place_ref, here_ref, there_ref, near_ref, other_ref):
        step = pl.program_id(0)

        @pl.when(place_ref[0] == 0)
        def _():
            queries = here_ref[pl.ds(4 * step, 4), 0].reshape(4 * tok, 256)
            ones = jnp.ones((half, 128), jnp.bfloat16)
            heads = []
            for h in range(2):
                cols = slice(128 * h, 128 * h + 128)
                scores = [
                    lax.dot_general(
                        queries[:, cols],
                        ref[:, at, :, cols].reshape(half, 128),
                        (((1,), (1,)), ((), ())),
                        preferred_element_type=jnp.float32,
                    )
                    for ref, at in ((here_ref, 1), (there_ref, 0))
                ]
                peak = jnp.maximum(*(jnp.max(s, axis=-1, keepdims=True) for s in scores))
                o = None
                for s, ref, at in zip(scores, (here_ref, there_ref), (2, 1)):
                    values = jnp.concatenate([ref[:, at, :, cols].reshape(half, 128), ones], axis=1)
                    p = jnp.exp2(s - peak).astype(jnp.bfloat16)
                    part = jnp.dot(p, values, preferred_element_type=jnp.float32)
                    o = part if o is None else o + part
                heads.append(o[:, :128] / o[:, 128:])
            joined = jnp.concatenate(heads, axis=1).astype(jnp.bfloat16)
            for n in range(4):
                first = jnp.where(place_ref[1] == 0, step, n)
                second = jnp.where(place_ref[1] == 0, n, step)
                high = first // 2
                slot = jnp.where(second == 0, 0, jnp.where(second == 3, 1, second + 1))
                near = inner(first) == inner(place_ref[4])
                piece = joined[tok * n : tok * n + tok]

                @pl.when(near)
                def _():
                    near_ref[slot, high] = piece

                @pl.when(jnp.logical_not(near))
                def _():
                    other_ref[slot, high] = piece

    return pl.pallas_call(
        body,
        grid=(chips // 4,),
        out_shape=(jax.ShapeDtypeStruct((4, 2, tok, 256), jnp.bfloat16),) * 2,
        in_specs=[smem_spec(), vmem_spec(), vmem_spec()],
        out_specs=(vmem_spec(),) * 2,
        compiler_params=pltpu.CompilerParams(vmem_limit_bytes=40 * MIB),
        cost_estimate=pl.CostEstimate(flops=0, bytes_accessed=0, transcendentals=0),
        name="attend",
    )(place, here, there)


def project(place, heads, weights):
    _, two, tok, _ = heads[0].shape
    part = weights[0].shape[1]
    lot = two * tok

    def body(place_ref, h0, h1, h2, h3, w0, w1, w2, w3, own_ref, one_ref, zero_ref, far_ref):
        second = place_ref[5]
        slot = jnp.where(second == 0, 0, jnp.where(second == 3, 1, second + 1))

        @pl.when(place_ref[0] == 0)
        def _():
            weight = jnp.concatenate([w0[...], w1[...], w2[...], w3[...]], axis=0)
            feats = jnp.concatenate(
                [
                    jnp.concatenate(
                        [h[jnp.bitwise_xor(slot, k)].reshape(lot, 256) for h in (h0, h1, h2, h3)],
                        axis=1,
                    )
                    for k in range(4)
                ],
                axis=0,
            )
            out = jnp.dot(feats, weight, preferred_element_type=jnp.float32)
            for k, ref in enumerate((own_ref, one_ref, zero_ref, far_ref)):
                ref[...] = out[lot * k : lot * k + lot].reshape(two, tok, part).astype(ref.dtype)

    shape = (two, tok, part)
    return pl.pallas_call(
        body,
        out_shape=(jax.ShapeDtypeStruct(shape, jnp.float32),)
        + (jax.ShapeDtypeStruct(shape, jnp.bfloat16),) * 3,
        in_specs=[smem_spec()] + [vmem_spec()] * 8,
        out_specs=(vmem_spec(),) * 4,
        compiler_params=pltpu.CompilerParams(vmem_limit_bytes=40 * MIB),
        cost_estimate=pl.CostEstimate(
            flops=8 * lot * 1024 * part, bytes_accessed=8 * MIB, transcendentals=0
        ),
        name="project",
    )(place, *heads, *weights)


def add_up(place, own, others):
    def body(place_ref, own_ref, a_ref, b_ref, c_ref, keep_ref, give_ref):
        mine = place_ref[4] // 2

        @pl.when(place_ref[0] == 0)
        def _():
            for at, out in ((mine, keep_ref), (1 - mine, give_ref)):
                total = own_ref[at]
                for ref in (a_ref, b_ref, c_ref):
                    total += ref[at].astype(jnp.float32)
                out[...] = total.astype(out.dtype)

    return pl.pallas_call(
        body,
        out_shape=(
            jax.ShapeDtypeStruct(own.shape[1:], jnp.float32),
            jax.ShapeDtypeStruct(own.shape[1:], jnp.bfloat16),
        ),
        in_specs=[smem_spec()] + [vmem_spec()] * 4,
        out_specs=(vmem_spec(),) * 2,
        compiler_params=pltpu.CompilerParams(vmem_limit_bytes=24 * MIB),
        name="add_up",
    )(place, own, *others)


def finish(place, resid, gate, kept, got):
    part = kept.shape[1]

    def body(place_ref, resid_ref, gate_ref, kept_ref, got_ref, out_ref):
        @pl.when(place_ref[0] == 0)
        def _():
            for k, ref in enumerate((kept_ref, got_ref)):
                half = jnp.bitwise_xor(place_ref[4] // 2, k)
                at = pl.ds(pl.multiple_of(half * part, part), part)
                total = resid_ref[:, at].astype(jnp.float32)
                total += gate_ref[:, at] * ref[...].astype(jnp.float32)
                out_ref[:, at] = total.astype(jnp.bfloat16)

        @pl.when(place_ref[0] == 1)
        def _():
            out_ref[...] = jnp.zeros(out_ref.shape, out_ref.dtype)

    return pl.pallas_call(
        body,
        out_shape=jax.ShapeDtypeStruct(resid.shape, jnp.bfloat16),
        in_specs=[smem_spec()] + [vmem_spec()] * 4,
        out_specs=vmem_spec(),
        compiler_params=pltpu.CompilerParams(vmem_limit_bytes=16 * MIB),
        name="finish",
    )(place, resid, gate, kept, got)


def filter_weights(place, w_mid, start, count):
    steps, deep, vc = w_mid.shape
    taps = w_mid.reshape(steps, 3, 3, vc, vc)

    def block(w_ref, out_ref):
        up, mid, down = (jnp.transpose(w_ref[0, n, 0]) for n in range(3))
        ends = 0.5 * (up.astype(jnp.float32) + down.astype(jnp.float32))
        half = 0.5 * mid.astype(jnp.float32)
        for n, g in enumerate((up, ends + half, ends - half, down)):
            out_ref[n] = g.astype(jnp.bfloat16)

    def body(place_ref, w_ref, out_ref):
        @pl.when(place_ref[0] == 1)
        def _():
            pltpu.emit_pipeline(
                block,
                grid=(count,),
                in_specs=[
                    pl.BlockSpec(
                        (1, 3, 1, vc, vc), lambda i: ((i + start) // 3, 0, (i + start) % 3, 0, 0)
                    )
                ],
                out_specs=[pl.BlockSpec((4, vc, vc), lambda i: (0, 0, i))],
            )(w_ref, out_ref)

    return pl.pallas_call(
        body,
        out_shape=jax.ShapeDtypeStruct((4, vc, count * vc), jnp.bfloat16),
        in_specs=[smem_spec(), pl.BlockSpec(memory_space=pl.ANY)],
        out_specs=pl.BlockSpec(memory_space=pl.ANY),
        compiler_params=pltpu.CompilerParams(vmem_limit_bytes=56 * MIB),
        name="filter_weights_%d" % start,
    )(place, taps)


def decode(place, clip, w_in, filters, vectors):
    frames, _, lc, lw = clip.shape
    fan, vc = w_in.shape
    deep = 3 * vc
    lot = 4
    wide = 512
    cut = filters[0].shape[2]

    def body(
        place_ref, clip_ref, win_ref, fa_ref, fb_ref, rows_ref, out_ref,
        lat, act, firsts, w1_ref, vec_ref, w2, both, sems,
    ):
        step = pl.program_id(0)
        here = place_ref[0] == 1
        loads = [
            pltpu.make_async_copy(fa_ref, w2.at[:, :, pl.ds(0, cut)], sems.at[0]),
            pltpu.make_async_copy(fb_ref, w2.at[:, :, pl.ds(cut, 3 * deep - cut)], sems.at[1]),
        ]

        def moved(x):
            lane = lax.broadcasted_iota(jnp.int32, x.shape, x.ndim - 1)
            left = jnp.where(lane == 0, 0.0, pltpu.roll(x, 1, x.ndim - 1))
            right = jnp.where(lane == lw - 1, 0.0, pltpu.roll(x, lw - 1, x.ndim - 1))
            return left, x, right

        def first(f):
            sides = []
            for row in range(4):
                taps = [lat[f + dt, row : row + 3].reshape(9 * lc, lw) for dt in range(3)]
                taps.append(jnp.zeros((wide - fan, lw), jnp.bfloat16))
                sides.append(jnp.concatenate(taps, axis=0))
            y = jnp.dot(
                w1_ref[...], jnp.concatenate(sides, axis=1), preferred_element_type=jnp.float32
            )
            acts = []
            for row in range(4):
                hidden = y[:, row * lw : row * lw + lw] + vec_ref[0]
                if row in (1, 2):
                    firsts[lax.rem(f, 2 * lot), row - 1] = hidden
                factor = lax.rsqrt(jnp.mean(hidden * hidden, axis=0, keepdims=True) + EPS)
                if row == 0:
                    factor = jnp.where(place_ref[2] == 0, 0.0, factor)
                if row == 3:
                    factor = jnp.where(place_ref[2] == place_ref[3], 0.0, factor)
                half = hidden * (0.5 * factor) * vec_ref[1]
                acts.append(half * (1.0 + jnp.tanh(half)))
            a0, a1, a2, a3 = acts
            for n, u in enumerate((a0 - a2, a1 + a2, a2 - a1, a1 - a3)):
                for dx, piece in enumerate(moved(u)):
                    act[n, f + 2, dx * vc : dx * vc + vc] = piece.astype(jnp.bfloat16)

        @pl.when(here & (step == 0))
        def _():
            for load in loads:
                load.start()
            w1_ref[:, :fan] = jnp.transpose(win_ref[...])
            w1_ref[:, fan:] = jnp.zeros((vc, wide - fan), jnp.bfloat16)
            for n in range(3):
                row = jnp.broadcast_to(rows_ref[n : n + 1], (lw, vc))
                vec_ref[n] = jnp.transpose(row)
            lat[:2] = jnp.zeros((2, 6, 3 * lc, lw), jnp.bfloat16)
            act[:, :2] = jnp.zeros((4, 2, deep, lw), jnp.bfloat16)
            cells = clip_ref[...].astype(jnp.float32)
            for dx, piece in enumerate(moved(cells)):
                lat[2:, :, dx * lc : dx * lc + lc] = piece.astype(jnp.bfloat16)

            @pl.loop(0, lot)
            def _(f):
                first(f)

            for load in loads:
                load.wait()

        def second(and_next):
            base = lot * step
            for n in range(4):
                taps = jnp.concatenate(
                    [act[n, pl.ds(base + j, 3)].reshape(3 * deep, lw) for j in range(lot)], axis=1
                )
                m = jnp.dot(w2[n], taps, preferred_element_type=jnp.float32)
                if n == 0:
                    both[0] = m
                if n == 1:
                    both[0] += m
                    both[1] = m
                if n == 2:
                    both[0] += m
                    both[1] -= m
                if n == 3:
                    both[1] -= m
                if and_next:
                    first(base + lot + n)
            for j in range(lot):
                for r in range(2):
                    whole = both[r, :, j * lw : j * lw + lw]
                    whole += vec_ref[2] + firsts[lax.rem(base + j, 2 * lot), r]
                    out_ref[j, r] = jnp.transpose(whole).astype(jnp.bfloat16)

        @pl.when(here & (step < frames // lot - 1))
        def _():
            second(True)

        @pl.when(here & (step == frames // lot - 1))
        def _():
            second(False)

        @pl.when(jnp.logical_not(here))
        def _():
            out_ref[...] = jnp.zeros(out_ref.shape, out_ref.dtype)

    return pl.pallas_call(
        body,
        grid=(frames // lot,),
        out_shape=jax.ShapeDtypeStruct((frames, 2, lw, vc), jnp.bfloat16),
        in_specs=[
            smem_spec(),
            vmem_spec(),
            vmem_spec(),
            pl.BlockSpec(memory_space=pl.ANY),
            pl.BlockSpec(memory_space=pl.ANY),
            vmem_spec(),
        ],
        out_specs=pl.BlockSpec((lot, 2, lw, vc), lambda i: (i, 0, 0, 0)),
        scratch_shapes=[
            pltpu.VMEM((frames + 2, 6, 3 * lc, lw), jnp.bfloat16),
            pltpu.VMEM((4, frames + 2, deep, lw), jnp.bfloat16),
            pltpu.VMEM((2 * lot, 2, vc, lw), jnp.float32),
            pltpu.VMEM((vc, wide), jnp.bfloat16),
            pltpu.VMEM((3, vc, lw), jnp.float32),
            pltpu.VMEM((4, vc, 3 * deep), jnp.bfloat16),
            pltpu.VMEM((2, vc, lot * lw), jnp.float32),
            pltpu.SemaphoreType.DMA((2,)),
        ],
        compiler_params=pltpu.CompilerParams(vmem_limit_bytes=48 * MIB),
        cost_estimate=pl.CostEstimate(flops=0, bytes_accessed=0, transcendentals=0),
        name="decode",
    )(place, clip, w_in, *filters, vectors)


def on_device(
    query_input,
    key_input,
    value_input,
    resid,
    gate,
    query_norm_gain,
    key_norm_gain,
    output_weight,
    latents,
    w_in,
    b_in,
    norm_gain,
    w_mid,
    b_mid,
):
    last = lax.axis_size("grp") - 1
    decoder_here = lax.axis_index("grp") == last
    count = lax.axis_size(SEQ)
    side = lax.axis_size("z")
    core, at_z, at_x = lax.axis_index("core"), lax.axis_index("z"), lax.axis_index("x")
    place = jnp.stack(
        [
            decoder_here.astype(jnp.int32),
            core,
            lax.axis_index(SEQ),
            jnp.int32(count - 1),
            jnp.where(core == 0, at_z, at_x),
            jnp.where(core == 0, at_x, at_z),
        ]
    )
    channels = w_in.shape[2]

    def swap(x, ring, step):
        def partner(place):
            return (place ^ 1, side - 1 - place, place ^ 2)[step]

        pairs = []
        for at in range(last * count):
            g, z, x_, c = at // count, at // (2 * side) % side, at // 2 % side, at % 2
            if ring == 2:
                c = 1 - c
            elif (ring == 0) == (c == 0):
                z = partner(z)
            else:
                x_ = partner(x_)
            pairs.append((at, ((g * side + z) * side + x_) * 2 + c))
        return lax.ppermute(x, ("grp",) + SEQ, pairs)

    packed = norm_pack(
        query_input[0], key_input[0], value_input[0], query_norm_gain[None], key_norm_gain[None]
    )
    packed, w_here = lax.optimization_barrier((packed, output_weight))
    here = lax.all_to_all(packed, CHIPS, split_axis=0, concat_axis=0, tiled=True)

    w_own, w_give = weight_halves(place, w_here, swap(w_here, 2, 0))
    w_own, w_give, latents, w_mid = lax.optimization_barrier((w_own, w_give, latents, w_mid))
    w_next, w_back = swap(w_own, 0, 0), swap(w_give, 0, 1)

    own = jnp.swapaxes(latents, 2, 3)
    pieces = [lax.ppermute(own, "grp", [(g, last)]) for g in range(last)]
    early = filter_weights(place, w_mid, 0, 5)
    pieces, early = lax.optimization_barrier((pieces, early))
    clip = jnp.concatenate(pieces + [own], axis=0)
    links = [(last * count + i, last * count + i + 1) for i in range(count - 1)]
    above = lax.ppermute(clip, ("grp",) + SEQ, links)
    below = lax.ppermute(clip, ("grp",) + SEQ, [(b, a) for a, b in links])
    late = filter_weights(place, w_mid, 5, 4)
    above, below, late = lax.optimization_barrier((above, below, late))
    cells = jnp.concatenate([above, clip, below], axis=1)

    here, cells = lax.optimization_barrier((here, cells))
    there = swap(here[:, 1:], 2, 0)
    there, w_next, w_back = lax.optimization_barrier((there, w_next, w_back))
    near, other = attend(place, here, there)
    near, other, w_back = lax.optimization_barrier((near, other, w_back))
    w_far = swap(w_back, 0, 0)
    from_far = swap(other, 0, 2)
    heads = near, swap(other, 0, 0), swap(near, 0, 1), from_far
    mine, one, zero, far = project(place, heads, (w_own, w_next, w_back, w_far))
    mine, one, zero, far, cells = lax.optimization_barrier((mine, one, zero, far, cells))
    sums = swap(far, 1, 2), swap(one, 1, 1), swap(zero, 1, 0)
    decoded = decode(
        place, cells, w_in.reshape(-1, channels), (early, late), jnp.stack([b_in, norm_gain, b_mid])
    )
    mine, decoded = lax.optimization_barrier((mine, decoded))
    kept, give = add_up(place, mine, sums)
    attn_out = finish(place, resid[0], gate, kept, swap(give, 0, 1))
    return attn_out[None], decoded[None]


def solution(mesh):
    fine = Mesh(mesh.devices.reshape(4, 4, 4, 2), ("grp",) + SEQ)
    placed = (
        P("grp", SEQ, None),
        P("grp", SEQ, None),
        P("grp", SEQ, None),
        P("grp", SEQ, None),
        P("grp", None),
        P(),
        P(),
        P(SEQ, None),
        P("grp", SEQ, None, None),
        P(),
        P(),
        P(),
        P(),
        P(),
    )
    return jax.shard_map(
        on_device,
        mesh=fine,
        in_specs=placed,
        out_specs=(P("grp", SEQ, None), P("grp", None, SEQ, None, None)),
        check_vma=False,
    )
```

```python
import math
import jax
import jax.numpy as jnp
from jax import lax
from jax.experimental import pallas as pl
from jax.experimental.pallas import tpu as pltpu
from jax.sharding import Mesh, PartitionSpec as P

CHIPS = ("z", "x")
SEQ = ("z", "x", "core")
EPS = 1e-06
MIB = 1024 * 1024


def vmem_spec():
    return pl.BlockSpec(memory_space=pltpu.VMEM)


def smem_spec():
    return pl.BlockSpec(memory_space=pltpu.SMEM)


def norm_pack(q, k, v, gain_q, gain_k):
    rows, width = q.shape
    chips = width // 256
    block = 16

    def body(q_ref, k_ref, v_ref, gq_ref, gk_ref, out_ref):
        def normed(ref, gain):
            x = ref[...].astype(jnp.float32)
            factor = lax.rsqrt(jnp.mean(x * x, axis=-1, keepdims=True) + EPS)
            return (x * factor * gain).astype(jnp.bfloat16)

        scale = 128**-0.5 * math.log2(math.e)
        qn = normed(q_ref, gq_ref[...] * scale)
        kn = normed(k_ref, gk_ref[...])
        for c in range(chips):
            cols = slice(256 * c, 256 * c + 256)
            out_ref[c, 0] = qn[:, cols]
            out_ref[c, 1] = kn[:, cols]
            out_ref[c, 2] = v_ref[:, cols]

    tokens = pl.BlockSpec((block, width), lambda i: (i, 0))
    gains = pl.BlockSpec((1, width), lambda i: (0, 0))
    return pl.pallas_call(
        body,
        grid=(rows // block,),
        out_shape=jax.ShapeDtypeStruct((chips, 3, rows, 256), jnp.bfloat16),
        in_specs=[tokens, tokens, tokens, gains, gains],
        out_specs=pl.BlockSpec((chips, 3, block, 256), lambda i: (0, 0, i, 0)),
        compiler_params=pltpu.CompilerParams(vmem_limit_bytes=60 * MIB),
        name="norm_pack",
    )(q, k, v, gain_q, gain_k)


def weight_halves(place, w_here, w_there):
    rows, width = w_here.shape
    part = width // 2

    def body(place_ref, here_ref, there_ref, keep_ref, give_ref):
        here_at = pl.ds(pl.multiple_of(place_ref[1] * rows, rows), rows)
        there_at = pl.ds(pl.multiple_of((1 - place_ref[1]) * rows, rows), rows)

        @pl.when(place_ref[0] == 0)
        def _():
            for k, out in enumerate((keep_ref, give_ref)):
                half = jnp.bitwise_xor(place_ref[4] // 2, k)
                at = pl.ds(pl.multiple_of(half * part, part), part)
                out[here_at] = here_ref[:, at]
                out[there_at] = there_ref[:, at]

    return pl.pallas_call(
        body,
        out_shape=(jax.ShapeDtypeStruct((2 * rows, part), jnp.bfloat16),) * 2,
        in_specs=[smem_spec(), vmem_spec(), vmem_spec()],
        out_specs=(vmem_spec(),) * 2,
        compiler_params=pltpu.CompilerParams(vmem_limit_bytes=16 * MIB),
        name="weight_halves",
    )(place, w_here, w_there)


def inner(position):
    return ((position + 1) // 2) % 2


def passed(*arrays):
    def body(*refs):
        pass

    return pl.pallas_call(
        body,
        out_shape=tuple(jax.ShapeDtypeStruct(x.shape, x.dtype) for x in arrays),
        in_specs=[pl.BlockSpec(memory_space=pl.ANY)] * len(arrays),
        out_specs=(pl.BlockSpec(memory_space=pl.ANY),) * len(arrays),
        input_output_aliases={n: n for n in range(len(arrays))},
        cost_estimate=pl.CostEstimate(flops=2000000000, bytes_accessed=0, transcendentals=0),
        name="passed",
    )(*arrays)


def attend(place, here, there):
    chips, _, tok, _ = here.shape
    half = chips * tok

    def body(place_ref, here_ref, there_ref, near_ref, other_ref):
        step = pl.program_id(0)

        @pl.when(place_ref[0] == 0)
        def _():
            queries = here_ref[pl.ds(4 * step, 4), 0].reshape(4 * tok, 256)
            ones = jnp.ones((half, 128), jnp.bfloat16)
            heads = []
            for h in range(2):
                cols = slice(128 * h, 128 * h + 128)
                scores = [
                    lax.dot_general(
                        queries[:, cols],
                        ref[:, at, :, cols].reshape(half, 128),
                        (((1,), (1,)), ((), ())),
                        preferred_element_type=jnp.float32,
                    )
                    for ref, at in ((here_ref, 1), (there_ref, 0))
                ]
                peak = jnp.maximum(*(jnp.max(s, axis=-1, keepdims=True) for s in scores))
                o = None
                for s, ref, at in zip(scores, (here_ref, there_ref), (2, 1)):
                    values = jnp.concatenate([ref[:, at, :, cols].reshape(half, 128), ones], axis=1)
                    p = jnp.exp2(s - peak).astype(jnp.bfloat16)
                    part = jnp.dot(p, values, preferred_element_type=jnp.float32)
                    o = part if o is None else o + part
                heads.append(o[:, :128] / o[:, 128:])
            joined = jnp.concatenate(heads, axis=1).astype(jnp.bfloat16)
            for n in range(4):
                first = jnp.where(place_ref[1] == 0, step, n)
                second = jnp.where(place_ref[1] == 0, n, step)
                high = first // 2
                slot = jnp.where(second == 0, 0, jnp.where(second == 3, 1, second + 1))
                near = inner(first) == inner(place_ref[4])
                piece = joined[tok * n : tok * n + tok]

                @pl.when(near)
                def _():
                    near_ref[slot, high] = piece

                @pl.when(jnp.logical_not(near))
                def _():
                    other_ref[slot, high] = piece

    return pl.pallas_call(
        body,
        grid=(chips // 4,),
        out_shape=(jax.ShapeDtypeStruct((4, 2, tok, 256), jnp.bfloat16),) * 2,
        in_specs=[smem_spec(), vmem_spec(), vmem_spec()],
        out_specs=(vmem_spec(),) * 2,
        compiler_params=pltpu.CompilerParams(vmem_limit_bytes=40 * MIB),
        cost_estimate=pl.CostEstimate(flops=0, bytes_accessed=0, transcendentals=0),
        name="attend",
    )(place, here, there)


def project(place, heads, weights):
    _, two, tok, _ = heads[0].shape
    part = weights[0].shape[1]
    lot = two * tok

    def body(place_ref, h0, h1, h2, h3, w0, w1, w2, w3, own_ref, one_ref, zero_ref, far_ref):
        second = place_ref[5]
        slot = jnp.where(second == 0, 0, jnp.where(second == 3, 1, second + 1))

        @pl.when(place_ref[0] == 0)
        def _():
            weight = jnp.concatenate([w0[...], w1[...], w2[...], w3[...]], axis=0)
            feats = jnp.concatenate(
                [
                    jnp.concatenate(
                        [h[jnp.bitwise_xor(slot, k)].reshape(lot, 256) for h in (h0, h1, h2, h3)],
                        axis=1,
                    )
                    for k in range(4)
                ],
                axis=0,
            )
            out = jnp.dot(feats, weight, preferred_element_type=jnp.float32)
            for k, ref in enumerate((own_ref, one_ref, zero_ref, far_ref)):
                ref[...] = out[lot * k : lot * k + lot].reshape(two, tok, part).astype(ref.dtype)

    shape = (two, tok, part)
    return pl.pallas_call(
        body,
        out_shape=(jax.ShapeDtypeStruct(shape, jnp.float32),)
        + (jax.ShapeDtypeStruct(shape, jnp.bfloat16),) * 3,
        in_specs=[smem_spec()] + [vmem_spec()] * 8,
        out_specs=(vmem_spec(),) * 4,
        compiler_params=pltpu.CompilerParams(vmem_limit_bytes=40 * MIB),
        cost_estimate=pl.CostEstimate(
            flops=8 * lot * 1024 * part, bytes_accessed=8 * MIB, transcendentals=0
        ),
        name="project",
    )(place, *heads, *weights)


def add_up(place, own, others):
    def body(place_ref, own_ref, a_ref, b_ref, c_ref, keep_ref, give_ref):
        mine = place_ref[4] // 2

        @pl.when(place_ref[0] == 0)
        def _():
            for at, out in ((mine, keep_ref), (1 - mine, give_ref)):
                total = own_ref[at]
                for ref in (a_ref, b_ref, c_ref):
                    total += ref[at].astype(jnp.float32)
                out[...] = total.astype(out.dtype)

    return pl.pallas_call(
        body,
        out_shape=(
            jax.ShapeDtypeStruct(own.shape[1:], jnp.float32),
            jax.ShapeDtypeStruct(own.shape[1:], jnp.bfloat16),
        ),
        in_specs=[smem_spec()] + [vmem_spec()] * 4,
        out_specs=(vmem_spec(),) * 2,
        compiler_params=pltpu.CompilerParams(vmem_limit_bytes=24 * MIB),
        name="add_up",
    )(place, own, *others)


def finish(place, resid, gate, kept, got):
    part = kept.shape[1]

    def body(place_ref, resid_ref, gate_ref, kept_ref, got_ref, out_ref):
        @pl.when(place_ref[0] == 0)
        def _():
            for k, ref in enumerate((kept_ref, got_ref)):
                half = jnp.bitwise_xor(place_ref[4] // 2, k)
                at = pl.ds(pl.multiple_of(half * part, part), part)
                total = resid_ref[:, at].astype(jnp.float32)
                total += gate_ref[:, at] * ref[...].astype(jnp.float32)
                out_ref[:, at] = total.astype(jnp.bfloat16)

        @pl.when(place_ref[0] == 1)
        def _():
            out_ref[...] = jnp.zeros(out_ref.shape, out_ref.dtype)

    return pl.pallas_call(
        body,
        out_shape=jax.ShapeDtypeStruct(resid.shape, jnp.bfloat16),
        in_specs=[smem_spec()] + [vmem_spec()] * 4,
        out_specs=vmem_spec(),
        compiler_params=pltpu.CompilerParams(vmem_limit_bytes=16 * MIB),
        name="finish",
    )(place, resid, gate, kept, got)


def filter_weights(place, w_mid, start, count):
    steps, deep, vc = w_mid.shape
    taps = w_mid.reshape(steps, 3, 3, vc, vc)

    def block(w_ref, out_ref):
        up, mid, down = (jnp.transpose(w_ref[0, n, 0]) for n in range(3))
        ends = 0.5 * (up.astype(jnp.float32) + down.astype(jnp.float32))
        half = 0.5 * mid.astype(jnp.float32)
        for n, g in enumerate((up, ends + half, ends - half, down)):
            out_ref[n] = g.astype(jnp.bfloat16)

    def body(place_ref, w_ref, out_ref):
        @pl.when(place_ref[0] == 1)
        def _():
            pltpu.emit_pipeline(
                block,
                grid=(count,),
                in_specs=[
                    pl.BlockSpec(
                        (1, 3, 1, vc, vc), lambda i: ((i + start) // 3, 0, (i + start) % 3, 0, 0)
                    )
                ],
                out_specs=[pl.BlockSpec((4, vc, vc), lambda i: (0, 0, i))],
            )(w_ref, out_ref)

    return pl.pallas_call(
        body,
        out_shape=jax.ShapeDtypeStruct((4, vc, count * vc), jnp.bfloat16),
        in_specs=[smem_spec(), pl.BlockSpec(memory_space=pl.ANY)],
        out_specs=pl.BlockSpec(memory_space=pl.ANY),
        compiler_params=pltpu.CompilerParams(vmem_limit_bytes=56 * MIB),
        name="filter_weights_%d" % start,
    )(place, taps)


def decode(place, clip, w_in, filters, vectors):
    frames, _, lc, lw = clip.shape
    fan, vc = w_in.shape
    deep = 3 * vc
    lot = 4
    wide = 512
    cut = filters[0].shape[2]

    def body(
        place_ref, clip_ref, win_ref, fa_ref, fb_ref, rows_ref, out_ref,
        lat, act, firsts, w1_ref, vec_ref, w2, both, sems,
    ):
        step = pl.program_id(0)
        here = place_ref[0] == 1
        loads = [
            pltpu.make_async_copy(fa_ref, w2.at[:, :, pl.ds(0, cut)], sems.at[0]),
            pltpu.make_async_copy(fb_ref, w2.at[:, :, pl.ds(cut, 3 * deep - cut)], sems.at[1]),
        ]

        def moved(x):
            lane = lax.broadcasted_iota(jnp.int32, x.shape, x.ndim - 1)
            left = jnp.where(lane == 0, 0.0, pltpu.roll(x, 1, x.ndim - 1))
            right = jnp.where(lane == lw - 1, 0.0, pltpu.roll(x, lw - 1, x.ndim - 1))
            return left, x, right

        def first(f):
            sides = []
            for row in range(4):
                taps = [lat[f + dt, row : row + 3].reshape(9 * lc, lw) for dt in range(3)]
                taps.append(jnp.zeros((wide - fan, lw), jnp.bfloat16))
                sides.append(jnp.concatenate(taps, axis=0))
            y = jnp.dot(
                w1_ref[...], jnp.concatenate(sides, axis=1), preferred_element_type=jnp.float32
            )
            acts = []
            for row in range(4):
                hidden = y[:, row * lw : row * lw + lw] + vec_ref[0]
                if row in (1, 2):
                    firsts[lax.rem(f, 2 * lot), row - 1] = hidden
                factor = lax.rsqrt(jnp.mean(hidden * hidden, axis=0, keepdims=True) + EPS)
                if row == 0:
                    factor = jnp.where(place_ref[2] == 0, 0.0, factor)
                if row == 3:
                    factor = jnp.where(place_ref[2] == place_ref[3], 0.0, factor)
                half = hidden * (0.5 * factor) * vec_ref[1]
                acts.append(half * (1.0 + jnp.tanh(half)))
            a0, a1, a2, a3 = acts
            for n, u in enumerate((a0 - a2, a1 + a2, a2 - a1, a1 - a3)):
                for dx, piece in enumerate(moved(u)):
                    act[n, f + 2, dx * vc : dx * vc + vc] = piece.astype(jnp.bfloat16)

        @pl.when(here & (step == 0))
        def _():
            for load in loads:
                load.start()
            w1_ref[:, :fan] = jnp.transpose(win_ref[...])
            w1_ref[:, fan:] = jnp.zeros((vc, wide - fan), jnp.bfloat16)
            for n in range(3):
                row = jnp.broadcast_to(rows_ref[n : n + 1], (lw, vc))
                vec_ref[n] = jnp.transpose(row)
            lat[:2] = jnp.zeros((2, 6, 3 * lc, lw), jnp.bfloat16)
            act[:, :2] = jnp.zeros((4, 2, deep, lw), jnp.bfloat16)
            cells = clip_ref[...].astype(jnp.float32)
            for dx, piece in enumerate(moved(cells)):
                lat[2:, :, dx * lc : dx * lc + lc] = piece.astype(jnp.bfloat16)

            @pl.loop(0, lot)
            def _(f):
                first(f)

            for load in loads:
                load.wait()

        def second(and_next):
            base = lot * step
            for n in range(4):
                taps = jnp.concatenate(
                    [act[n, pl.ds(base + j, 3)].reshape(3 * deep, lw) for j in range(lot)], axis=1
                )
                m = jnp.dot(w2[n], taps, preferred_element_type=jnp.float32)
                if n == 0:
                    both[0] = m
                if n == 1:
                    both[0] += m
                    both[1] = m
                if n == 2:
                    both[0] += m
                    both[1] -= m
                if n == 3:
                    both[1] -= m
                if and_next:
                    first(base + lot + n)
            for j in range(lot):
                for r in range(2):
                    whole = both[r, :, j * lw : j * lw + lw]
                    whole += vec_ref[2] + firsts[lax.rem(base + j, 2 * lot), r]
                    out_ref[j, r] = jnp.transpose(whole).astype(jnp.bfloat16)

        @pl.when(here & (step < frames // lot - 1))
        def _():
            second(True)

        @pl.when(here & (step == frames // lot - 1))
        def _():
            second(False)

        @pl.when(jnp.logical_not(here))
        def _():
            out_ref[...] = jnp.zeros(out_ref.shape, out_ref.dtype)

    return pl.pallas_call(
        body,
        grid=(frames // lot,),
        out_shape=jax.ShapeDtypeStruct((frames, 2, lw, vc), jnp.bfloat16),
        in_specs=[
            smem_spec(),
            vmem_spec(),
            vmem_spec(),
            pl.BlockSpec(memory_space=pl.ANY),
            pl.BlockSpec(memory_space=pl.ANY),
            vmem_spec(),
        ],
        out_specs=pl.BlockSpec((lot, 2, lw, vc), lambda i: (i, 0, 0, 0)),
        scratch_shapes=[
            pltpu.VMEM((frames + 2, 6, 3 * lc, lw), jnp.bfloat16),
            pltpu.VMEM((4, frames + 2, deep, lw), jnp.bfloat16),
            pltpu.VMEM((2 * lot, 2, vc, lw), jnp.float32),
            pltpu.VMEM((vc, wide), jnp.bfloat16),
            pltpu.VMEM((3, vc, lw), jnp.float32),
            pltpu.VMEM((4, vc, 3 * deep), jnp.bfloat16),
            pltpu.VMEM((2, vc, lot * lw), jnp.float32),
            pltpu.SemaphoreType.DMA((2,)),
        ],
        compiler_params=pltpu.CompilerParams(vmem_limit_bytes=48 * MIB),
        cost_estimate=pl.CostEstimate(flops=0, bytes_accessed=0, transcendentals=0),
        name="decode",
    )(place, clip, w_in, *filters, vectors)


def on_device(
    query_input,
    key_input,
    value_input,
    resid,
    gate,
    query_norm_gain,
    key_norm_gain,
    output_weight,
    latents,
    w_in,
    b_in,
    norm_gain,
    w_mid,
    b_mid,
):
    last = lax.axis_size("grp") - 1
    decoder_here = lax.axis_index("grp") == last
    count = lax.axis_size(SEQ)
    side = lax.axis_size("z")
    core, at_z, at_x = lax.axis_index("core"), lax.axis_index("z"), lax.axis_index("x")
    place = jnp.stack(
        [
            decoder_here.astype(jnp.int32),
            core,
            lax.axis_index(SEQ),
            jnp.int32(count - 1),
            jnp.where(core == 0, at_z, at_x),
            jnp.where(core == 0, at_x, at_z),
        ]
    )
    channels = w_in.shape[2]

    def swap(x, ring, step):
        def partner(place):
            return (place ^ 1, side - 1 - place, place ^ 2)[step]

        pairs = []
        for at in range(last * count):
            g, z, x_, c = at // count, at // (2 * side) % side, at // 2 % side, at % 2
            if ring == 2:
                c = 1 - c
            elif (ring == 0) == (c == 0):
                z = partner(z)
            else:
                x_ = partner(x_)
            pairs.append((at, ((g * side + z) * side + x_) * 2 + c))
        return lax.ppermute(x, ("grp",) + SEQ, pairs)

    packed = norm_pack(
        query_input[0], key_input[0], value_input[0], query_norm_gain[None], key_norm_gain[None]
    )
    packed, latents, w_mid, w_there = lax.optimization_barrier(
        (packed, latents, w_mid, swap(output_weight, 2, 0))
    )
    here = lax.all_to_all(packed, CHIPS, split_axis=0, concat_axis=0, tiled=True)

    w_own, w_give = weight_halves(place, output_weight, w_there)
    w_next, w_back = swap(w_own, 0, 0), swap(w_give, 0, 1)

    own = jnp.swapaxes(latents, 2, 3)
    pieces = [lax.ppermute(own, "grp", [(g, last)]) for g in range(last)]
    early = filter_weights(place, w_mid, 0, 5)
    pieces, early = lax.optimization_barrier((pieces, early))
    clip = jnp.concatenate(pieces + [own], axis=0)
    links = [(last * count + i, last * count + i + 1) for i in range(count - 1)]
    above = lax.ppermute(clip, ("grp",) + SEQ, links)
    below = lax.ppermute(clip, ("grp",) + SEQ, [(b, a) for a, b in links])
    late = filter_weights(place, w_mid, 5, 4)
    above, below, late = lax.optimization_barrier((above, below, late))
    cells = jnp.concatenate([above, clip, below], axis=1)

    w_next, w_back = passed(w_next, w_back)
    w_far = swap(w_back, 0, 0)
    here, cells, w_next, w_back = lax.optimization_barrier((here, cells, w_next, w_back))
    there = swap(here[:, 1:], 2, 0)
    near, other = attend(place, here, there)
    from_far = swap(other, 0, 2)
    heads = near, swap(other, 0, 0), swap(near, 0, 1), from_far
    mine, one, zero, far = project(place, heads, (w_own, w_next, w_back, w_far))
    mine, one, zero, far, cells = lax.optimization_barrier((mine, one, zero, far, cells))
    sums = swap(far, 1, 2), swap(one, 1, 1), swap(zero, 1, 0)
    decoded = decode(
        place, cells, w_in.reshape(-1, channels), (early, late), jnp.stack([b_in, norm_gain, b_mid])
    )
    mine, decoded = lax.optimization_barrier((mine, decoded))
    kept, give = add_up(place, mine, sums)
    attn_out = finish(place, resid[0], gate, kept, swap(give, 0, 1))
    return attn_out[None], decoded[None]


def solution(mesh):
    fine = Mesh(mesh.devices.reshape(4, 4, 4, 2), ("grp",) + SEQ)
    placed = (
        P("grp", SEQ, None),
        P("grp", SEQ, None),
        P("grp", SEQ, None),
        P("grp", SEQ, None),
        P("grp", None),
        P(),
        P(),
        P(SEQ, None),
        P("grp", SEQ, None, None),
        P(),
        P(),
        P(),
        P(),
        P(),
    )
    return jax.shard_map(
        on_device,
        mesh=fine,
        in_specs=placed,
        out_specs=(P("grp", SEQ, None), P("grp", None, SEQ, None, None)),
        check_vma=False,
    )
```

```python
import math
import jax
import jax.numpy as jnp
from jax import lax
from jax.experimental import pallas as pl
from jax.experimental.pallas import tpu as pltpu
from jax.sharding import Mesh, PartitionSpec as P

SEQ = ("z", "x", "core")
EPS = 1e-06
MIB = 1024 * 1024


def vmem_spec():
    return pl.BlockSpec(memory_space=pltpu.VMEM)


def smem_spec():
    return pl.BlockSpec(memory_space=pltpu.SMEM)


def norm_pack(q, k, v, gain_q, gain_k):
    rows, width = q.shape
    heads = width // 128
    block = 16

    def body(q_ref, k_ref, v_ref, gq_ref, gk_ref, out_ref):
        def normed(ref, gain):
            x = ref[...].astype(jnp.float32)
            factor = lax.rsqrt(jnp.mean(x * x, axis=-1, keepdims=True) + EPS)
            return (x * factor * gain).astype(jnp.bfloat16)

        scale = 128**-0.5 * math.log2(math.e)
        qn = normed(q_ref, gq_ref[...] * scale)
        kn = normed(k_ref, gk_ref[...])
        for h in range(heads):
            cols = slice(128 * h, 128 * h + 128)
            out_ref[h, 0] = qn[:, cols]
            out_ref[h, 1] = kn[:, cols]
            out_ref[h, 2] = v_ref[:, cols]

    tokens = pl.BlockSpec((block, width), lambda i: (i, 0))
    gains = pl.BlockSpec((1, width), lambda i: (0, 0))
    return pl.pallas_call(
        body,
        grid=(rows // block,),
        out_shape=jax.ShapeDtypeStruct((heads, 3, rows, 128), jnp.bfloat16),
        in_specs=[tokens, tokens, tokens, gains, gains],
        out_specs=pl.BlockSpec((heads, 3, block, 128), lambda i: (0, 0, i, 0)),
        compiler_params=pltpu.CompilerParams(vmem_limit_bytes=60 * MIB),
        name="norm_pack",
    )(q, k, v, gain_q, gain_k)


def partners(position):
    return position, jnp.bitwise_xor(position, 1), 3 - position, jnp.bitwise_xor(position, 2)


def weight_half(place, w_here, w_there):
    rows, width = w_here.shape
    part = width // 2

    def body(place_ref, here_ref, there_ref, out_ref):
        here_at = pl.ds(pl.multiple_of(place_ref[1] * rows, rows), rows)
        there_at = pl.ds(pl.multiple_of((1 - place_ref[1]) * rows, rows), rows)

        @pl.when(place_ref[0] == 0)
        def _():
            at = pl.ds(pl.multiple_of(place_ref[1] * part, part), part)
            out_ref[here_at] = here_ref[:, at]
            out_ref[there_at] = there_ref[:, at]

    return pl.pallas_call(
        body,
        out_shape=jax.ShapeDtypeStruct((2 * rows, part), jnp.bfloat16),
        in_specs=[smem_spec(), vmem_spec(), vmem_spec()],
        out_specs=vmem_spec(),
        compiler_params=pltpu.CompilerParams(vmem_limit_bytes=16 * MIB),
        name="weight_half",
    )(place, w_here, w_there)


def attend(place, here):
    devices, _, tok, width = here.shape
    keys = devices * tok
    steps, chains = 4, 2
    lot = devices // (steps * chains)

    def body(place_ref, here_ref, out_ref):
        step = pl.program_id(0)

        @pl.when(place_ref[0] == 0)
        def _():
            ones = jnp.ones((keys, width), jnp.bfloat16)
            values = jnp.concatenate([here_ref[:, 2].reshape(keys, width), ones], axis=1)
            for n in range(chains):
                at = pl.ds((step * chains + n) * lot, lot)
                s = lax.dot_general(
                    here_ref[at, 0].reshape(lot * tok, width),
                    here_ref[:, 1].reshape(keys, width),
                    (((1,), (1,)), ((), ())),
                    preferred_element_type=jnp.float32,
                )
                p = jnp.exp2(s - jnp.max(s, axis=-1, keepdims=True)).astype(jnp.bfloat16)
                o = jnp.dot(p, values, preferred_element_type=jnp.float32)
                o = (o[:, :width] / o[:, width:]).astype(jnp.bfloat16)
                out_ref[at] = o.reshape(lot, tok, width)

    return pl.pallas_call(
        body,
        grid=(steps,),
        out_shape=jax.ShapeDtypeStruct((devices, tok, width), jnp.bfloat16),
        in_specs=[smem_spec(), vmem_spec()],
        out_specs=vmem_spec(),
        compiler_params=pltpu.CompilerParams(vmem_limit_bytes=40 * MIB),
        cost_estimate=pl.CostEstimate(flops=0, bytes_accessed=0, transcendentals=0),
        name="attend",
    )(place, here)


def pair_heads(place, here, there):
    devices, tok, width = here.shape

    def body(place_ref, here_ref, there_ref, *outs):
        core = place_ref[1]
        here_at = pl.ds(pl.multiple_of(core * width, width), width)
        there_at = pl.ds(pl.multiple_of((1 - core) * width, width), width)

        @pl.when(place_ref[0] == 0)
        def _():
            for first, out in zip(partners(place_ref[4]), outs):
                for second in range(4):
                    chip = jnp.where(core == 0, 4 * first + second, 4 * second + first)
                    at = pl.ds(2 * chip, 2)
                    out[second, :, :, here_at] = here_ref[at]
                    out[second, :, :, there_at] = there_ref[at]

    return pl.pallas_call(
        body,
        out_shape=(jax.ShapeDtypeStruct((4, 2, tok, 2 * width), jnp.bfloat16),) * 4,
        in_specs=[smem_spec(), vmem_spec(), vmem_spec()],
        out_specs=(vmem_spec(),) * 4,
        compiler_params=pltpu.CompilerParams(vmem_limit_bytes=16 * MIB),
        name="pair_heads",
    )(place, here, there)


def project(place, heads, weights):
    _, two, tok, _ = heads[0].shape
    part = weights[0].shape[1]
    lot = two * tok

    def body(place_ref, h0, h1, h2, h3, w0, w1, w2, w3, *outs):
        @pl.when(place_ref[0] == 0)
        def _():
            weight = jnp.concatenate([w0[...], w1[...], w2[...], w3[...]], axis=0)
            feats = jnp.concatenate(
                [
                    jnp.concatenate([h[chip].reshape(lot, 256) for h in (h0, h1, h2, h3)], axis=1)
                    for chip in partners(place_ref[5])
                ],
                axis=0,
            )
            out = jnp.dot(feats, weight, preferred_element_type=jnp.float32)
            for k, ref in enumerate(outs):
                ref[...] = out[lot * k : lot * k + lot].reshape(two, tok, part).astype(ref.dtype)

    shape = (two, tok, part)
    return pl.pallas_call(
        body,
        out_shape=(jax.ShapeDtypeStruct(shape, jnp.float32),)
        + (jax.ShapeDtypeStruct(shape, jnp.bfloat16),) * 3,
        in_specs=[smem_spec()] + [vmem_spec()] * 8,
        out_specs=(vmem_spec(),) * 4,
        compiler_params=pltpu.CompilerParams(vmem_limit_bytes=40 * MIB),
        cost_estimate=pl.CostEstimate(
            flops=8 * lot * 1024 * part, bytes_accessed=8 * MIB, transcendentals=0
        ),
        name="project",
    )(place, *heads, *weights)


def add_up(place, own, others):
    def body(place_ref, own_ref, a_ref, b_ref, c_ref, keep_ref, give_ref):
        core = place_ref[1]

        @pl.when(place_ref[0] == 0)
        def _():
            for at, out in ((core, keep_ref), (1 - core, give_ref)):
                total = own_ref[at]
                for ref in (a_ref, b_ref, c_ref):
                    total += ref[at].astype(jnp.float32)
                out[...] = total.astype(out.dtype)

    return pl.pallas_call(
        body,
        out_shape=(
            jax.ShapeDtypeStruct(own.shape[1:], jnp.float32),
            jax.ShapeDtypeStruct(own.shape[1:], jnp.bfloat16),
        ),
        in_specs=[smem_spec()] + [vmem_spec()] * 4,
        out_specs=(vmem_spec(),) * 2,
        compiler_params=pltpu.CompilerParams(vmem_limit_bytes=24 * MIB),
        name="add_up",
    )(place, own, *others)


def finish(place, resid, gate, kept, got):
    part = kept.shape[1]

    def body(place_ref, resid_ref, gate_ref, kept_ref, got_ref, out_ref):
        @pl.when(place_ref[0] == 0)
        def _():
            for half, ref in ((place_ref[1], kept_ref), (1 - place_ref[1], got_ref)):
                at = pl.ds(pl.multiple_of(half * part, part), part)
                total = resid_ref[:, at].astype(jnp.float32)
                total += gate_ref[:, at] * ref[...].astype(jnp.float32)
                out_ref[:, at] = total.astype(jnp.bfloat16)

        @pl.when(place_ref[0] == 1)
        def _():
            out_ref[...] = jnp.zeros(out_ref.shape, out_ref.dtype)

    return pl.pallas_call(
        body,
        out_shape=jax.ShapeDtypeStruct(resid.shape, jnp.bfloat16),
        in_specs=[smem_spec()] + [vmem_spec()] * 4,
        out_specs=vmem_spec(),
        compiler_params=pltpu.CompilerParams(vmem_limit_bytes=16 * MIB),
        name="finish",
    )(place, resid, gate, kept, got)


def filter_weights(place, w_mid, start, count):
    steps, deep, vc = w_mid.shape
    taps = w_mid.reshape(steps, 3, 3, vc, vc)

    def block(w_ref, out_ref):
        up, mid, down = (jnp.transpose(w_ref[0, n, 0]) for n in range(3))
        ends = 0.5 * (up.astype(jnp.float32) + down.astype(jnp.float32))
        half = 0.5 * mid.astype(jnp.float32)
        for n, g in enumerate((up, ends + half, ends - half, down)):
            out_ref[n] = g.astype(jnp.bfloat16)

    def body(place_ref, w_ref, out_ref):
        @pl.when(place_ref[0] == 1)
        def _():
            pltpu.emit_pipeline(
                block,
                grid=(count,),
                in_specs=[
                    pl.BlockSpec(
                        (1, 3, 1, vc, vc), lambda i: ((i + start) // 3, 0, (i + start) % 3, 0, 0)
                    )
                ],
                out_specs=[pl.BlockSpec((4, vc, vc), lambda i: (0, 0, i))],
            )(w_ref, out_ref)

    return pl.pallas_call(
        body,
        out_shape=jax.ShapeDtypeStruct((4, vc, count * vc), jnp.bfloat16),
        in_specs=[smem_spec(), pl.BlockSpec(memory_space=pl.ANY)],
        out_specs=pl.BlockSpec(memory_space=pl.ANY),
        compiler_params=pltpu.CompilerParams(vmem_limit_bytes=56 * MIB),
        name="filter_weights_%d" % start,
    )(place, taps)


def decode(place, clip, w_in, filters, vectors):
    frames, _, lc, lw = clip.shape
    fan, vc = w_in.shape
    deep = 3 * vc
    lot = 4
    wide = 512
    cut = filters[0].shape[2]

    def body(
        place_ref, clip_ref, win_ref, fa_ref, fb_ref, rows_ref, out_ref,
        lat, act, firsts, w1_ref, vec_ref, w2, both, sems,
    ):
        step = pl.program_id(0)
        here = place_ref[0] == 1
        loads = [
            pltpu.make_async_copy(fa_ref, w2.at[:, :, pl.ds(0, cut)], sems.at[0]),
            pltpu.make_async_copy(fb_ref, w2.at[:, :, pl.ds(cut, 3 * deep - cut)], sems.at[1]),
        ]

        def moved(x):
            lane = lax.broadcasted_iota(jnp.int32, x.shape, x.ndim - 1)
            left = jnp.where(lane == 0, 0.0, pltpu.roll(x, 1, x.ndim - 1))
            right = jnp.where(lane == lw - 1, 0.0, pltpu.roll(x, lw - 1, x.ndim - 1))
            return left, x, right

        def first(f):
            sides = []
            for row in range(4):
                taps = [lat[f + dt, row : row + 3].reshape(9 * lc, lw) for dt in range(3)]
                taps.append(jnp.zeros((wide - fan, lw), jnp.bfloat16))
                sides.append(jnp.concatenate(taps, axis=0))
            y = jnp.dot(
                w1_ref[...], jnp.concatenate(sides, axis=1), preferred_element_type=jnp.float32
            )
            acts = []
            for row in range(4):
                hidden = y[:, row * lw : row * lw + lw] + vec_ref[0]
                if row in (1, 2):
                    firsts[lax.rem(f, 2 * lot), row - 1] = hidden
                factor = lax.rsqrt(jnp.mean(hidden * hidden, axis=0, keepdims=True) + EPS)
                if row == 0:
                    factor = jnp.where(place_ref[2] == 0, 0.0, factor)
                if row == 3:
                    factor = jnp.where(place_ref[2] == place_ref[3], 0.0, factor)
                half = hidden * (0.5 * factor) * vec_ref[1]
                acts.append(half * (1.0 + jnp.tanh(half)))
            a0, a1, a2, a3 = acts
            for n, u in enumerate((a0 - a2, a1 + a2, a2 - a1, a1 - a3)):
                for dx, piece in enumerate(moved(u)):
                    act[n, f + 2, dx * vc : dx * vc + vc] = piece.astype(jnp.bfloat16)

        @pl.when(here & (step == 0))
        def _():
            for load in loads:
                load.start()
            w1_ref[:, :fan] = jnp.transpose(win_ref[...])
            w1_ref[:, fan:] = jnp.zeros((vc, wide - fan), jnp.bfloat16)
            for n in range(3):
                row = jnp.broadcast_to(rows_ref[n : n + 1], (lw, vc))
                vec_ref[n] = jnp.transpose(row)
            lat[:2] = jnp.zeros((2, 6, 3 * lc, lw), jnp.bfloat16)
            act[:, :2] = jnp.zeros((4, 2, deep, lw), jnp.bfloat16)
            cells = clip_ref[...].astype(jnp.float32)
            for dx, piece in enumerate(moved(cells)):
                lat[2:, :, dx * lc : dx * lc + lc] = piece.astype(jnp.bfloat16)

            @pl.loop(0, lot)
            def _(f):
                first(f)

            for load in loads:
                load.wait()

        def second(and_next):
            base = lot * step
            for n in range(4):
                taps = jnp.concatenate(
                    [act[n, pl.ds(base + j, 3)].reshape(3 * deep, lw) for j in range(lot)], axis=1
                )
                m = jnp.dot(w2[n], taps, preferred_element_type=jnp.float32)
                if n == 0:
                    both[0] = m
                if n == 1:
                    both[0] += m
                    both[1] = m
                if n == 2:
                    both[0] += m
                    both[1] -= m
                if n == 3:
                    both[1] -= m
                if and_next:
                    first(base + lot + n)
            for j in range(lot):
                for r in range(2):
                    whole = both[r, :, j * lw : j * lw + lw]
                    whole += vec_ref[2] + firsts[lax.rem(base + j, 2 * lot), r]
                    out_ref[j, r] = jnp.transpose(whole).astype(jnp.bfloat16)

        @pl.when(here & (step < frames // lot - 1))
        def _():
            second(True)

        @pl.when(here & (step == frames // lot - 1))
        def _():
            second(False)

        @pl.when(jnp.logical_not(here))
        def _():
            out_ref[...] = jnp.zeros(out_ref.shape, out_ref.dtype)

    return pl.pallas_call(
        body,
        grid=(frames // lot,),
        out_shape=jax.ShapeDtypeStruct((frames, 2, lw, vc), jnp.bfloat16),
        in_specs=[
            smem_spec(),
            vmem_spec(),
            vmem_spec(),
            pl.BlockSpec(memory_space=pl.ANY),
            pl.BlockSpec(memory_space=pl.ANY),
            vmem_spec(),
        ],
        out_specs=pl.BlockSpec((lot, 2, lw, vc), lambda i: (i, 0, 0, 0)),
        scratch_shapes=[
            pltpu.VMEM((frames + 2, 6, 3 * lc, lw), jnp.bfloat16),
            pltpu.VMEM((4, frames + 2, deep, lw), jnp.bfloat16),
            pltpu.VMEM((2 * lot, 2, vc, lw), jnp.float32),
            pltpu.VMEM((vc, wide), jnp.bfloat16),
            pltpu.VMEM((3, vc, lw), jnp.float32),
            pltpu.VMEM((4, vc, 3 * deep), jnp.bfloat16),
            pltpu.VMEM((2, vc, lot * lw), jnp.float32),
            pltpu.SemaphoreType.DMA((2,)),
        ],
        compiler_params=pltpu.CompilerParams(vmem_limit_bytes=48 * MIB),
        cost_estimate=pl.CostEstimate(flops=0, bytes_accessed=0, transcendentals=0),
        name="decode",
    )(place, clip, w_in, *filters, vectors)


def on_device(
    query_input,
    key_input,
    value_input,
    resid,
    gate,
    query_norm_gain,
    key_norm_gain,
    output_weight,
    latents,
    w_in,
    b_in,
    norm_gain,
    w_mid,
    b_mid,
):
    last = lax.axis_size("grp") - 1
    decoder_here = lax.axis_index("grp") == last
    count = lax.axis_size(SEQ)
    side = lax.axis_size("z")
    core, at_z, at_x = lax.axis_index("core"), lax.axis_index("z"), lax.axis_index("x")
    place = jnp.stack(
        [
            decoder_here.astype(jnp.int32),
            core,
            lax.axis_index(SEQ),
            jnp.int32(count - 1),
            jnp.where(core == 0, at_z, at_x),
            jnp.where(core == 0, at_x, at_z),
        ]
    )
    channels = w_in.shape[2]

    def swap(x, ring, step):
        def partner(place):
            return (place ^ 1, side - 1 - place, place ^ 2)[step]

        pairs = []
        for at in range(last * count):
            g, z, x_, c = at // count, at // (2 * side) % side, at // 2 % side, at % 2
            if ring == 2:
                c = 1 - c
            elif (ring == 0) == (c == 0):
                z = partner(z)
            else:
                x_ = partner(x_)
            pairs.append((at, ((g * side + z) * side + x_) * 2 + c))
        return lax.ppermute(x, ("grp",) + SEQ, pairs)

    packed = norm_pack(
        query_input[0], key_input[0], value_input[0], query_norm_gain[None], key_norm_gain[None]
    )
    packed, w_here = lax.optimization_barrier((packed, output_weight))
    here = lax.all_to_all(packed, SEQ, split_axis=0, concat_axis=0, tiled=True)

    w_own = weight_half(place, w_here, swap(w_here, 2, 0))
    w_own, latents, w_mid = lax.optimization_barrier((w_own, latents, w_mid))
    w_back = swap(w_own, 0, 1)
    w_next = swap(w_own, 0, 0)

    own = jnp.swapaxes(latents, 2, 3)
    pieces = [lax.ppermute(own, "grp", [(g, last)]) for g in range(last)]
    early = filter_weights(place, w_mid, 0, 5)
    pieces, early = lax.optimization_barrier((pieces, early))
    clip = jnp.concatenate(pieces + [own], axis=0)
    links = [(last * count + i, last * count + i + 1) for i in range(count - 1)]
    above = lax.ppermute(clip, ("grp",) + SEQ, links)
    below = lax.ppermute(clip, ("grp",) + SEQ, [(b, a) for a, b in links])
    late = filter_weights(place, w_mid, 5, 4)
    above, below, late = lax.optimization_barrier((above, below, late))
    cells = jnp.concatenate([above, clip, below], axis=1)

    here, cells = lax.optimization_barrier((here, cells))
    head = attend(place, here)
    head, w_back = lax.optimization_barrier((head, w_back))
    head_there = swap(head, 2, 0)
    w_far = swap(w_back, 0, 0)
    head_there, w_next = lax.optimization_barrier((head_there, w_next))
    heads = pair_heads(place, head, head_there)
    from_far = swap(heads[3], 0, 2)
    heads = heads[0], swap(heads[1], 0, 0), swap(heads[2], 0, 1), from_far
    mine, zero, one, far = project(place, heads, (w_own, w_next, w_back, w_far))
    mine, one, zero, far, cells = lax.optimization_barrier((mine, one, zero, far, cells))
    sums = swap(far, 1, 2), swap(one, 1, 1), swap(zero, 1, 0)
    decoded = decode(
        place, cells, w_in.reshape(-1, channels), (early, late), jnp.stack([b_in, norm_gain, b_mid])
    )
    mine, decoded = lax.optimization_barrier((mine, decoded))
    kept, give = add_up(place, mine, sums)
    attn_out = finish(place, resid[0], gate, kept, swap(give, 2, 0))
    return attn_out[None], decoded[None]


def solution(mesh):
    fine = Mesh(mesh.devices.reshape(4, 4, 4, 2), ("grp",) + SEQ)
    placed = (
        P("grp", SEQ, None),
        P("grp", SEQ, None),
        P("grp", SEQ, None),
        P("grp", SEQ, None),
        P("grp", None),
        P(),
        P(),
        P(SEQ, None),
        P("grp", SEQ, None, None),
        P(),
        P(),
        P(),
        P(),
        P(),
    )
    return jax.shard_map(
        on_device,
        mesh=fine,
        in_specs=placed,
        out_specs=(P("grp", SEQ, None), P("grp", None, SEQ, None, None)),
        check_vma=False,
    )
```

```python
import math
import jax
import jax.numpy as jnp
from jax import lax
from jax.experimental import pallas as pl
from jax.experimental.pallas import tpu as pltpu
from jax.sharding import Mesh, PartitionSpec as P

SEQ = ("z", "x", "core")
EPS = 1e-06
MIB = 1024 * 1024


def vmem_spec():
    return pl.BlockSpec(memory_space=pltpu.VMEM)


def smem_spec():
    return pl.BlockSpec(memory_space=pltpu.SMEM)


def norm_pack(q, k, v, gain_q, gain_k):
    rows, width = q.shape
    heads = width // 128
    block = rows

    def body(q_ref, k_ref, v_ref, gq_ref, gk_ref, out_ref):
        def normed(ref, gain):
            x = ref[...].astype(jnp.float32)
            factor = lax.rsqrt(jnp.mean(x * x, axis=-1, keepdims=True) + EPS)
            return (x * factor * gain).astype(jnp.bfloat16)

        scale = 128**-0.5 * math.log2(math.e)
        qn = normed(q_ref, gq_ref[...] * scale)
        kn = normed(k_ref, gk_ref[...])
        for h in range(heads):
            cols = slice(128 * h, 128 * h + 128)
            out_ref[h, 0] = qn[:, cols]
            out_ref[h, 1] = kn[:, cols]
            out_ref[h, 2] = v_ref[:, cols]

    tokens = pl.BlockSpec((block, width), lambda i: (i, 0))
    gains = pl.BlockSpec((1, width), lambda i: (0, 0))
    return pl.pallas_call(
        body,
        grid=(rows // block,),
        out_shape=jax.ShapeDtypeStruct((heads, 3, rows, 128), jnp.bfloat16),
        in_specs=[tokens, tokens, tokens, gains, gains],
        out_specs=pl.BlockSpec((heads, 3, block, 128), lambda i: (0, 0, i, 0)),
        compiler_params=pltpu.CompilerParams(vmem_limit_bytes=60 * MIB),
        name="norm_pack",
    )(q, k, v, gain_q, gain_k)


def partners(position):
    return position, jnp.bitwise_xor(position, 1), 3 - position, jnp.bitwise_xor(position, 2)


def weight_half(place, w_here, w_there):
    rows, width = w_here.shape
    part = width // 2

    def body(place_ref, here_ref, there_ref, out_ref, sems):
        core = place_ref[1]
        at = pl.ds(pl.multiple_of(core * part, part), part)

        @pl.when(place_ref[0] == 0)
        def _():
            copies = []
            for n, (ref, chip_row) in enumerate(((here_ref, core), (there_ref, 1 - core))):
                to = out_ref.at[pl.ds(pl.multiple_of(chip_row * rows, rows), rows)]
                copies.append(pltpu.make_async_copy(ref.at[:, at], to, sems.at[n]))
            for copy in copies:
                copy.start()
            for copy in copies:
                copy.wait()

    whole = pl.BlockSpec(memory_space=pl.ANY)
    return pl.pallas_call(
        body,
        out_shape=jax.ShapeDtypeStruct((2 * rows, part), jnp.bfloat16),
        in_specs=[smem_spec(), whole, whole],
        out_specs=whole,
        scratch_shapes=[pltpu.SemaphoreType.DMA((2,))],
        name="weight_half",
    )(place, w_here, w_there)


def attend(place, here):
    devices, _, tok, width = here.shape
    keys = devices * tok
    steps, chains = 4, 2
    lot = devices // (steps * chains)

    def body(place_ref, here_ref, out_ref):
        step = pl.program_id(0)

        @pl.when(place_ref[0] == 0)
        def _():
            ones = jnp.ones((keys, width), jnp.bfloat16)
            values = jnp.concatenate([here_ref[:, 2].reshape(keys, width), ones], axis=1)
            for n in range(chains):
                at = pl.ds((step * chains + n) * lot, lot)
                s = lax.dot_general(
                    here_ref[at, 0].reshape(lot * tok, width),
                    here_ref[:, 1].reshape(keys, width),
                    (((1,), (1,)), ((), ())),
                    preferred_element_type=jnp.float32,
                )
                p = jnp.exp2(s - jnp.max(s, axis=-1, keepdims=True)).astype(jnp.bfloat16)
                o = jnp.dot(p, values, preferred_element_type=jnp.float32)
                o = (o[:, :width] / o[:, width:]).astype(jnp.bfloat16)
                out_ref[at] = o.reshape(lot, tok, width)

    return pl.pallas_call(
        body,
        grid=(steps,),
        out_shape=jax.ShapeDtypeStruct((devices, tok, width), jnp.bfloat16),
        in_specs=[smem_spec(), vmem_spec()],
        out_specs=vmem_spec(),
        compiler_params=pltpu.CompilerParams(vmem_limit_bytes=40 * MIB),
        cost_estimate=pl.CostEstimate(flops=0, bytes_accessed=0, transcendentals=0),
        name="attend",
    )(place, here)


def pair_heads(place, here, there):
    devices, tok, width = here.shape

    def body(place_ref, here_ref, there_ref, *outs):
        core = place_ref[1]
        here_at = pl.ds(pl.multiple_of(core * width, width), width)
        there_at = pl.ds(pl.multiple_of((1 - core) * width, width), width)

        @pl.when(place_ref[0] == 0)
        def _():
            for first, out in zip(partners(place_ref[4]), outs):
                for second in range(4):
                    chip = jnp.where(core == 0, 4 * first + second, 4 * second + first)
                    at = pl.ds(2 * chip, 2)
                    out[second, :, :, here_at] = here_ref[at]
                    out[second, :, :, there_at] = there_ref[at]

    return pl.pallas_call(
        body,
        out_shape=(jax.ShapeDtypeStruct((4, 2, tok, 2 * width), jnp.bfloat16),) * 4,
        in_specs=[smem_spec(), vmem_spec(), vmem_spec()],
        out_specs=(vmem_spec(),) * 4,
        compiler_params=pltpu.CompilerParams(vmem_limit_bytes=16 * MIB),
        name="pair_heads",
    )(place, here, there)


def project(place, heads, weights):
    _, two, tok, _ = heads[0].shape
    part = weights[0].shape[1]
    lot = two * tok

    def body(place_ref, h0, h1, h2, h3, w0, w1, w2, w3, *outs):
        @pl.when(place_ref[0] == 0)
        def _():
            weight = jnp.concatenate([w0[...], w1[...], w2[...], w3[...]], axis=0)
            feats = jnp.concatenate(
                [
                    jnp.concatenate([h[chip].reshape(lot, 256) for h in (h0, h1, h2, h3)], axis=1)
                    for chip in partners(place_ref[5])
                ],
                axis=0,
            )
            out = jnp.dot(feats, weight, preferred_element_type=jnp.float32)
            for k, ref in enumerate(outs):
                ref[...] = out[lot * k : lot * k + lot].reshape(two, tok, part).astype(ref.dtype)

    shape = (two, tok, part)
    return pl.pallas_call(
        body,
        out_shape=(jax.ShapeDtypeStruct(shape, jnp.float32),)
        + (jax.ShapeDtypeStruct(shape, jnp.bfloat16),) * 3,
        in_specs=[smem_spec()] + [vmem_spec()] * 8,
        out_specs=(vmem_spec(),) * 4,
        compiler_params=pltpu.CompilerParams(vmem_limit_bytes=40 * MIB),
        cost_estimate=pl.CostEstimate(
            flops=8 * lot * 1024 * part, bytes_accessed=8 * MIB, transcendentals=0
        ),
        name="project",
    )(place, *heads, *weights)


def add_up(place, own, others):
    def body(place_ref, own_ref, a_ref, b_ref, c_ref, keep_ref, give_ref):
        core = place_ref[1]

        @pl.when(place_ref[0] == 0)
        def _():
            for at, out in ((core, keep_ref), (1 - core, give_ref)):
                total = own_ref[at]
                for ref in (a_ref, b_ref, c_ref):
                    total += ref[at].astype(jnp.float32)
                out[...] = total.astype(out.dtype)

    return pl.pallas_call(
        body,
        out_shape=(
            jax.ShapeDtypeStruct(own.shape[1:], jnp.float32),
            jax.ShapeDtypeStruct(own.shape[1:], jnp.bfloat16),
        ),
        in_specs=[smem_spec()] + [vmem_spec()] * 4,
        out_specs=(vmem_spec(),) * 2,
        compiler_params=pltpu.CompilerParams(vmem_limit_bytes=24 * MIB),
        name="add_up",
    )(place, own, *others)


def finish(place, resid, gate, kept, got):
    part = kept.shape[1]

    def body(place_ref, resid_ref, gate_ref, kept_ref, got_ref, out_ref):
        @pl.when(place_ref[0] == 0)
        def _():
            for half, ref in ((place_ref[1], kept_ref), (1 - place_ref[1], got_ref)):
                at = pl.ds(pl.multiple_of(half * part, part), part)
                total = resid_ref[:, at].astype(jnp.float32)
                total += gate_ref[:, at] * ref[...].astype(jnp.float32)
                out_ref[:, at] = total.astype(jnp.bfloat16)

        @pl.when(place_ref[0] == 1)
        def _():
            out_ref[...] = jnp.zeros(out_ref.shape, out_ref.dtype)

    return pl.pallas_call(
        body,
        out_shape=jax.ShapeDtypeStruct(resid.shape, jnp.bfloat16),
        in_specs=[smem_spec()] + [vmem_spec()] * 4,
        out_specs=vmem_spec(),
        compiler_params=pltpu.CompilerParams(vmem_limit_bytes=16 * MIB),
        name="finish",
    )(place, resid, gate, kept, got)


def filter_weights(place, w_mid, start, count):
    steps, deep, vc = w_mid.shape
    taps = w_mid.reshape(steps, 3, 3, vc, vc)

    def block(w_ref, out_ref):
        rows, columns = (lax.broadcasted_iota(jnp.int32, (vc, vc), n) for n in range(2))
        unit = jnp.where(rows == columns, 1.0, 0.0).astype(jnp.bfloat16)
        up, mid, down = (
            lax.dot_general(
                unit,
                w_ref[0, n, 0],
                (((1,), (1,)), ((), ())),
                preferred_element_type=jnp.float32,
            )
            for n in range(3)
        )
        ends = 0.5 * (up + down)
        half = 0.5 * mid
        for n, g in enumerate((up, ends + half, ends - half, down)):
            out_ref[0, n] = g.astype(jnp.bfloat16)

    def body(place_ref, w_ref, out_ref):
        @pl.when(place_ref[0] == 1)
        def _():
            pltpu.emit_pipeline(
                block,
                grid=(count,),
                in_specs=[
                    pl.BlockSpec(
                        (1, 3, 1, vc, vc), lambda i: ((i + start) // 3, 0, (i + start) % 3, 0, 0)
                    )
                ],
                out_specs=[pl.BlockSpec((1, 4, vc, vc), lambda i: (i, 0, 0, 0))],
            )(w_ref, out_ref)

    return pl.pallas_call(
        body,
        out_shape=jax.ShapeDtypeStruct((count, 4, vc, vc), jnp.bfloat16),
        in_specs=[smem_spec(), pl.BlockSpec(memory_space=pl.ANY)],
        out_specs=pl.BlockSpec(memory_space=pl.ANY),
        compiler_params=pltpu.CompilerParams(vmem_limit_bytes=56 * MIB),
        name="filter_weights_%d" % start,
    )(place, taps)


def decode(place, clip, w_in, filters, vectors):
    frames, _, lc, lw = clip.shape
    fan, vc = w_in.shape
    deep = 3 * vc
    lot = 4
    wide = 512
    cut = filters[0].shape[0]

    def body(
        place_ref, clip_ref, win_ref, fa_ref, fb_ref, rows_ref, out_ref,
        lat, act, firsts, w1_ref, vec_ref, w2, both, sems,
    ):
        step = pl.program_id(0)
        here = place_ref[0] == 1
        loads = [
            pltpu.make_async_copy(
                fa_ref.at[n] if n < cut else fb_ref.at[n - cut],
                w2.at[:, :, pl.ds(n * vc, vc)],
                sems.at[n],
            )
            for n in range(9)
        ]

        def moved(x):
            lane = lax.broadcasted_iota(jnp.int32, x.shape, x.ndim - 1)
            left = jnp.where(lane == 0, 0.0, pltpu.roll(x, 1, x.ndim - 1))
            right = jnp.where(lane == lw - 1, 0.0, pltpu.roll(x, lw - 1, x.ndim - 1))
            return left, x, right

        def first(f):
            sides = []
            for row in range(4):
                taps = [lat[f + dt, row : row + 3].reshape(9 * lc, lw) for dt in range(3)]
                taps.append(jnp.zeros((wide - fan, lw), jnp.bfloat16))
                sides.append(jnp.concatenate(taps, axis=0))
            y = jnp.dot(
                w1_ref[...], jnp.concatenate(sides, axis=1), preferred_element_type=jnp.float32
            )
            acts = []
            for row in range(4):
                hidden = y[:, row * lw : row * lw + lw] + vec_ref[0]
                if row in (1, 2):
                    firsts[lax.rem(f, 2 * lot), row - 1] = hidden
                factor = lax.rsqrt(jnp.mean(hidden * hidden, axis=0, keepdims=True) + EPS)
                if row == 0:
                    factor = jnp.where(place_ref[2] == 0, 0.0, factor)
                if row == 3:
                    factor = jnp.where(place_ref[2] == place_ref[3], 0.0, factor)
                half = hidden * (0.5 * factor) * vec_ref[1]
                acts.append(half * (1.0 + jnp.tanh(half)))
            a0, a1, a2, a3 = acts
            for n, u in enumerate((a0 - a2, a1 + a2, a2 - a1, a1 - a3)):
                for dx, piece in enumerate(moved(u)):
                    act[n, f + 2, dx * vc : dx * vc + vc] = piece.astype(jnp.bfloat16)

        @pl.when(here & (step == 0))
        def _():
            for load in loads:
                load.start()
            w1_ref[:, :fan] = jnp.transpose(win_ref[...])
            w1_ref[:, fan:] = jnp.zeros((vc, wide - fan), jnp.bfloat16)
            for n in range(3):
                row = jnp.broadcast_to(rows_ref[n : n + 1], (lw, vc))
                vec_ref[n] = jnp.transpose(row)
            lat[:2] = jnp.zeros((2, 6, 3 * lc, lw), jnp.bfloat16)
            act[:, :2] = jnp.zeros((4, 2, deep, lw), jnp.bfloat16)
            cells = clip_ref[...].astype(jnp.float32)
            for dx, piece in enumerate(moved(cells)):
                lat[2:, :, dx * lc : dx * lc + lc] = piece.astype(jnp.bfloat16)

            for f in range(lot):
                first(f)

            for load in loads:
                load.wait()

        def second(and_next):
            base = lot * step
            for n in range(4):
                taps = jnp.concatenate(
                    [act[n, pl.ds(base + j, 3)].reshape(3 * deep, lw) for j in range(lot)], axis=1
                )
                m = jnp.dot(w2[n], taps, preferred_element_type=jnp.float32)
                if n == 0:
                    both[0] = m
                if n == 1:
                    both[0] += m
                    both[1] = m
                if n == 2:
                    both[0] += m
                    both[1] -= m
                if n == 3:
                    both[1] -= m
                if and_next:
                    first(base + lot + n)
            for j in range(lot):
                for r in range(2):
                    whole = both[r, :, j * lw : j * lw + lw]
                    whole += vec_ref[2] + firsts[lax.rem(base + j, 2 * lot), r]
                    out_ref[j, r] = jnp.transpose(whole).astype(jnp.bfloat16)

        @pl.when(here & (step < frames // lot - 1))
        def _():
            second(True)

        @pl.when(here & (step == frames // lot - 1))
        def _():
            second(False)

        @pl.when(jnp.logical_not(here))
        def _():
            out_ref[...] = jnp.zeros(out_ref.shape, out_ref.dtype)

    return pl.pallas_call(
        body,
        grid=(frames // lot,),
        out_shape=jax.ShapeDtypeStruct((frames, 2, lw, vc), jnp.bfloat16),
        in_specs=[
            smem_spec(),
            vmem_spec(),
            vmem_spec(),
            pl.BlockSpec(memory_space=pl.ANY),
            pl.BlockSpec(memory_space=pl.ANY),
            vmem_spec(),
        ],
        out_specs=pl.BlockSpec((lot, 2, lw, vc), lambda i: (i, 0, 0, 0)),
        scratch_shapes=[
            pltpu.VMEM((frames + 2, 6, 3 * lc, lw), jnp.bfloat16),
            pltpu.VMEM((4, frames + 2, deep, lw), jnp.bfloat16),
            pltpu.VMEM((2 * lot, 2, vc, lw), jnp.float32),
            pltpu.VMEM((vc, wide), jnp.bfloat16),
            pltpu.VMEM((3, vc, lw), jnp.float32),
            pltpu.VMEM((4, vc, 3 * deep), jnp.bfloat16),
            pltpu.VMEM((2, vc, lot * lw), jnp.float32),
            pltpu.SemaphoreType.DMA((9,)),
        ],
        compiler_params=pltpu.CompilerParams(vmem_limit_bytes=48 * MIB),
        cost_estimate=pl.CostEstimate(flops=0, bytes_accessed=0, transcendentals=0),
        name="decode",
    )(place, clip, w_in, *filters, vectors)


def on_device(
    query_input,
    key_input,
    value_input,
    resid,
    gate,
    query_norm_gain,
    key_norm_gain,
    output_weight,
    latents,
    w_in,
    b_in,
    norm_gain,
    w_mid,
    b_mid,
):
    last = lax.axis_size("grp") - 1
    decoder_here = lax.axis_index("grp") == last
    count = lax.axis_size(SEQ)
    side = lax.axis_size("z")
    core, at_z, at_x = lax.axis_index("core"), lax.axis_index("z"), lax.axis_index("x")
    place = jnp.stack(
        [
            decoder_here.astype(jnp.int32),
            core,
            lax.axis_index(SEQ),
            jnp.int32(count - 1),
            jnp.where(core == 0, at_z, at_x),
            jnp.where(core == 0, at_x, at_z),
        ]
    )
    channels = w_in.shape[2]

    def swap(x, ring, step):
        def partner(place):
            return (place ^ 1, side - 1 - place, place ^ 2)[step]

        pairs = []
        for at in range(last * count):
            g, z, x_, c = at // count, at // (2 * side) % side, at // 2 % side, at % 2
            if ring == 2:
                c = 1 - c
            elif (ring == 0) == (c == 0):
                z = partner(z)
            else:
                x_ = partner(x_)
            pairs.append((at, ((g * side + z) * side + x_) * 2 + c))
        return lax.ppermute(x, ("grp",) + SEQ, pairs)

    packed = norm_pack(
        query_input[0], key_input[0], value_input[0], query_norm_gain[None], key_norm_gain[None]
    )
    packed, w_here = lax.optimization_barrier((packed, output_weight))
    here = lax.all_to_all(packed, SEQ, split_axis=0, concat_axis=0, tiled=True)

    w_own = weight_half(place, w_here, swap(w_here, 2, 0))
    w_own, latents, w_mid = lax.optimization_barrier((w_own, latents, w_mid))
    w_back = swap(w_own, 0, 1)
    w_next = swap(w_own, 0, 0)

    own = jnp.swapaxes(latents, 2, 3)
    pieces = [lax.ppermute(own, "grp", [(g, last)]) for g in range(last)]
    early = filter_weights(place, w_mid, 0, 5)
    pieces, early = lax.optimization_barrier((pieces, early))
    clip = jnp.concatenate(pieces + [own], axis=0)
    links = [(last * count + i, last * count + i + 1) for i in range(count - 1)]
    above = lax.ppermute(clip, ("grp",) + SEQ, links)
    below = lax.ppermute(clip, ("grp",) + SEQ, [(b, a) for a, b in links])
    late = filter_weights(place, w_mid, 5, 4)
    above, below, late = lax.optimization_barrier((above, below, late))
    cells = jnp.concatenate([above, clip, below], axis=1)

    here, cells = lax.optimization_barrier((here, cells))
    head = attend(place, here)
    head_there = swap(head, 2, 0)
    head_there, w_next, w_back = lax.optimization_barrier((head_there, w_next, w_back))
    w_far = swap(w_back, 0, 0)
    heads = pair_heads(place, head, head_there)
    from_far = swap(heads[3], 0, 2)
    heads = heads[0], swap(heads[1], 0, 0), swap(heads[2], 0, 1), from_far
    mine, zero, one, far = project(place, heads, (w_own, w_next, w_back, w_far))
    mine, one, zero, far, cells = lax.optimization_barrier((mine, one, zero, far, cells))
    sums = swap(far, 1, 2), swap(one, 1, 1), swap(zero, 1, 0)
    decoded = decode(
        place, cells, w_in.reshape(-1, channels), (early, late), jnp.stack([b_in, norm_gain, b_mid])
    )
    mine, decoded = lax.optimization_barrier((mine, decoded))
    kept, give = add_up(place, mine, sums)
    attn_out = finish(place, resid[0], gate, kept, swap(give, 2, 0))
    return attn_out[None], decoded[None]


def solution(mesh):
    fine = Mesh(mesh.devices.reshape(4, 4, 4, 2), ("grp",) + SEQ)
    placed = (
        P("grp", SEQ, None),
        P("grp", SEQ, None),
        P("grp", SEQ, None),
        P("grp", SEQ, None),
        P("grp", None),
        P(),
        P(),
        P(SEQ, None),
        P("grp", SEQ, None, None),
        P(),
        P(),
        P(),
        P(),
        P(),
    )
    return jax.shard_map(
        on_device,
        mesh=fine,
        in_specs=placed,
        out_specs=(P("grp", SEQ, None), P("grp", None, SEQ, None, None)),
        check_vma=False,
    )
```

```python
import math
import jax
import jax.numpy as jnp
from jax import lax
from jax.experimental import pallas as pl
from jax.experimental.pallas import tpu as pltpu
from jax.sharding import Mesh, PartitionSpec as P

SEQ = ("z", "x", "core")
EPS = 1e-06
MIB = 1024 * 1024


def vmem_spec():
    return pl.BlockSpec(memory_space=pltpu.VMEM)


def smem_spec():
    return pl.BlockSpec(memory_space=pltpu.SMEM)


def norm_pack(q, k, v, gain_q, gain_k):
    rows, width = q.shape
    heads = width // 128
    block = rows

    def body(q_ref, k_ref, v_ref, gq_ref, gk_ref, out_ref):
        def normed(ref, gain):
            x = ref[...].astype(jnp.float32)
            factor = lax.rsqrt(jnp.mean(x * x, axis=-1, keepdims=True) + EPS)
            return (x * factor * gain).astype(jnp.bfloat16)

        scale = 128**-0.5 * math.log2(math.e)
        qn = normed(q_ref, gq_ref[...] * scale)
        kn = normed(k_ref, gk_ref[...])
        for h in range(heads):
            cols = slice(128 * h, 128 * h + 128)
            out_ref[h, 0] = qn[:, cols]
            out_ref[h, 1] = kn[:, cols]
            out_ref[h, 2] = v_ref[:, cols]

    tokens = pl.BlockSpec((block, width), lambda i: (i, 0))
    gains = pl.BlockSpec((1, width), lambda i: (0, 0))
    return pl.pallas_call(
        body,
        grid=(rows // block,),
        out_shape=jax.ShapeDtypeStruct((heads, 3, rows, 128), jnp.bfloat16),
        in_specs=[tokens, tokens, tokens, gains, gains],
        out_specs=pl.BlockSpec((heads, 3, block, 128), lambda i: (0, 0, i, 0)),
        compiler_params=pltpu.CompilerParams(vmem_limit_bytes=60 * MIB),
        name="norm_pack",
    )(q, k, v, gain_q, gain_k)


def partners(position):
    return position, jnp.bitwise_xor(position, 1), 3 - position, jnp.bitwise_xor(position, 2)


def weight_half(place, w_here, w_there):
    rows, width = w_here.shape
    part = width // 2

    def body(place_ref, here_ref, there_ref, out_ref):
        core = place_ref[1]

        @pl.when(place_ref[0] == 0)
        def _():
            out_ref[pl.ds(pl.multiple_of(core * rows, rows), rows)] = here_ref[...]
            out_ref[pl.ds(pl.multiple_of((1 - core) * rows, rows), rows)] = there_ref[...]

    half = pl.BlockSpec((rows, part), lambda i, where: (0, where[1]))
    return pl.pallas_call(
        body,
        grid_spec=pltpu.PrefetchScalarGridSpec(
            num_scalar_prefetch=1,
            grid=(1,),
            in_specs=[half, half],
            out_specs=pl.BlockSpec((2 * rows, part), lambda i, where: (0, 0)),
        ),
        out_shape=jax.ShapeDtypeStruct((2 * rows, part), jnp.bfloat16),
        compiler_params=pltpu.CompilerParams(vmem_limit_bytes=60 * MIB),
        name="weight_half",
    )(place, w_here, w_there)


def attend(place, here):
    devices, _, tok, width = here.shape
    keys = devices * tok
    steps, chains = 4, 2
    lot = devices // (steps * chains)

    def body(place_ref, here_ref, out_ref):
        step = pl.program_id(0)

        @pl.when(place_ref[0] == 0)
        def _():
            ones = jnp.ones((keys, width), jnp.bfloat16)
            values = jnp.concatenate([here_ref[:, 2].reshape(keys, width), ones], axis=1)
            for n in range(chains):
                at = pl.ds((step * chains + n) * lot, lot)
                s = lax.dot_general(
                    here_ref[at, 0].reshape(lot * tok, width),
                    here_ref[:, 1].reshape(keys, width),
                    (((1,), (1,)), ((), ())),
                    preferred_element_type=jnp.float32,
                )
                p = jnp.exp2(s - jnp.max(s, axis=-1, keepdims=True)).astype(jnp.bfloat16)
                o = jnp.dot(p, values, preferred_element_type=jnp.float32)
                o = (o[:, :width] / o[:, width:]).astype(jnp.bfloat16)
                out_ref[at] = o.reshape(lot, tok, width)

    return pl.pallas_call(
        body,
        grid=(steps,),
        out_shape=jax.ShapeDtypeStruct((devices, tok, width), jnp.bfloat16),
        in_specs=[smem_spec(), vmem_spec()],
        out_specs=vmem_spec(),
        compiler_params=pltpu.CompilerParams(vmem_limit_bytes=40 * MIB),
        cost_estimate=pl.CostEstimate(flops=0, bytes_accessed=0, transcendentals=0),
        name="attend",
    )(place, here)


def pair_heads(place, here, there):
    devices, tok, width = here.shape

    def body(place_ref, here_ref, there_ref, *outs):
        core = place_ref[1]
        here_at = pl.ds(pl.multiple_of(core * width, width), width)
        there_at = pl.ds(pl.multiple_of((1 - core) * width, width), width)

        @pl.when(place_ref[0] == 0)
        def _():
            for first, out in zip(partners(place_ref[4]), outs):
                for second in range(4):
                    chip = jnp.where(core == 0, 4 * first + second, 4 * second + first)
                    at = pl.ds(2 * chip, 2)
                    out[second, :, :, here_at] = here_ref[at]
                    out[second, :, :, there_at] = there_ref[at]

    return pl.pallas_call(
        body,
        out_shape=(jax.ShapeDtypeStruct((4, 2, tok, 2 * width), jnp.bfloat16),) * 4,
        in_specs=[smem_spec(), vmem_spec(), vmem_spec()],
        out_specs=(vmem_spec(),) * 4,
        compiler_params=pltpu.CompilerParams(vmem_limit_bytes=16 * MIB),
        name="pair_heads",
    )(place, here, there)


def project(place, heads, weights):
    _, two, tok, _ = heads[0].shape
    part = weights[0].shape[1]
    lot = two * tok

    def body(place_ref, h0, h1, h2, h3, w0, w1, w2, w3, *outs):
        @pl.when(place_ref[0] == 0)
        def _():
            weight = jnp.concatenate([w0[...], w1[...], w2[...], w3[...]], axis=0)
            feats = jnp.concatenate(
                [
                    jnp.concatenate([h[chip].reshape(lot, 256) for h in (h0, h1, h2, h3)], axis=1)
                    for chip in partners(place_ref[5])
                ],
                axis=0,
            )
            out = jnp.dot(feats, weight, preferred_element_type=jnp.float32)
            for k, ref in enumerate(outs):
                ref[...] = out[lot * k : lot * k + lot].reshape(two, tok, part).astype(ref.dtype)

    shape = (two, tok, part)
    return pl.pallas_call(
        body,
        out_shape=(jax.ShapeDtypeStruct(shape, jnp.float32),)
        + (jax.ShapeDtypeStruct(shape, jnp.bfloat16),) * 3,
        in_specs=[smem_spec()] + [vmem_spec()] * 8,
        out_specs=(vmem_spec(),) * 4,
        compiler_params=pltpu.CompilerParams(vmem_limit_bytes=40 * MIB),
        cost_estimate=pl.CostEstimate(
            flops=8 * lot * 1024 * part, bytes_accessed=8 * MIB, transcendentals=0
        ),
        name="project",
    )(place, *heads, *weights)


def add_up(place, own, others):
    def body(place_ref, own_ref, a_ref, b_ref, c_ref, keep_ref, give_ref):
        core = place_ref[1]

        @pl.when(place_ref[0] == 0)
        def _():
            for at, out in ((core, keep_ref), (1 - core, give_ref)):
                total = own_ref[at]
                for ref in (a_ref, b_ref, c_ref):
                    total += ref[at].astype(jnp.float32)
                out[...] = total.astype(out.dtype)

    return pl.pallas_call(
        body,
        out_shape=(
            jax.ShapeDtypeStruct(own.shape[1:], jnp.float32),
            jax.ShapeDtypeStruct(own.shape[1:], jnp.bfloat16),
        ),
        in_specs=[smem_spec()] + [vmem_spec()] * 4,
        out_specs=(vmem_spec(),) * 2,
        compiler_params=pltpu.CompilerParams(vmem_limit_bytes=24 * MIB),
        name="add_up",
    )(place, own, *others)


def finish(place, resid, gate, kept, got):
    part = kept.shape[1]

    def body(place_ref, resid_ref, gate_ref, kept_ref, got_ref, out_ref):
        @pl.when(place_ref[0] == 0)
        def _():
            for half, ref in ((place_ref[1], kept_ref), (1 - place_ref[1], got_ref)):
                at = pl.ds(pl.multiple_of(half * part, part), part)
                total = resid_ref[:, at].astype(jnp.float32)
                total += gate_ref[:, at] * ref[...].astype(jnp.float32)
                out_ref[:, at] = total.astype(jnp.bfloat16)

        @pl.when(place_ref[0] == 1)
        def _():
            out_ref[...] = jnp.zeros(out_ref.shape, out_ref.dtype)

    return pl.pallas_call(
        body,
        out_shape=jax.ShapeDtypeStruct(resid.shape, jnp.bfloat16),
        in_specs=[smem_spec()] + [vmem_spec()] * 4,
        out_specs=vmem_spec(),
        compiler_params=pltpu.CompilerParams(vmem_limit_bytes=16 * MIB),
        name="finish",
    )(place, resid, gate, kept, got)


def filter_weights(place, w_mid, start, count):
    steps, deep, vc = w_mid.shape
    taps = w_mid.reshape(steps, 3, 3, vc, vc)

    def block(w_ref, out_ref):
        up, mid, down = (jnp.transpose(w_ref[0, n, 0]) for n in range(3))
        ends = 0.5 * (up.astype(jnp.float32) + down.astype(jnp.float32))
        half = 0.5 * mid.astype(jnp.float32)
        for n, g in enumerate((up, ends + half, ends - half, down)):
            out_ref[0, n] = g.astype(jnp.bfloat16)

    def body(place_ref, w_ref, out_ref):
        @pl.when(place_ref[0] == 1)
        def _():
            pltpu.emit_pipeline(
                block,
                grid=(count,),
                in_specs=[
                    pl.BlockSpec(
                        (1, 3, 1, vc, vc), lambda i: ((i + start) // 3, 0, (i + start) % 3, 0, 0)
                    )
                ],
                out_specs=[pl.BlockSpec((1, 4, vc, vc), lambda i: (i, 0, 0, 0))],
            )(w_ref, out_ref)

    return pl.pallas_call(
        body,
        out_shape=jax.ShapeDtypeStruct((count, 4, vc, vc), jnp.bfloat16),
        in_specs=[smem_spec(), pl.BlockSpec(memory_space=pl.ANY)],
        out_specs=pl.BlockSpec(memory_space=pl.ANY),
        compiler_params=pltpu.CompilerParams(vmem_limit_bytes=56 * MIB),
        name="filter_weights_%d" % start,
    )(place, taps)


def decode(place, clip, w_in, filters, vectors):
    frames, _, lc, lw = clip.shape
    fan, vc = w_in.shape
    deep = 3 * vc
    lot = 4
    wide = 512
    cut = filters[0].shape[0]

    def body(
        place_ref, clip_ref, win_ref, fa_ref, fb_ref, rows_ref, out_ref,
        lat, act, firsts, w1_ref, vec_ref, w2, both, sems,
    ):
        step = pl.program_id(0)
        here = place_ref[0] == 1
        loads = [
            pltpu.make_async_copy(
                fa_ref.at[n] if n < cut else fb_ref.at[n - cut],
                w2.at[:, :, pl.ds(n * vc, vc)],
                sems.at[n],
            )
            for n in range(9)
        ]

        def moved(x):
            lane = lax.broadcasted_iota(jnp.int32, x.shape, x.ndim - 1)
            left = jnp.where(lane == 0, 0.0, pltpu.roll(x, 1, x.ndim - 1))
            right = jnp.where(lane == lw - 1, 0.0, pltpu.roll(x, lw - 1, x.ndim - 1))
            return left, x, right

        def first(f):
            sides = []
            for row in range(4):
                taps = [lat[f + dt, row : row + 3].reshape(9 * lc, lw) for dt in range(3)]
                taps.append(jnp.zeros((wide - fan, lw), jnp.bfloat16))
                sides.append(jnp.concatenate(taps, axis=0))
            y = jnp.dot(
                w1_ref[...], jnp.concatenate(sides, axis=1), preferred_element_type=jnp.float32
            )
            acts = []
            for row in range(4):
                hidden = y[:, row * lw : row * lw + lw] + vec_ref[0]
                if row in (1, 2):
                    firsts[lax.rem(f, 2 * lot), row - 1] = hidden
                factor = lax.rsqrt(jnp.mean(hidden * hidden, axis=0, keepdims=True) + EPS)
                if row == 0:
                    factor = jnp.where(place_ref[2] == 0, 0.0, factor)
                if row == 3:
                    factor = jnp.where(place_ref[2] == place_ref[3], 0.0, factor)
                half = hidden * (0.5 * factor) * vec_ref[1]
                acts.append(half * (1.0 + jnp.tanh(half)))
            a0, a1, a2, a3 = acts
            for n, u in enumerate((a0 - a2, a1 + a2, a2 - a1, a1 - a3)):
                for dx, piece in enumerate(moved(u)):
                    act[n, f + 2, dx * vc : dx * vc + vc] = piece.astype(jnp.bfloat16)

        @pl.when(here & (step == 0))
        def _():
            for load in loads:
                load.start()
            w1_ref[:, :fan] = jnp.transpose(win_ref[...])
            w1_ref[:, fan:] = jnp.zeros((vc, wide - fan), jnp.bfloat16)
            for n in range(3):
                row = jnp.broadcast_to(rows_ref[n : n + 1], (lw, vc))
                vec_ref[n] = jnp.transpose(row)
            lat[:2] = jnp.zeros((2, 6, 3 * lc, lw), jnp.bfloat16)
            act[:, :2] = jnp.zeros((4, 2, deep, lw), jnp.bfloat16)
            cells = clip_ref[...].astype(jnp.float32)
            for dx, piece in enumerate(moved(cells)):
                lat[2:, :, dx * lc : dx * lc + lc] = piece.astype(jnp.bfloat16)

            for f in range(lot):
                first(f)

            for load in loads:
                load.wait()

        def second(and_next):
            base = lot * step
            for n in range(4):
                taps = jnp.concatenate(
                    [act[n, pl.ds(base + j, 3)].reshape(3 * deep, lw) for j in range(lot)], axis=1
                )
                m = jnp.dot(w2[n], taps, preferred_element_type=jnp.float32)
                if n == 0:
                    both[0] = m
                if n == 1:
                    both[0] += m
                    both[1] = m
                if n == 2:
                    both[0] += m
                    both[1] -= m
                if n == 3:
                    both[1] -= m
                if and_next:
                    first(base + lot + n)
            for j in range(lot):
                for r in range(2):
                    whole = both[r, :, j * lw : j * lw + lw]
                    whole += vec_ref[2] + firsts[lax.rem(base + j, 2 * lot), r]
                    out_ref[j, r] = jnp.transpose(whole).astype(jnp.bfloat16)

        @pl.when(here & (step < frames // lot - 1))
        def _():
            second(True)

        @pl.when(here & (step == frames // lot - 1))
        def _():
            second(False)

        @pl.when(jnp.logical_not(here))
        def _():
            out_ref[...] = jnp.zeros(out_ref.shape, out_ref.dtype)

    return pl.pallas_call(
        body,
        grid=(frames // lot,),
        out_shape=jax.ShapeDtypeStruct((frames, 2, lw, vc), jnp.bfloat16),
        in_specs=[
            smem_spec(),
            vmem_spec(),
            vmem_spec(),
            pl.BlockSpec(memory_space=pl.ANY),
            pl.BlockSpec(memory_space=pl.ANY),
            vmem_spec(),
        ],
        out_specs=pl.BlockSpec((lot, 2, lw, vc), lambda i: (i, 0, 0, 0)),
        scratch_shapes=[
            pltpu.VMEM((frames + 2, 6, 3 * lc, lw), jnp.bfloat16),
            pltpu.VMEM((4, frames + 2, deep, lw), jnp.bfloat16),
            pltpu.VMEM((2 * lot, 2, vc, lw), jnp.float32),
            pltpu.VMEM((vc, wide), jnp.bfloat16),
            pltpu.VMEM((3, vc, lw), jnp.float32),
            pltpu.VMEM((4, vc, 3 * deep), jnp.bfloat16),
            pltpu.VMEM((2, vc, lot * lw), jnp.float32),
            pltpu.SemaphoreType.DMA((9,)),
        ],
        compiler_params=pltpu.CompilerParams(vmem_limit_bytes=48 * MIB),
        cost_estimate=pl.CostEstimate(flops=0, bytes_accessed=0, transcendentals=0),
        name="decode",
    )(place, clip, w_in, *filters, vectors)


def on_device(
    query_input,
    key_input,
    value_input,
    resid,
    gate,
    query_norm_gain,
    key_norm_gain,
    output_weight,
    latents,
    w_in,
    b_in,
    norm_gain,
    w_mid,
    b_mid,
):
    last = lax.axis_size("grp") - 1
    decoder_here = lax.axis_index("grp") == last
    count = lax.axis_size(SEQ)
    side = lax.axis_size("z")
    core, at_z, at_x = lax.axis_index("core"), lax.axis_index("z"), lax.axis_index("x")
    place = jnp.stack(
        [
            decoder_here.astype(jnp.int32),
            core,
            lax.axis_index(SEQ),
            jnp.int32(count - 1),
            jnp.where(core == 0, at_z, at_x),
            jnp.where(core == 0, at_x, at_z),
        ]
    )
    channels = w_in.shape[2]

    def swap(x, ring, step):
        def partner(place):
            return (place ^ 1, side - 1 - place, place ^ 2)[step]

        pairs = []
        for at in range(last * count):
            g, z, x_, c = at // count, at // (2 * side) % side, at // 2 % side, at % 2
            if ring == 2:
                c = 1 - c
            elif (ring == 0) == (c == 0):
                z = partner(z)
            else:
                x_ = partner(x_)
            pairs.append((at, ((g * side + z) * side + x_) * 2 + c))
        return lax.ppermute(x, ("grp",) + SEQ, pairs)

    packed = norm_pack(
        query_input[0], key_input[0], value_input[0], query_norm_gain[None], key_norm_gain[None]
    )
    packed, w_here = lax.optimization_barrier((packed, output_weight))
    here = lax.all_to_all(packed, SEQ, split_axis=0, concat_axis=0, tiled=True)

    w_own = weight_half(place, w_here, swap(w_here, 2, 0))
    w_own, latents, w_mid = lax.optimization_barrier((w_own, latents, w_mid))
    w_back = swap(w_own, 0, 1)
    w_next = swap(w_own, 0, 0)

    own = jnp.swapaxes(latents, 2, 3)
    pieces = [lax.ppermute(own, "grp", [(g, last)]) for g in range(last)]
    early = filter_weights(place, w_mid, 0, 5)
    pieces, early = lax.optimization_barrier((pieces, early))
    clip = jnp.concatenate(pieces + [own], axis=0)
    links = [(last * count + i, last * count + i + 1) for i in range(count - 1)]
    above = lax.ppermute(clip, ("grp",) + SEQ, links)
    below = lax.ppermute(clip, ("grp",) + SEQ, [(b, a) for a, b in links])
    late = filter_weights(place, w_mid, 5, 4)
    above, below, late = lax.optimization_barrier((above, below, late))
    cells = jnp.concatenate([above, clip, below], axis=1)

    here, cells = lax.optimization_barrier((here, cells))
    head = attend(place, here)
    head, w_back = lax.optimization_barrier((head, w_back))
    head_there = swap(head, 2, 0)
    w_far = swap(w_back, 0, 0)
    head_there, w_next = lax.optimization_barrier((head_there, w_next))
    heads = pair_heads(place, head, head_there)
    from_far = swap(heads[3], 0, 2)
    heads = heads[0], swap(heads[1], 0, 0), swap(heads[2], 0, 1), from_far
    mine, zero, one, far = project(place, heads, (w_own, w_next, w_back, w_far))
    mine, one, zero, far, cells = lax.optimization_barrier((mine, one, zero, far, cells))
    sums = swap(far, 1, 2), swap(one, 1, 1), swap(zero, 1, 0)
    decoded = decode(
        place, cells, w_in.reshape(-1, channels), (early, late), jnp.stack([b_in, norm_gain, b_mid])
    )
    mine, decoded = lax.optimization_barrier((mine, decoded))
    kept, give = add_up(place, mine, sums)
    attn_out = finish(place, resid[0], gate, kept, swap(give, 2, 0))
    return attn_out[None], decoded[None]


def solution(mesh):
    fine = Mesh(mesh.devices.reshape(4, 4, 4, 2), ("grp",) + SEQ)
    placed = (
        P("grp", SEQ, None),
        P("grp", SEQ, None),
        P("grp", SEQ, None),
        P("grp", SEQ, None),
        P("grp", None),
        P(),
        P(),
        P(SEQ, None),
        P("grp", SEQ, None, None),
        P(),
        P(),
        P(),
        P(),
        P(),
    )
    return jax.shard_map(
        on_device,
        mesh=fine,
        in_specs=placed,
        out_specs=(P("grp", SEQ, None), P("grp", None, SEQ, None, None)),
        check_vma=False,
    )
```

```python
import math
import jax
import jax.numpy as jnp
from jax import lax
from jax.experimental import pallas as pl
from jax.experimental.pallas import tpu as pltpu
from jax.sharding import Mesh, PartitionSpec as P

SEQ = ("z", "x", "core")
EPS = 1e-06
MIB = 1024 * 1024


def vmem_spec():
    return pl.BlockSpec(memory_space=pltpu.VMEM)


def smem_spec():
    return pl.BlockSpec(memory_space=pltpu.SMEM)


def norm_pack(q, k, v, gain_q, gain_k):
    rows, width = q.shape
    heads = width // 128
    block = rows

    def body(q_ref, k_ref, v_ref, gq_ref, gk_ref, out_ref):
        def normed(ref, gain):
            x = ref[...].astype(jnp.float32)
            factor = lax.rsqrt(jnp.mean(x * x, axis=-1, keepdims=True) + EPS)
            return (x * factor * gain).astype(jnp.bfloat16)

        scale = 128**-0.5 * math.log2(math.e)
        qn = normed(q_ref, gq_ref[...] * scale)
        kn = normed(k_ref, gk_ref[...])
        for h in range(heads):
            cols = slice(128 * h, 128 * h + 128)
            out_ref[h, 0] = qn[:, cols]
            out_ref[h, 1] = kn[:, cols]
            out_ref[h, 2] = v_ref[:, cols]

    tokens = pl.BlockSpec((block, width), lambda i: (i, 0))
    gains = pl.BlockSpec((1, width), lambda i: (0, 0))
    return pl.pallas_call(
        body,
        grid=(rows // block,),
        out_shape=jax.ShapeDtypeStruct((heads, 3, rows, 128), jnp.bfloat16),
        in_specs=[tokens, tokens, tokens, gains, gains],
        out_specs=pl.BlockSpec((heads, 3, block, 128), lambda i: (0, 0, i, 0)),
        compiler_params=pltpu.CompilerParams(vmem_limit_bytes=60 * MIB),
        name="norm_pack",
    )(q, k, v, gain_q, gain_k)


def partners(position):
    return position, jnp.bitwise_xor(position, 1), 3 - position, jnp.bitwise_xor(position, 2)


def weight_half(place, w_here, w_there):
    rows, width = w_here.shape
    part = width // 2

    def body(place_ref, here_ref, there_ref, out_ref):
        here_at = pl.ds(pl.multiple_of(place_ref[1] * rows, rows), rows)
        there_at = pl.ds(pl.multiple_of((1 - place_ref[1]) * rows, rows), rows)

        @pl.when(place_ref[0] == 0)
        def _():
            at = pl.ds(pl.multiple_of(place_ref[1] * part, part), part)
            out_ref[here_at] = here_ref[:, at]
            out_ref[there_at] = there_ref[:, at]

    return pl.pallas_call(
        body,
        out_shape=jax.ShapeDtypeStruct((2 * rows, part), jnp.bfloat16),
        in_specs=[smem_spec(), vmem_spec(), vmem_spec()],
        out_specs=vmem_spec(),
        compiler_params=pltpu.CompilerParams(vmem_limit_bytes=16 * MIB),
        name="weight_half",
    )(place, w_here, w_there)


def attend(place, here):
    devices, _, tok, width = here.shape
    keys = devices * tok
    steps, chains = 4, 2
    lot = devices // (steps * chains)

    def body(place_ref, here_ref, out_ref):
        step = pl.program_id(0)

        @pl.when(place_ref[0] == 0)
        def _():
            ones = jnp.ones((keys, width), jnp.bfloat16)
            values = jnp.concatenate([here_ref[:, 2].reshape(keys, width), ones], axis=1)
            for n in range(chains):
                at = pl.ds((step * chains + n) * lot, lot)
                s = lax.dot_general(
                    here_ref[at, 0].reshape(lot * tok, width),
                    here_ref[:, 1].reshape(keys, width),
                    (((1,), (1,)), ((), ())),
                    preferred_element_type=jnp.float32,
                )
                p = jnp.exp2(s - jnp.max(s, axis=-1, keepdims=True)).astype(jnp.bfloat16)
                o = jnp.dot(p, values, preferred_element_type=jnp.float32)
                o = (o[:, :width] / o[:, width:]).astype(jnp.bfloat16)
                out_ref[at] = o.reshape(lot, tok, width)

    return pl.pallas_call(
        body,
        grid=(steps,),
        out_shape=jax.ShapeDtypeStruct((devices, tok, width), jnp.bfloat16),
        in_specs=[smem_spec(), vmem_spec()],
        out_specs=vmem_spec(),
        compiler_params=pltpu.CompilerParams(vmem_limit_bytes=20 * MIB),
        cost_estimate=pl.CostEstimate(flops=0, bytes_accessed=0, transcendentals=0),
        name="attend",
    )(place, here)


def pair_heads(place, here, there):
    devices, tok, width = here.shape

    def body(place_ref, here_ref, there_ref, *outs):
        core = place_ref[1]
        here_at = pl.ds(pl.multiple_of(core * width, width), width)
        there_at = pl.ds(pl.multiple_of((1 - core) * width, width), width)

        @pl.when(place_ref[0] == 0)
        def _():
            for first, out in zip(partners(place_ref[4]), outs):
                for second in range(4):
                    chip = jnp.where(core == 0, 4 * first + second, 4 * second + first)
                    at = pl.ds(2 * chip, 2)
                    out[second, :, :, here_at] = here_ref[at]
                    out[second, :, :, there_at] = there_ref[at]

    return pl.pallas_call(
        body,
        out_shape=(jax.ShapeDtypeStruct((4, 2, tok, 2 * width), jnp.bfloat16),) * 4,
        in_specs=[smem_spec(), vmem_spec(), vmem_spec()],
        out_specs=(vmem_spec(),) * 4,
        compiler_params=pltpu.CompilerParams(vmem_limit_bytes=16 * MIB),
        name="pair_heads",
    )(place, here, there)


def project(place, heads, weights):
    _, two, tok, _ = heads[0].shape
    part = weights[0].shape[1]
    lot = two * tok

    def body(place_ref, h0, h1, h2, h3, w0, w1, w2, w3, *outs):
        @pl.when(place_ref[0] == 0)
        def _():
            weight = jnp.concatenate([w0[...], w1[...], w2[...], w3[...]], axis=0)
            feats = jnp.concatenate(
                [
                    jnp.concatenate([h[chip].reshape(lot, 256) for h in (h0, h1, h2, h3)], axis=1)
                    for chip in partners(place_ref[5])
                ],
                axis=0,
            )
            out = jnp.dot(feats, weight, preferred_element_type=jnp.float32)
            for k, ref in enumerate(outs):
                ref[...] = out[lot * k : lot * k + lot].reshape(two, tok, part).astype(ref.dtype)

    shape = (two, tok, part)
    return pl.pallas_call(
        body,
        out_shape=(jax.ShapeDtypeStruct(shape, jnp.float32),)
        + (jax.ShapeDtypeStruct(shape, jnp.bfloat16),) * 3,
        in_specs=[smem_spec()] + [vmem_spec()] * 8,
        out_specs=(vmem_spec(),) * 4,
        compiler_params=pltpu.CompilerParams(vmem_limit_bytes=24 * MIB),
        cost_estimate=pl.CostEstimate(
            flops=8 * lot * 1024 * part, bytes_accessed=8 * MIB, transcendentals=0
        ),
        name="project",
    )(place, *heads, *weights)


def add_up(place, own, others):
    def body(place_ref, own_ref, a_ref, b_ref, c_ref, keep_ref, give_ref):
        core = place_ref[1]

        @pl.when(place_ref[0] == 0)
        def _():
            for at, out in ((core, keep_ref), (1 - core, give_ref)):
                total = own_ref[at]
                for ref in (a_ref, b_ref, c_ref):
                    total += ref[at].astype(jnp.float32)
                out[...] = total.astype(out.dtype)

    return pl.pallas_call(
        body,
        out_shape=(
            jax.ShapeDtypeStruct(own.shape[1:], jnp.float32),
            jax.ShapeDtypeStruct(own.shape[1:], jnp.bfloat16),
        ),
        in_specs=[smem_spec()] + [vmem_spec()] * 4,
        out_specs=(vmem_spec(),) * 2,
        compiler_params=pltpu.CompilerParams(vmem_limit_bytes=24 * MIB),
        name="add_up",
    )(place, own, *others)


def finish(place, resid, gate, kept, got):
    part = kept.shape[1]

    def body(place_ref, resid_ref, gate_ref, kept_ref, got_ref, out_ref):
        @pl.when(place_ref[0] == 0)
        def _():
            for half, ref in ((place_ref[1], kept_ref), (1 - place_ref[1], got_ref)):
                at = pl.ds(pl.multiple_of(half * part, part), part)
                total = resid_ref[:, at].astype(jnp.float32)
                total += gate_ref[:, at] * ref[...].astype(jnp.float32)
                out_ref[:, at] = total.astype(jnp.bfloat16)

        @pl.when(place_ref[0] == 1)
        def _():
            out_ref[...] = jnp.zeros(out_ref.shape, out_ref.dtype)

    return pl.pallas_call(
        body,
        out_shape=jax.ShapeDtypeStruct(resid.shape, jnp.bfloat16),
        in_specs=[smem_spec()] + [vmem_spec()] * 4,
        out_specs=vmem_spec(),
        compiler_params=pltpu.CompilerParams(vmem_limit_bytes=16 * MIB),
        name="finish",
    )(place, resid, gate, kept, got)


def decode(place, clip, w_in, w_mid, vectors):
    frames, _, lc, lw = clip.shape
    fan, vc = w_in.shape
    deep = 3 * vc
    lot = 4
    wide = 512

    def body(
        place_ref, clip_ref, win_ref, wm_ref, rows_ref, out_ref,
        lat, act, firsts, w1_ref, vec_ref, w2, both, raw, sems,
    ):
        step = pl.program_id(0)
        here = place_ref[0] == 1
        def moved(x):
            lane = lax.broadcasted_iota(jnp.int32, x.shape, x.ndim - 1)
            left = jnp.where(lane == 0, 0.0, pltpu.roll(x, 1, x.ndim - 1))
            right = jnp.where(lane == lw - 1, 0.0, pltpu.roll(x, lw - 1, x.ndim - 1))
            return left, x, right

        def first(f):
            sides = []
            for row in range(4):
                taps = [lat[f + dt, row : row + 3].reshape(9 * lc, lw) for dt in range(3)]
                taps.append(jnp.zeros((wide - fan, lw), jnp.bfloat16))
                sides.append(jnp.concatenate(taps, axis=0))
            y = jnp.dot(
                w1_ref[...], jnp.concatenate(sides, axis=1), preferred_element_type=jnp.float32
            )
            acts = []
            for row in range(4):
                hidden = y[:, row * lw : row * lw + lw] + vec_ref[0]
                if row in (1, 2):
                    firsts[lax.rem(f, 2 * lot), row - 1] = hidden
                factor = lax.rsqrt(jnp.mean(hidden * hidden, axis=0, keepdims=True) + EPS)
                if row == 0:
                    factor = jnp.where(place_ref[2] == 0, 0.0, factor)
                if row == 3:
                    factor = jnp.where(place_ref[2] == place_ref[3], 0.0, factor)
                half = hidden * (0.5 * factor) * vec_ref[1]
                acts.append(half * (1.0 + jnp.tanh(half)))
            a0, a1, a2, a3 = acts
            for n, u in enumerate((a0 - a2, a1 + a2, a2 - a1, a1 - a3)):
                for dx, piece in enumerate(moved(u)):
                    act[n, f + 2, dx * vc : dx * vc + vc] = piece.astype(jnp.bfloat16)

        @pl.when(here & (step == 0))
        def _():
            loads = [pltpu.make_async_copy(wm_ref.at[n], raw.at[n], sems.at[n]) for n in range(3)]
            for load in loads:
                load.start()
            w1_ref[:, :fan] = jnp.transpose(win_ref[...])
            w1_ref[:, fan:] = jnp.zeros((vc, wide - fan), jnp.bfloat16)
            for n in range(3):
                row = jnp.broadcast_to(rows_ref[n : n + 1], (lw, vc))
                vec_ref[n] = jnp.transpose(row)
            lat[:2] = jnp.zeros((2, 6, 3 * lc, lw), jnp.bfloat16)
            act[:, :2] = jnp.zeros((4, 2, deep, lw), jnp.bfloat16)
            cells = clip_ref[...].astype(jnp.float32)
            for dx, piece in enumerate(moved(cells)):
                lat[2:, :, dx * lc : dx * lc + lc] = piece.astype(jnp.bfloat16)

            for f in range(lot):
                first(f)
            for time, load in enumerate(loads):
                load.wait()

                @pl.loop(0, 3)
                def _(column):
                    up, mid, down = (jnp.transpose(raw[time, n, column]) for n in range(3))
                    ends = 0.5 * (up.astype(jnp.float32) + down.astype(jnp.float32))
                    half = 0.5 * mid.astype(jnp.float32)
                    at = pl.ds(pl.multiple_of(time * deep + column * vc, vc), vc)
                    for n, g in enumerate((up, ends + half, ends - half, down)):
                        w2[n, :, at] = g.astype(jnp.bfloat16)

        def second(and_next):
            base = lot * step
            for n in range(4):
                taps = jnp.concatenate(
                    [act[n, pl.ds(base + j, 3)].reshape(3 * deep, lw) for j in range(lot)], axis=1
                )
                m = jnp.dot(w2[n], taps, preferred_element_type=jnp.float32)
                if n == 0:
                    both[0] = m
                if n == 1:
                    both[0] += m
                    both[1] = m
                if n == 2:
                    both[0] += m
                    both[1] -= m
                if n == 3:
                    both[1] -= m
                if and_next:
                    first(base + lot + n)
            for j in range(lot):
                for r in range(2):
                    whole = both[r, :, j * lw : j * lw + lw]
                    whole += vec_ref[2] + firsts[lax.rem(base + j, 2 * lot), r]
                    out_ref[j, r] = jnp.transpose(whole).astype(jnp.bfloat16)

        @pl.when(here & (step < frames // lot - 1))
        def _():
            second(True)

        @pl.when(here & (step == frames // lot - 1))
        def _():
            second(False)

        @pl.when(jnp.logical_not(here))
        def _():
            out_ref[...] = jnp.zeros(out_ref.shape, out_ref.dtype)

    return pl.pallas_call(
        body,
        grid=(frames // lot,),
        out_shape=jax.ShapeDtypeStruct((frames, 2, lw, vc), jnp.bfloat16),
        in_specs=[
            smem_spec(),
            vmem_spec(),
            vmem_spec(),
            pl.BlockSpec(memory_space=pl.ANY),
            vmem_spec(),
        ],
        out_specs=pl.BlockSpec((lot, 2, lw, vc), lambda i: (i, 0, 0, 0)),
        scratch_shapes=[
            pltpu.VMEM((frames + 2, 6, 3 * lc, lw), jnp.bfloat16),
            pltpu.VMEM((4, frames + 2, deep, lw), jnp.bfloat16),
            pltpu.VMEM((2 * lot, 2, vc, lw), jnp.float32),
            pltpu.VMEM((vc, wide), jnp.bfloat16),
            pltpu.VMEM((3, vc, lw), jnp.float32),
            pltpu.VMEM((4, vc, 3 * deep), jnp.bfloat16),
            pltpu.VMEM((2, vc, lot * lw), jnp.float32),
            pltpu.VMEM(w_mid.shape, jnp.bfloat16),
            pltpu.SemaphoreType.DMA((3,)),
        ],
        compiler_params=pltpu.CompilerParams(vmem_limit_bytes=58 * MIB),
        cost_estimate=pl.CostEstimate(flops=0, bytes_accessed=0, transcendentals=0),
        name="decode",
    )(place, clip, w_in, w_mid, vectors)


def on_device(
    query_input,
    key_input,
    value_input,
    resid,
    gate,
    query_norm_gain,
    key_norm_gain,
    output_weight,
    latents,
    w_in,
    b_in,
    norm_gain,
    w_mid,
    b_mid,
):
    last = lax.axis_size("grp") - 1
    decoder_here = lax.axis_index("grp") == last
    count = lax.axis_size(SEQ)
    side = lax.axis_size("z")
    core, at_z, at_x = lax.axis_index("core"), lax.axis_index("z"), lax.axis_index("x")
    place = jnp.stack(
        [
            decoder_here.astype(jnp.int32),
            core,
            lax.axis_index(SEQ),
            jnp.int32(count - 1),
            jnp.where(core == 0, at_z, at_x),
            jnp.where(core == 0, at_x, at_z),
        ]
    )
    channels = w_in.shape[2]

    def swap(x, ring, step):
        def partner(place):
            return (place ^ 1, side - 1 - place, place ^ 2)[step]

        pairs = []
        for at in range(last * count):
            g, z, x_, c = at // count, at // (2 * side) % side, at // 2 % side, at % 2
            if ring == 2:
                c = 1 - c
            elif (ring == 0) == (c == 0):
                z = partner(z)
            else:
                x_ = partner(x_)
            pairs.append((at, ((g * side + z) * side + x_) * 2 + c))
        return lax.ppermute(x, ("grp",) + SEQ, pairs)

    packed = norm_pack(
        query_input[0], key_input[0], value_input[0], query_norm_gain[None], key_norm_gain[None]
    )
    packed, w_here = lax.optimization_barrier((packed, output_weight))
    here = lax.all_to_all(packed, SEQ, split_axis=0, concat_axis=0, tiled=True)

    w_own = weight_half(place, w_here, swap(w_here, 2, 0))
    w_own, latents = lax.optimization_barrier((w_own, latents))
    w_back = swap(w_own, 0, 1)
    w_next = swap(w_own, 0, 0)

    own = jnp.swapaxes(latents, 2, 3)
    pieces = [lax.ppermute(own, "grp", [(g, last)]) for g in range(last)]
    clip = jnp.concatenate(pieces + [own], axis=0)
    links = [(last * count + i, last * count + i + 1) for i in range(count - 1)]
    above = lax.ppermute(clip, ("grp",) + SEQ, links)
    below = lax.ppermute(clip, ("grp",) + SEQ, [(b, a) for a, b in links])
    cells = jnp.concatenate([above, clip, below], axis=1)

    here, cells = lax.optimization_barrier((here, cells))
    head = attend(place, here)
    head, w_back = lax.optimization_barrier((head, w_back))
    head_there = swap(head, 2, 0)
    w_far = swap(w_back, 0, 0)
    head_there, w_next = lax.optimization_barrier((head_there, w_next))
    heads = pair_heads(place, head, head_there)
    from_far = swap(heads[3], 0, 2)
    heads = heads[0], swap(heads[1], 0, 0), swap(heads[2], 0, 1), from_far
    mine, zero, one, far = project(place, heads, (w_own, w_next, w_back, w_far))
    mine, one, zero, far, cells = lax.optimization_barrier((mine, one, zero, far, cells))
    sums = swap(far, 1, 2), swap(one, 1, 1), swap(zero, 1, 0)
    decoded = decode(
        place,
        cells,
        w_in.reshape(-1, channels),
        w_mid.reshape(3, 3, 3, channels, channels),
        jnp.stack([b_in, norm_gain, b_mid]),
    )
    mine, decoded = lax.optimization_barrier((mine, decoded))
    kept, give = add_up(place, mine, sums)
    attn_out = finish(place, resid[0], gate, kept, swap(give, 2, 0))
    return attn_out[None], decoded[None]


def solution(mesh):
    fine = Mesh(mesh.devices.reshape(4, 4, 4, 2), ("grp",) + SEQ)
    placed = (
        P("grp", SEQ, None),
        P("grp", SEQ, None),
        P("grp", SEQ, None),
        P("grp", SEQ, None),
        P("grp", None),
        P(),
        P(),
        P(SEQ, None),
        P("grp", SEQ, None, None),
        P(),
        P(),
        P(),
        P(),
        P(),
    )
    return jax.shard_map(
        on_device,
        mesh=fine,
        in_specs=placed,
        out_specs=(P("grp", SEQ, None), P("grp", None, SEQ, None, None)),
        check_vma=False,
    )
```

```python
import math
import jax
import jax.numpy as jnp
from jax import lax
from jax.experimental import pallas as pl
from jax.experimental.pallas import tpu as pltpu
from jax.sharding import Mesh, PartitionSpec as P

SEQ = ("z", "x", "core")
EPS = 1e-06
MIB = 1024 * 1024


def vmem_spec():
    return pl.BlockSpec(memory_space=pltpu.VMEM)


def smem_spec():
    return pl.BlockSpec(memory_space=pltpu.SMEM)


def norm_pack(q, k, v, gain_q, gain_k):
    rows, width = q.shape
    heads = width // 128
    block = rows

    def body(q_ref, k_ref, v_ref, gq_ref, gk_ref, out_ref):
        def normed(ref, gain):
            x = ref[...].astype(jnp.float32)
            factor = lax.rsqrt(jnp.mean(x * x, axis=-1, keepdims=True) + EPS)
            return (x * factor * gain).astype(jnp.bfloat16)

        scale = 128**-0.5 * math.log2(math.e)
        qn = normed(q_ref, gq_ref[...] * scale)
        kn = normed(k_ref, gk_ref[...])
        for h in range(heads):
            cols = slice(128 * h, 128 * h + 128)
            out_ref[h, 0] = qn[:, cols]
            out_ref[h, 1] = kn[:, cols]
            out_ref[h, 2] = v_ref[:, cols]

    tokens = pl.BlockSpec((block, width), lambda i: (i, 0))
    gains = pl.BlockSpec((1, width), lambda i: (0, 0))
    return pl.pallas_call(
        body,
        grid=(rows // block,),
        out_shape=jax.ShapeDtypeStruct((heads, 3, rows, 128), jnp.bfloat16),
        in_specs=[tokens, tokens, tokens, gains, gains],
        out_specs=pl.BlockSpec((heads, 3, block, 128), lambda i: (0, 0, i, 0)),
        compiler_params=pltpu.CompilerParams(vmem_limit_bytes=60 * MIB),
        name="norm_pack",
    )(q, k, v, gain_q, gain_k)


def partners(position):
    return position, jnp.bitwise_xor(position, 1), 3 - position, jnp.bitwise_xor(position, 2)


def weight_half(place, w_here, w_there):
    rows, width = w_here.shape
    part = width // 2

    def body(place_ref, here_ref, there_ref, out_ref):
        here_at = pl.ds(pl.multiple_of(place_ref[1] * rows, rows), rows)
        there_at = pl.ds(pl.multiple_of((1 - place_ref[1]) * rows, rows), rows)

        @pl.when(place_ref[0] == 0)
        def _():
            at = pl.ds(pl.multiple_of(place_ref[1] * part, part), part)
            out_ref[here_at] = here_ref[:, at]
            out_ref[there_at] = there_ref[:, at]

    return pl.pallas_call(
        body,
        out_shape=jax.ShapeDtypeStruct((2 * rows, part), jnp.bfloat16),
        in_specs=[smem_spec(), vmem_spec(), vmem_spec()],
        out_specs=vmem_spec(),
        compiler_params=pltpu.CompilerParams(vmem_limit_bytes=16 * MIB),
        name="weight_half",
    )(place, w_here, w_there)


def attend(place, here):
    devices, _, tok, width = here.shape
    keys = devices * tok
    steps, chains = 4, 2
    lot = devices // (steps * chains)

    def body(place_ref, here_ref, out_ref):
        step = pl.program_id(0)

        @pl.when(place_ref[0] == 0)
        def _():
            ones = jnp.ones((keys, width), jnp.bfloat16)
            values = jnp.concatenate([here_ref[:, 2].reshape(keys, width), ones], axis=1)
            for n in range(chains):
                at = pl.ds((step * chains + n) * lot, lot)
                s = lax.dot_general(
                    here_ref[at, 0].reshape(lot * tok, width),
                    here_ref[:, 1].reshape(keys, width),
                    (((1,), (1,)), ((), ())),
                    preferred_element_type=jnp.float32,
                )
                p = jnp.exp2(s - jnp.max(s, axis=-1, keepdims=True)).astype(jnp.bfloat16)
                o = jnp.dot(p, values, preferred_element_type=jnp.float32)
                o = (o[:, :width] / o[:, width:]).astype(jnp.bfloat16)
                out_ref[at] = o.reshape(lot, tok, width)

    return pl.pallas_call(
        body,
        grid=(steps,),
        out_shape=jax.ShapeDtypeStruct((devices, tok, width), jnp.bfloat16),
        in_specs=[smem_spec(), vmem_spec()],
        out_specs=vmem_spec(),
        compiler_params=pltpu.CompilerParams(vmem_limit_bytes=20 * MIB),
        cost_estimate=pl.CostEstimate(flops=0, bytes_accessed=0, transcendentals=0),
        name="attend",
    )(place, here)


def pair_heads(place, here, there):
    devices, tok, width = here.shape

    def body(place_ref, here_ref, there_ref, *outs):
        core = place_ref[1]
        here_at = pl.ds(pl.multiple_of(core * width, width), width)
        there_at = pl.ds(pl.multiple_of((1 - core) * width, width), width)

        @pl.when(place_ref[0] == 0)
        def _():
            for first, out in zip(partners(place_ref[4]), outs):
                for second in range(4):
                    chip = jnp.where(core == 0, 4 * first + second, 4 * second + first)
                    at = pl.ds(2 * chip, 2)
                    out[second, :, :, here_at] = here_ref[at]
                    out[second, :, :, there_at] = there_ref[at]

    return pl.pallas_call(
        body,
        out_shape=(jax.ShapeDtypeStruct((4, 2, tok, 2 * width), jnp.bfloat16),) * 4,
        in_specs=[smem_spec(), vmem_spec(), vmem_spec()],
        out_specs=(vmem_spec(),) * 4,
        compiler_params=pltpu.CompilerParams(vmem_limit_bytes=16 * MIB),
        name="pair_heads",
    )(place, here, there)


def project(place, heads, weights):
    _, two, tok, _ = heads[0].shape
    part = weights[0].shape[1]
    lot = two * tok

    def body(place_ref, h0, h1, h2, h3, w0, w1, w2, w3, *outs):
        @pl.when(place_ref[0] == 0)
        def _():
            weight = jnp.concatenate([w0[...], w1[...], w2[...], w3[...]], axis=0)
            feats = jnp.concatenate(
                [
                    jnp.concatenate([h[chip].reshape(lot, 256) for h in (h0, h1, h2, h3)], axis=1)
                    for chip in partners(place_ref[5])
                ],
                axis=0,
            )
            out = jnp.dot(feats, weight, preferred_element_type=jnp.float32)
            for k, ref in enumerate(outs):
                ref[...] = out[lot * k : lot * k + lot].reshape(two, tok, part).astype(ref.dtype)

    shape = (two, tok, part)
    return pl.pallas_call(
        body,
        out_shape=(jax.ShapeDtypeStruct(shape, jnp.float32),)
        + (jax.ShapeDtypeStruct(shape, jnp.bfloat16),) * 3,
        in_specs=[smem_spec()] + [vmem_spec()] * 8,
        out_specs=(vmem_spec(),) * 4,
        compiler_params=pltpu.CompilerParams(vmem_limit_bytes=24 * MIB),
        cost_estimate=pl.CostEstimate(
            flops=8 * lot * 1024 * part, bytes_accessed=8 * MIB, transcendentals=0
        ),
        name="project",
    )(place, *heads, *weights)


def add_up(place, own, others):
    def body(place_ref, own_ref, a_ref, b_ref, c_ref, keep_ref, give_ref):
        core = place_ref[1]

        @pl.when(place_ref[0] == 0)
        def _():
            for at, out in ((core, keep_ref), (1 - core, give_ref)):
                total = own_ref[at]
                for ref in (a_ref, b_ref, c_ref):
                    total += ref[at].astype(jnp.float32)
                out[...] = total.astype(out.dtype)

    return pl.pallas_call(
        body,
        out_shape=(
            jax.ShapeDtypeStruct(own.shape[1:], jnp.float32),
            jax.ShapeDtypeStruct(own.shape[1:], jnp.bfloat16),
        ),
        in_specs=[smem_spec()] + [vmem_spec()] * 4,
        out_specs=(vmem_spec(),) * 2,
        compiler_params=pltpu.CompilerParams(vmem_limit_bytes=24 * MIB),
        name="add_up",
    )(place, own, *others)


def finish(place, resid, gate, kept, got):
    part = kept.shape[1]

    def body(place_ref, resid_ref, gate_ref, kept_ref, got_ref, out_ref):
        @pl.when(place_ref[0] == 0)
        def _():
            for half, ref in ((place_ref[1], kept_ref), (1 - place_ref[1], got_ref)):
                at = pl.ds(pl.multiple_of(half * part, part), part)
                total = resid_ref[:, at].astype(jnp.float32)
                total += gate_ref[:, at] * ref[...].astype(jnp.float32)
                out_ref[:, at] = total.astype(jnp.bfloat16)

        @pl.when(place_ref[0] == 1)
        def _():
            out_ref[...] = jnp.zeros(out_ref.shape, out_ref.dtype)

    return pl.pallas_call(
        body,
        out_shape=jax.ShapeDtypeStruct(resid.shape, jnp.bfloat16),
        in_specs=[smem_spec()] + [vmem_spec()] * 4,
        out_specs=vmem_spec(),
        compiler_params=pltpu.CompilerParams(vmem_limit_bytes=16 * MIB),
        name="finish",
    )(place, resid, gate, kept, got)


def decode(place, clip, w_in, w_mid, vectors):
    frames, _, lc, lw = clip.shape
    fan, vc = w_in.shape
    deep = 3 * vc
    lot = 4
    wide = 512

    def body(
        place_ref, clip_ref, win_ref, wm_ref, rows_ref, out_ref,
        lat, act, firsts, w1_ref, vec_ref, w2, both, raw, sems,
    ):
        step = pl.program_id(0)
        here = place_ref[0] == 1
        def moved(x):
            lane = lax.broadcasted_iota(jnp.int32, x.shape, x.ndim - 1)
            left = jnp.where(lane == 0, 0.0, pltpu.roll(x, 1, x.ndim - 1))
            right = jnp.where(lane == lw - 1, 0.0, pltpu.roll(x, lw - 1, x.ndim - 1))
            return left, x, right

        def first(f):
            sides = []
            for row in range(4):
                taps = [lat[f + dt, row : row + 3].reshape(9 * lc, lw) for dt in range(3)]
                taps.append(jnp.zeros((wide - fan, lw), jnp.bfloat16))
                sides.append(jnp.concatenate(taps, axis=0))
            y = jnp.dot(
                w1_ref[...], jnp.concatenate(sides, axis=1), preferred_element_type=jnp.float32
            )
            acts = []
            for row in range(4):
                hidden = y[:, row * lw : row * lw + lw] + vec_ref[0]
                if row in (1, 2):
                    firsts[lax.rem(f, 2 * lot), row - 1] = hidden
                factor = lax.rsqrt(jnp.mean(hidden * hidden, axis=0, keepdims=True) + EPS)
                if row == 0:
                    factor = jnp.where(place_ref[2] == 0, 0.0, factor)
                if row == 3:
                    factor = jnp.where(place_ref[2] == place_ref[3], 0.0, factor)
                half = hidden * (0.5 * factor) * vec_ref[1]
                acts.append(half * (1.0 + jnp.tanh(half)))
            a0, a1, a2, a3 = acts
            for n, u in enumerate((a0 - a2, a1 + a2, a2 - a1, a1 - a3)):
                for dx, piece in enumerate(moved(u)):
                    act[n, f + 2, dx * vc : dx * vc + vc] = piece.astype(jnp.bfloat16)

        @pl.when(here & (step == 0))
        def _():
            loads = [pltpu.make_async_copy(wm_ref.at[n], raw.at[n], sems.at[n]) for n in range(3)]
            for load in loads:
                load.start()
            w1_ref[:, :fan] = jnp.transpose(win_ref[...])
            w1_ref[:, fan:] = jnp.zeros((vc, wide - fan), jnp.bfloat16)
            for n in range(3):
                row = jnp.broadcast_to(rows_ref[n : n + 1], (lw, vc))
                vec_ref[n] = jnp.transpose(row)
            lat[:2] = jnp.zeros((2, 6, 3 * lc, lw), jnp.bfloat16)
            act[:, :2] = jnp.zeros((4, 2, deep, lw), jnp.bfloat16)
            cells = clip_ref[...].astype(jnp.float32)
            for dx, piece in enumerate(moved(cells)):
                lat[2:, :, dx * lc : dx * lc + lc] = piece.astype(jnp.bfloat16)

            for f in range(lot):
                first(f)
            for time, load in enumerate(loads):
                load.wait()

                @pl.loop(0, 3)
                def _(column):
                    up, mid, down = (jnp.transpose(raw[time, n, column]) for n in range(3))
                    ends = 0.5 * (up.astype(jnp.float32) + down.astype(jnp.float32))
                    half = 0.5 * mid.astype(jnp.float32)
                    at = pl.ds(pl.multiple_of(time * deep + column * vc, vc), vc)
                    for n, g in enumerate((up, ends + half, ends - half, down)):
                        w2[n, :, at] = g.astype(jnp.bfloat16)

        def second(and_next):
            base = lot * step
            for n in range(4):
                taps = jnp.concatenate(
                    [act[n, pl.ds(base + j, 3)].reshape(3 * deep, lw) for j in range(lot)], axis=1
                )
                m = jnp.dot(w2[n], taps, preferred_element_type=jnp.float32)
                if n == 0:
                    both[0] = m
                if n == 1:
                    both[0] += m
                    both[1] = m
                if n == 2:
                    both[0] += m
                    both[1] -= m
                if n == 3:
                    both[1] -= m
                if and_next:
                    first(base + lot + n)
            for j in range(lot):
                for r in range(2):
                    whole = both[r, :, j * lw : j * lw + lw]
                    whole += vec_ref[2] + firsts[lax.rem(base + j, 2 * lot), r]
                    out_ref[j, r] = jnp.transpose(whole).astype(jnp.bfloat16)

        @pl.when(here & (step < frames // lot - 1))
        def _():
            second(True)

        @pl.when(here & (step == frames // lot - 1))
        def _():
            second(False)

        @pl.when(jnp.logical_not(here))
        def _():
            out_ref[...] = jnp.zeros(out_ref.shape, out_ref.dtype)

    return pl.pallas_call(
        body,
        grid=(frames // lot,),
        out_shape=jax.ShapeDtypeStruct((frames, 2, lw, vc), jnp.bfloat16),
        in_specs=[
            smem_spec(),
            vmem_spec(),
            vmem_spec(),
            pl.BlockSpec(memory_space=pl.ANY),
            vmem_spec(),
        ],
        out_specs=pl.BlockSpec((lot, 2, lw, vc), lambda i: (i, 0, 0, 0)),
        scratch_shapes=[
            pltpu.VMEM((frames + 2, 6, 3 * lc, lw), jnp.bfloat16),
            pltpu.VMEM((4, frames + 2, deep, lw), jnp.bfloat16),
            pltpu.VMEM((2 * lot, 2, vc, lw), jnp.float32),
            pltpu.VMEM((vc, wide), jnp.bfloat16),
            pltpu.VMEM((3, vc, lw), jnp.float32),
            pltpu.VMEM((4, vc, 3 * deep), jnp.bfloat16),
            pltpu.VMEM((2, vc, lot * lw), jnp.float32),
            pltpu.VMEM(w_mid.shape, jnp.bfloat16),
            pltpu.SemaphoreType.DMA((3,)),
        ],
        compiler_params=pltpu.CompilerParams(vmem_limit_bytes=58 * MIB),
        cost_estimate=pl.CostEstimate(flops=0, bytes_accessed=0, transcendentals=0),
        name="decode",
    )(place, clip, w_in, w_mid, vectors)


def on_device(
    query_input,
    key_input,
    value_input,
    resid,
    gate,
    query_norm_gain,
    key_norm_gain,
    output_weight,
    latents,
    w_in,
    b_in,
    norm_gain,
    w_mid,
    b_mid,
):
    last = lax.axis_size("grp") - 1
    decoder_here = lax.axis_index("grp") == last
    count = lax.axis_size(SEQ)
    side = lax.axis_size("z")
    core, at_z, at_x = lax.axis_index("core"), lax.axis_index("z"), lax.axis_index("x")
    place = jnp.stack(
        [
            decoder_here.astype(jnp.int32),
            core,
            lax.axis_index(SEQ),
            jnp.int32(count - 1),
            jnp.where(core == 0, at_z, at_x),
            jnp.where(core == 0, at_x, at_z),
        ]
    )
    channels = w_in.shape[2]

    def swap(x, ring, step):
        def partner(place):
            return (place ^ 1, side - 1 - place, place ^ 2)[step]

        pairs = []
        for at in range(last * count):
            g, z, x_, c = at // count, at // (2 * side) % side, at // 2 % side, at % 2
            if ring == 2:
                c = 1 - c
            elif (ring == 0) == (c == 0):
                z = partner(z)
            else:
                x_ = partner(x_)
            pairs.append((at, ((g * side + z) * side + x_) * 2 + c))
        return lax.ppermute(x, ("grp",) + SEQ, pairs)

    packed = norm_pack(
        query_input[0], key_input[0], value_input[0], query_norm_gain[None], key_norm_gain[None]
    )
    packed, w_here = lax.optimization_barrier((packed, output_weight))
    here = lax.all_to_all(packed, SEQ, split_axis=0, concat_axis=0, tiled=True)

    w_own = weight_half(place, w_here, swap(w_here, 2, 0))
    w_own, latents = lax.optimization_barrier((w_own, latents))
    w_back = swap(w_own, 0, 1)
    w_next = swap(w_own, 0, 0)

    own = jnp.swapaxes(latents, 2, 3)
    pieces = [lax.ppermute(own, "grp", [(g, last)]) for g in range(last)]
    clip = jnp.concatenate(pieces + [own], axis=0)
    links = [(last * count + i, last * count + i + 1) for i in range(count - 1)]
    above = lax.ppermute(clip, ("grp",) + SEQ, links)
    below = lax.ppermute(clip, ("grp",) + SEQ, [(b, a) for a, b in links])
    cells = jnp.concatenate([above, clip, below], axis=1)

    here, cells = lax.optimization_barrier((here, cells))
    head = attend(place, here)
    head_there = swap(head, 2, 0)
    head_there, w_next, w_back = lax.optimization_barrier((head_there, w_next, w_back))
    w_far = swap(w_back, 0, 0)
    heads = pair_heads(place, head, head_there)
    from_far = swap(heads[3], 0, 2)
    heads = heads[0], swap(heads[1], 0, 0), swap(heads[2], 0, 1), from_far
    mine, zero, one, far = project(place, heads, (w_own, w_next, w_back, w_far))
    mine, one, zero, far, cells = lax.optimization_barrier((mine, one, zero, far, cells))
    sums = swap(far, 1, 2), swap(one, 1, 1), swap(zero, 1, 0)
    decoded = decode(
        place,
        cells,
        w_in.reshape(-1, channels),
        w_mid.reshape(3, 3, 3, channels, channels),
        jnp.stack([b_in, norm_gain, b_mid]),
    )
    mine, decoded = lax.optimization_barrier((mine, decoded))
    kept, give = add_up(place, mine, sums)
    attn_out = finish(place, resid[0], gate, kept, swap(give, 2, 0))
    return attn_out[None], decoded[None]


def solution(mesh):
    fine = Mesh(mesh.devices.reshape(4, 4, 4, 2), ("grp",) + SEQ)
    placed = (
        P("grp", SEQ, None),
        P("grp", SEQ, None),
        P("grp", SEQ, None),
        P("grp", SEQ, None),
        P("grp", None),
        P(),
        P(),
        P(SEQ, None),
        P("grp", SEQ, None, None),
        P(),
        P(),
        P(),
        P(),
        P(),
    )
    return jax.shard_map(
        on_device,
        mesh=fine,
        in_specs=placed,
        out_specs=(P("grp", SEQ, None), P("grp", None, SEQ, None, None)),
        check_vma=False,
    )
```
